128 devices in a mesh: inst: 4 (over x_lo, core), tp: 32 (over z, x_hi, y).
Axes of the slice: x: 4 (x_hi: 2, x_lo: 2; x = x_hi * 2 + x_lo), y: 4, z: 4, core: 2. Of those that a mesh axis runs over, the one named last changes fastest.
Arguments:
- mixer_input: bfloat16 [4, 1024, 16384], P(None, 'inst', 'tp'), may hold values from -6 to 6
- gate_input: bfloat16 [4, 1024, 16384], P(None, 'inst', 'tp'), may hold values from -6 to 6
- conv_state: bfloat16 [1024, 3, 16384], P('inst', None, 'tp'), may hold values from -6 to 6
- scan_state: float32 [1024, 16, 16384], P('inst', None, 'tp'), may hold values from -6 to 6
- leave_slot: int32 [4, 4, 32], P('inst'), may hold values from 0 to 255, as said below
- land_slot: int32 [4, 4, 32], P(None, 'inst'), may hold values from 0 to 255, as said below
- move_count: int32 [4, 4], replicated, may hold values from 0 to 32, as said below
- conv_weight: float32 [4, 16384], P(None, 'tp'), may hold values from -3 to 3
- conv_bias: float32 [16384], P('tp'), may hold values from -3 to 3
- delta_down: bfloat16 [16384, 512], P('tp'), may hold values from -0.046875 to 0.046875
- state_proj: bfloat16 [32, 16384], P(None, 'tp'), may hold values from -0.046875 to 0.046875
- delta_up: bfloat16 [512, 16384], P(None, 'tp'), may hold values from -0.25 to 0.25
- delta_bias: float32 [16384], P('tp'), may hold values from -3 to 1
- decay_log: float32 [16, 16384], P(None, 'tp'), may hold values from 0 to 2.77
- skip_gain: float32 [16384], P('tp'), may hold values from 0.5 to 2
- out_weight: bfloat16 [16384, 8192], P('tp'), may hold values from -0.09375 to 0.09375
- residual: bfloat16 [4, 1024, 8192], P(None, 'inst', 'tp'), may hold values from -30 to 30
- norm_gain: float32 [8192], replicated, may hold values from 0.5 to 1.5
Outputs:
- normed: bfloat16 [4, 1024, 8192], P(None, 'inst', 'tp')
- final_state: float32 [1024, 16, 16384], P('inst', None, 'tp')
The draws below stay inside these ranges and needn't reach their ends.
Inputs may be any that keep to these rules, and one draw needn't show every extreme that they name: For k < move_count[i, j], leave_slot[i, j, k] are distinct slots of instance i over all j and k; entries at k >= move_count[i, j] are ignored. For k < move_count[i, j], land_slot[i, j, k] are distinct slots of instance j over all i and k, none of them a slot that leaves instance j; their old contents are overwritten. Entries at k >= move_count[i, j] are ignored. `move_count`: zero on the diagonal. In every draw one instance receives exactly 32 requests from each other instance.
All inputs are finite; a program needn't handle non-finite values.
Results may differ from the reference program's by a relative error of at most 0.025.
Values may be sent and summed in bfloat16 or wider, within the bound.
A program may use at most 192 MiB of HBM per device.

```python
import jax
import jax.numpy as jnp
from jax import lax

D = 8192
DI = 16384
NS = 16
RK = 512
CONVW = 4
STEPS = 4
REQ = 256
SLOTS = 1024
CAP = 32
N_INST = 4


def migration_plan(key):
    count_key, busy_key, order_key = jax.random.split(key, 3)
    counts = jax.random.randint(count_key, (N_INST, N_INST), 0, CAP + 1)
    busiest = jax.random.randint(busy_key, (), 0, N_INST)
    inst_ids = jnp.arange(N_INST, dtype=jnp.int32)
    counts = jnp.where(inst_ids[None, :] == busiest, CAP, counts)
    counts = jnp.where(inst_ids[:, None] == inst_ids[None, :], 0, counts).astype(jnp.int32)
    orders = jax.vmap(lambda sub_key: jax.random.permutation(sub_key, REQ))(jax.random.split(order_key, N_INST)).astype(jnp.int32)
    lane_index = jnp.arange(CAP, dtype=jnp.int32)
    send_offset = jnp.cumsum(counts, axis=1) - counts
    recv_offset = jnp.cumsum(counts, axis=0) - counts
    send_place = jnp.minimum(send_offset[:, :, None] + lane_index, REQ - 1)
    recv_place = jnp.minimum(recv_offset[:, :, None] + lane_index, REQ - 1)
    leaving = orders[inst_ids[:, None, None], send_place]
    landing = orders[inst_ids[None, :, None], REQ - 1 - recv_place]
    return (leaving.astype(jnp.int32), landing.astype(jnp.int32), counts)


def draw_leave_slot(key, part):
    return migration_plan(key)[0]


def draw_land_slot(key, part):
    return migration_plan(key)[1]


def draw_move_count(key, part):
    return migration_plan(key)[2]


def draw_residual(key, part):
    key = jax.random.fold_in(key, 11)
    noise_key, row_key = jax.random.split(key, 2)
    columns = 0.2 * 10.0 ** (jnp.arange(D, dtype=jnp.float32) / D)
    row_scale = 0.2 * 10.0 ** jax.random.uniform(row_key, (STEPS, SLOTS, 1), jnp.float32)
    noise = jnp.clip(jax.random.normal(noise_key, (STEPS, SLOTS, D), jnp.float32), -6.0, 6.0)
    values = noise * row_scale * columns
    return values.astype(jnp.bfloat16)


def spiked(drawn, own_key, source, target, blocks, factor):
    def block_of(position):
        return (jnp.arange(drawn.shape[position]) // (drawn.shape[position] // blocks)).reshape((-1,) + (1,) * (drawn.ndim - 1 - position))

    first = jax.random.permutation(own_key, blocks)[block_of(target)]
    second = (block_of(target) + blocks // 2) % blocks
    return jnp.where((block_of(source) == first) | (block_of(source) == second), factor * drawn, drawn)


def block_scale(rng, dims, cuts, least, largest):
    def one(position, shards_of):
        heights = jax.random.uniform(jax.random.fold_in(jax.random.fold_in(rng, 6), position), (shards_of,), jnp.float32, least / len(cuts), largest / len(cuts))
        return jnp.repeat(jnp.exp(heights), dims[position] // shards_of).reshape((-1,) + (1,) * (len(dims) - position - 1))

    level = one(*cuts[0])
    for cut in cuts[1:]:
        level = level * one(*cut)
    return level


def scatter_about(stream_key, shape, deviation, limit, shards=(), held_as=jnp.bfloat16):
    loudness = block_scale(stream_key, shape, shards, -0.22, 0.18) if shards else 1.0
    entries = jax.random.normal(stream_key, shape, jnp.float32) * deviation * loudness
    return jnp.minimum(jnp.maximum(entries, -limit), limit).astype(held_as)


def gaussian_with(rng, shape, spread, bound, pieces, heavy, kind=jnp.bfloat16):
    drawn = spread * jax.random.normal(rng, shape, jnp.float32)
    if pieces:
        drawn = drawn * block_scale(rng, shape, pieces, -0.22, 0.18)
    return jnp.clip(spiked(drawn, jax.random.fold_in(rng, 3), *heavy), -bound, bound).astype(kind)


def setup_inputs(seed: int = 0) -> dict:
    key_of = jax.random.split(jax.random.key(seed), 19)
    mixer_input = scatter_about(key_of[0], (STEPS, SLOTS, DI), 1.0, 6.0, ((1, 4), (2, 32)))
    gate_input = scatter_about(key_of[1], (STEPS, SLOTS, DI), 1.0, 6.0, ((1, 4), (2, 32)))
    conv_state = scatter_about(key_of[2], (SLOTS, CONVW - 1, DI), 1.0, 6.0, ((0, 4), (2, 32)))
    scan_state = scatter_about(key_of[3], (SLOTS, NS, DI), 1.0, 6.0, ((0, 4), (2, 32)), jnp.float32)
    leave_slot = draw_leave_slot(jax.random.fold_in(key_of[18], 71), 0)
    land_slot = draw_land_slot(jax.random.fold_in(key_of[18], 71), 0)
    move_count = draw_move_count(jax.random.fold_in(key_of[18], 71), 0)
    conv_weight = scatter_about(key_of[7], (CONVW, DI), CONVW ** -0.5, 3.0, ((1, 32),), jnp.float32)
    conv_bias = scatter_about(key_of[8], (DI,), 0.5, 3.0, ((0, 32),), jnp.float32)
    delta_down = scatter_about(key_of[9], (DI, RK), DI ** -0.5, 0.046875, ((0, 32),))
    state_proj = scatter_about(key_of[10], (2 * NS, DI), DI ** -0.5, 0.046875, ((1, 32),))
    delta_up = scatter_about(key_of[11], (RK, DI), RK ** -0.5, 0.25, ((1, 32),))
    delta_bias = jnp.clip(-3.0 + 4.0 * jax.random.uniform(key_of[12], (DI,), jnp.float32) ** block_scale(key_of[12], (DI,), ((0, 32),), -0.2, 0.2), -3.0, 1.0)
    decay_log = jnp.clip(2.77 * jax.random.uniform(key_of[13], (NS, DI), jnp.float32) ** block_scale(key_of[13], (NS, DI), ((1, 32),), -0.2, 0.2), 0.0, 2.77)
    skip_gain = jnp.clip(0.5 + 1.5 * jax.random.uniform(key_of[14], (DI,), jnp.float32) ** block_scale(key_of[14], (DI,), ((0, 32),), -0.2, 0.2), 0.5, 2.0)
    out_weight = gaussian_with(key_of[15], (DI, D), DI ** -0.5, 0.09375, ((0, 32),), (0, 1, 32, 2.75))
    residual = draw_residual(jax.random.fold_in(key_of[18], 71), 0)
    norm_gain = jnp.clip(1.0 + 0.1 * jax.random.normal(key_of[17], (D,), jnp.float32), 0.5, 1.5)
    return {"mixer_input": mixer_input, "gate_input": gate_input, "conv_state": conv_state, "scan_state": scan_state, "leave_slot": leave_slot, "land_slot": land_slot, "move_count": move_count, "conv_weight": conv_weight, "conv_bias": conv_bias, "delta_down": delta_down, "state_proj": state_proj, "delta_up": delta_up, "delta_bias": delta_bias, "decay_log": decay_log, "skip_gain": skip_gain, "out_weight": out_weight, "residual": residual, "norm_gain": norm_gain}


EPSILON = 1e-05

def conv_mix(history, conv_weight, conv_bias):
    total = conv_bias + conv_weight[0] * history[0:STEPS].astype(jnp.float32)
    for offset in range(1, CONVW):
        total = total + conv_weight[offset] * history[offset:offset + STEPS].astype(jnp.float32)
    return jax.nn.silu(total).astype(jnp.bfloat16)

def recurrence(carried, delta_all, conv_out, gate_input, input_terms, output_terms, decay_rate, skip_gain):
    outputs = []
    for moment in range(STEPS):
        step_rate = delta_all[moment]
        signal = conv_out[moment].astype(jnp.float32)
        inject = jnp.transpose(input_terms[:, moment, :])[:, :, None] * (step_rate * signal)[:, None, :]
        carried = jnp.exp(step_rate[:, None, :] * decay_rate[None]) * carried + inject
        readout = lax.optimization_barrier(jnp.sum(carried * jnp.transpose(output_terms[:, moment, :])[:, :, None], axis=1)) + skip_gain * signal
        outputs.append((readout * jax.nn.silu(gate_input[moment].astype(jnp.float32))).astype(jnp.bfloat16))
    return (carried, jnp.stack(outputs))

def migrate(scan_state, conv_state, leave_slot, land_slot, move_count):
    slot_total = N_INST * REQ
    lane_index = jnp.arange(CAP, dtype=jnp.int32)
    usable = lane_index[None, None, :] < move_count[:, :, None]
    slot_base = jnp.arange(N_INST, dtype=jnp.int32) * REQ
    source = slot_base[:, None, None] + leave_slot
    target = slot_base[None, :, None] + land_slot
    leaving = jnp.where(usable, source, slot_total).reshape(-1)
    landing = jnp.where(usable, target, slot_total).reshape(-1)
    keeper = jnp.ones((slot_total,), jnp.float32).at[leaving].set(0.0, mode='drop')
    picked = source.reshape(-1)
    state_now = (scan_state * keeper[:, None, None]).at[landing].set(scan_state[picked], mode='drop')
    conv_now = (conv_state * keeper[:, None, None].astype(conv_state.dtype)).at[landing].set(conv_state[picked], mode='drop')
    return (state_now, conv_now)

def by_instance(values):
    return jnp.transpose(values.reshape(STEPS, N_INST, REQ, DI), (1, 0, 2, 3))

def reference(mixer_input, gate_input, conv_state, scan_state, leave_slot, land_slot, move_count, conv_weight, conv_bias, delta_down, state_proj, delta_up, delta_bias, decay_log, skip_gain, out_weight, residual, norm_gain):
    state_now, conv_now = migrate(scan_state, conv_state, leave_slot, land_slot, move_count)
    history = jnp.concatenate([jnp.transpose(conv_now, (1, 0, 2)), mixer_input], axis=0)
    conv_out = conv_mix(history, conv_weight, conv_bias)
    flat_rows = conv_out.reshape(STEPS * SLOTS, DI)
    delta_low = jnp.dot(flat_rows, delta_down, preferred_element_type=jnp.float32)
    io_terms = lax.dot_general(state_proj, flat_rows, (((1,), (1,)), ((), ())), preferred_element_type=jnp.float32)
    delta_all = jax.nn.softplus(jnp.dot(delta_low.astype(jnp.bfloat16), delta_up, preferred_element_type=jnp.float32) + delta_bias)
    decay_rate = -jnp.exp(decay_log)
    io_split = jnp.transpose(io_terms.reshape(2 * NS, STEPS, N_INST, REQ), (2, 0, 1, 3))

    def per_instance(packed):
        carried, delta_part, conv_part, gate_part, io_part = packed
        return recurrence(carried, delta_part, conv_part, gate_part, io_part[:NS], io_part[NS:], decay_rate, skip_gain)
    final_state, gated = lax.map(per_instance, (state_now.reshape(N_INST, REQ, NS, DI), by_instance(delta_all), by_instance(conv_out), by_instance(gate_input), io_split))
    gated_rows = jnp.transpose(gated, (1, 0, 2, 3)).reshape(STEPS * SLOTS, DI)
    mixed = jnp.dot(gated_rows, out_weight, preferred_element_type=jnp.float32)
    hidden_sum = residual.reshape(STEPS * SLOTS, D).astype(jnp.float32) + mixed
    mean_square = lax.optimization_barrier(jnp.mean(hidden_sum * hidden_sum, axis=1, keepdims=True))
    normed = (hidden_sum * lax.rsqrt(mean_square + EPSILON) * norm_gain).astype(jnp.bfloat16)
    return (normed.reshape(STEPS, SLOTS, D), final_state.reshape(SLOTS, NS, DI))
```

```python
import jax
import jax.numpy as jnp
from jax import lax
from jax.experimental import pallas as pl
from jax.experimental.pallas import tpu as pltpu
from jax.sharding import PartitionSpec as P

D = 8192
NS = 16
STEPS = 4
EPSILON = 1e-05
LOG2E = 1.4426950408889634
MESH = pl.DeviceIdType.MESH
F32 = jnp.float32
BF16 = jnp.bfloat16

PAIRS = (1, 8, 3, 24, 4)
LEVELS = 5
GROUP = 16
PART_ROWS = (208, 208, 208, 208, 192)


def flips():
    me = lax.axis_index("tp")
    return me, [(1 << bit) * (1 - 2 * ((me // (1 << bit)) % 2)) for bit in range(5)]


def flipped(place, mask):
    me, delta = place
    for bit in range(5):
        if (mask >> bit) & 1:
            me = me + delta[bit]
    return me


def pair_of(part, level):
    return PAIRS[(part + level) % LEVELS]


def mask_of(part, code):
    mask = 0
    for level in range(LEVELS):
        if (code >> (4 - level)) & 1:
            mask ^= pair_of(part, level)
    return mask


def tp_device(index):
    return (lax.axis_index("inst"), index)


def inst_partner(mask):
    inst = lax.axis_index("inst")
    core, low = inst % 2, inst // 2
    if mask & 1:
        core = 1 - core
    if mask & 2:
        low = 1 - low
    return low * 2 + core


def dot_nt(a, b):
    return lax.dot_general(a, b, (((1,), (1,)), ((), ())), preferred_element_type=F32)


def dot_tn(a, b):
    return lax.dot_general(a, b, (((0,), (0,)), ((), ())), preferred_element_type=F32)


def dot_nn(a, b):
    return jnp.dot(a, b, preferred_element_type=F32)


def project_kernel(
    leave_smem, leave_ref, land_ref, count_ref, mix_ref, conv_ref, state_ref, weight_ref, bias_ref,
    down_ref, proj_ref,
    low_out, io_out, u_out, map_out, moved_out,
    state_v, pack_conv, got_conv, pack_state, got_state, low, io, snd, rcv, ag, snd_io, rcv_io, ag_io,
    state_sem, conv_ss, conv_rs, mig_ss, mig_rs, out_sem, rs_ss, rs_rs, ag_ss, ag_rs,
):
    place = flips()
    inst = lax.axis_index("inst")
    state_copy = pltpu.make_async_copy(state_ref, state_v, state_sem)
    state_copy.start()
    barrier = pltpu.get_barrier_semaphore()
    for mask in PAIRS:
        pl.semaphore_signal(
            barrier, inc=1, device_id=tp_device(flipped(place, mask)), device_id_type=MESH
        )
    for mask in (1, 2, 3):
        pl.semaphore_signal(
            barrier, inc=1, device_id=(inst_partner(mask), place[0]), device_id_type=MESH
        )
    pl.semaphore_wait(barrier, len(PAIRS) + 3)

    lanes = lax.broadcasted_iota(jnp.int32, (1, 32), 1)
    leave_row = jnp.concatenate(
        [jnp.where(lanes < count_ref[inst, j], leave_ref[0, j : j + 1, :], -1) for j in range(4)], axis=1
    )
    land_row = jnp.concatenate(
        [jnp.where(lanes < count_ref[j, inst], land_ref[j], -1) for j in range(4)], axis=1
    )
    slots = lax.broadcasted_iota(jnp.int32, (256, 128), 0)
    leave_hot = jnp.where(slots == leave_row, 1.0, 0.0)
    land_hot = jnp.where(slots == land_row, 1.0, 0.0)
    keep = 1.0 - jnp.sum(leave_hot + land_hot, axis=1, keepdims=True)
    leave_hot = leave_hot.astype(BF16)
    land_hot = land_hot.astype(BF16)

    for k in range(3):
        pack_conv[:, k] = dot_tn(leave_hot, conv_ref[k]).astype(BF16).reshape(4, 32, 512)
    conv_copies = []
    for mask in (1, 2, 3):
        other = inst_partner(mask)
        copy = pltpu.make_async_remote_copy(
            pack_conv.at[other], got_conv.at[inst], conv_ss.at[mask - 1], conv_rs.at[mask - 1],
            device_id=(other, place[0]), device_id_type=MESH,
        )
        copy.start()
        conv_copies.append(copy)
    got_conv[inst] = jnp.zeros((3, 32, 512), BF16)

    number = (lax.broadcasted_iota(jnp.int32, (8, 128), 1) + 1).astype(F32).astype(BF16)
    landed = dot_nt(number, land_hot)
    left = dot_nt(jnp.ones((8, 128), BF16), leave_hot)
    map_out[...] = (landed - left - 1.0).astype(jnp.int32)

    taps = [weight_ref[k : k + 1, :] for k in range(4)]
    bias = bias_ref[...]

    def step(t, history):
        total = bias
        for k in range(4):
            source = history[t + k] if t + k < 3 else mix_ref[t + k - 3].astype(F32)
            total = total + taps[k] * source
        u = jax.nn.silu(total).astype(BF16)
        u_out[t] = u
        low[t, 0:16] = dot_nn(u, down_ref[:, 0:256]).reshape(16, 16, 256)
        low[t, 16:32] = dot_nn(u, down_ref[:, 256:512]).reshape(16, 16, 256)
        return u

    def rs_copy(p, k):
        lo, hi = 1 << (4 - k), 2 << (4 - k)
        s, r = (snd.at[p], rcv.at[p]) if p < 4 else (snd_io, rcv_io)
        return pltpu.make_async_remote_copy(
            s.at[lo:hi], r.at[lo:hi], rs_ss.at[p, k], rs_rs.at[p, k],
            device_id=tp_device(flipped(place, pair_of(p, k))), device_id_type=MESH,
        )

    def summed(p, code, k):
        owner = flipped(place, mask_of(p, code))
        acc = low[p, owner] if p < 4 else io[owner]
        for j in range(k):
            more = rcv[p, (1 << (4 - j)) + code] if p < 4 else rcv_io[(1 << (4 - j)) + code]
            acc = acc + more.astype(F32)
        return acc

    def rs_level(p, k):
        if k:
            rs_copy(p, k - 1).wait_recv()
        for code in range(1 << (4 - k), 2 << (4 - k)):
            acc = summed(p, code, k)
            if p < 4:
                snd[p, code] = acc.astype(BF16)
            else:
                snd_io[code] = acc
        rs_copy(p, k).start()

    us = [None] * 4
    us[3] = step(3, None)
    rs_level(3, 0)

    state_copy.wait()
    state_copies = []
    for mask in (1, 2, 3):
        other = inst_partner(mask)

        def pack(i, carry):
            pack_state[other, i] = state_v[leave_smem[0, other, i]].astype(BF16)
            return carry

        lax.fori_loop(0, 32, pack, 0, unroll=4)
        copy = pltpu.make_async_remote_copy(
            pack_state.at[other], got_state.at[inst], mig_ss.at[mask - 1], mig_rs.at[mask - 1],
            device_id=(other, place[0]), device_id_type=MESH,
        )
        copy.start()
        state_copies.append(copy)

    for copy in conv_copies:
        copy.wait_recv()
    history = []
    for k in range(3):
        moved = dot_nn(land_hot, got_conv[:, k].reshape(128, 512))
        history.append(conv_ref[k].astype(F32) * keep + moved)
    for t in range(3):
        us[t] = step(t, history)
        rs_level(t, 0)
    proj = proj_ref[...]
    total = jnp.zeros((256, 128), F32)
    for t in range(4):
        pieces = [jnp.zeros_like(proj) if j != t else proj for j in range(4)]
        total = total + dot_nt(us[t], jnp.concatenate(pieces, axis=0))
    io[...] = total.reshape(32, 8, 128)
    rs_level(4, 0)
    order = (3, 0, 1, 2, 4)
    for k in range(1, LEVELS):
        for p in order:
            rs_level(p, k)

    def ag_copy(p, k):
        n = 1 << (4 - k)
        a = ag.at[p] if p < 4 else ag_io
        return pltpu.make_async_remote_copy(
            a.at[0:n], a.at[n : 2 * n], ag_ss.at[p, k], ag_rs.at[p, k],
            device_id=tp_device(flipped(place, pair_of(p, k))), device_id_type=MESH,
        )

    for p in order:
        rs_copy(p, 4).wait_recv()
        acc = summed(p, 0, LEVELS)
        if p < 4:
            ag[p, 0] = acc.astype(BF16)
        else:
            ag_io[0] = acc
        ag_copy(p, 4).start()
    for k in range(3, -1, -1):
        for p in order:
            ag_copy(p, k + 1).wait_recv()
            ag_copy(p, k).start()
    for p in order:
        ag_copy(p, 0).wait_recv()
        for code in range(32):
            owner = flipped(place, mask_of(p, code))
            if p < 4:
                low_out[p, owner] = ag[p, code]
            else:
                io_out[owner] = ag_io[code]

    outs = []
    for mask in (1, 2, 3):
        state_copies[mask - 1].wait_recv()
        other = inst_partner(mask)
        copy = pltpu.make_async_copy(got_state.at[other], moved_out.at[other], out_sem.at[mask - 1])
        copy.start()
        outs.append(copy)
    for copy in conv_copies + state_copies:
        copy.wait_send()
    for p in range(5):
        for k in range(LEVELS):
            rs_copy(p, k).wait_send()
            ag_copy(p, k).wait_send()
    for copy in outs:
        copy.wait()


def project(leave, land, count, mix, conv, state, weight, bias, down, proj):
    vmem = pl.BlockSpec(memory_space=pltpu.VMEM)
    smem = pl.BlockSpec(memory_space=pltpu.SMEM)
    hbm = pl.BlockSpec(memory_space=pl.ANY)
    return pl.pallas_call(
        project_kernel,
        out_shape=(
            jax.ShapeDtypeStruct((4, 32, 16, 256), BF16),
            jax.ShapeDtypeStruct((32, 8, 128), F32),
            jax.ShapeDtypeStruct((4, 256, 512), BF16),
            jax.ShapeDtypeStruct((8, 256), jnp.int32),
            jax.ShapeDtypeStruct((4, 32, 16, 512), BF16),
        ),
        in_specs=[smem, vmem, vmem, smem, vmem, vmem, hbm, vmem, vmem, vmem, vmem],
        out_specs=(vmem, vmem, vmem, vmem, hbm),
        scratch_shapes=[
            pltpu.VMEM((256, 16, 512), F32),
            pltpu.VMEM((4, 3, 32, 512), BF16),
            pltpu.VMEM((4, 3, 32, 512), BF16),
            pltpu.VMEM((4, 32, 16, 512), BF16),
            pltpu.VMEM((4, 32, 16, 512), BF16),
            pltpu.VMEM((4, 32, 16, 256), F32),
            pltpu.VMEM((32, 8, 128), F32),
            pltpu.VMEM((4, 32, 16, 256), BF16),
            pltpu.VMEM((4, 32, 16, 256), BF16),
            pltpu.VMEM((4, 32, 16, 256), BF16),
            pltpu.VMEM((32, 8, 128), F32),
            pltpu.VMEM((32, 8, 128), F32),
            pltpu.VMEM((32, 8, 128), F32),
            pltpu.SemaphoreType.DMA,
            pltpu.SemaphoreType.DMA((3,)),
            pltpu.SemaphoreType.DMA((3,)),
            pltpu.SemaphoreType.DMA((3,)),
            pltpu.SemaphoreType.DMA((3,)),
            pltpu.SemaphoreType.DMA((3,)),
            pltpu.SemaphoreType.DMA((5, 5)),
            pltpu.SemaphoreType.DMA((5, 5)),
            pltpu.SemaphoreType.DMA((5, 5)),
            pltpu.SemaphoreType.DMA((5, 5)),
        ],
        compiler_params=pltpu.CompilerParams(
            collective_id=0, has_side_effects=True, vmem_limit_bytes=50 << 20
        ),
        name="project",
    )(leave, leave, land, count, mix, conv, state, weight, bias, down, proj)


def recur_kernel(
    map_ref, low_ref, io_ref, up_ref, dbias_ref, decay_ref, skip_ref, u_ref, gate_ref, state_ref, moved_ref,
    final_ref, gated_ref,
    delta, bbd, cbd, inject, held, decay,
):
    group = pl.program_id(0)

    @pl.when(group == 0)
    def _():
        decay[...] = jnp.exp(decay_ref[...]) * (-LOG2E)
        io = io_ref[...].astype(BF16)
        row = lax.broadcasted_iota(jnp.int32, (128, 256), 0)
        lane = lax.broadcasted_iota(jnp.int32, (128, 256), 1)
        slot = lax.broadcasted_iota(jnp.int32, (256, 256), 0)
        across = lax.broadcasted_iota(jnp.int32, (256, 256), 1)
        same = (slot % GROUP) == (across // NS)
        for t in range(STEPS):
            for offset, kept in ((0, bbd), (NS, cbd)):
                spread = jnp.where(row == (lane % NS) + (2 * NS * t + offset), 1.0, 0.0).astype(BF16)
                kept[t] = jnp.where(same, dot_nn(io, spread), 0.0).astype(BF16)
            rate = dot_nn(low_ref[t, 0], up_ref[0:256, :]) + dot_nn(low_ref[t, 1], up_ref[256:512, :])
            delta[t] = jax.nn.softplus(rate + dbias_ref[...])

    base = pl.multiple_of(group * GROUP, GROUP)
    for s in range(GROUP):
        source = map_ref[0, base + s]
        moved = moved_ref[jnp.maximum(source, 0)].astype(F32)
        final_ref[s] = jnp.where(source >= 0, moved, jnp.where(source == -1, state_ref[s], 0.0))
    for t in range(STEPS):
        u = u_ref[t].astype(F32)
        here = delta[t, pl.ds(base, GROUP), :]
        inject[...] = dot_tn(bbd[t, pl.ds(base, GROUP), :], (here * u).astype(BF16))
        for s in range(GROUP):
            rate = delta[t, pl.ds(base + s, 1), :]
            carried = final_ref[s] * jnp.exp2(rate * decay[...]) + inject[NS * s : NS * s + NS, :]
            final_ref[s] = carried
            held[NS * s : NS * s + NS, :] = carried.astype(BF16)
        readout = dot_nn(cbd[t, pl.ds(base, GROUP), :], held[...]) + skip_ref[...] * u
        gated_ref[t] = (readout * jax.nn.silu(gate_ref[t].astype(F32))).astype(BF16)


def recur(source, low, io, up, dbias, decay, skip, u, gate, state, moved):
    smem = pl.BlockSpec(memory_space=pltpu.SMEM)
    vmem = pl.BlockSpec(memory_space=pltpu.VMEM)
    steps = pl.BlockSpec((STEPS, GROUP, 512), lambda g: (0, g, 0))
    slots = pl.BlockSpec((GROUP, NS, 512), lambda g: (g, 0, 0))
    return pl.pallas_call(
        recur_kernel,
        grid=(256 // GROUP,),
        out_shape=(
            jax.ShapeDtypeStruct((256, NS, 512), F32),
            jax.ShapeDtypeStruct((STEPS, 256, 512), BF16),
        ),
        in_specs=[smem, vmem, vmem, vmem, vmem, vmem, vmem, steps, steps, slots, vmem],
        out_specs=(slots, steps),
        scratch_shapes=[
            pltpu.VMEM((STEPS, 256, 512), F32),
            pltpu.VMEM((STEPS, 256, 256), BF16),
            pltpu.VMEM((STEPS, 256, 256), BF16),
            pltpu.VMEM((NS * GROUP, 512), F32),
            pltpu.VMEM((NS * GROUP, 512), BF16),
            pltpu.VMEM((NS, 512), F32),
        ],
        compiler_params=pltpu.CompilerParams(vmem_limit_bytes=40 << 20),
        name="recur",
    )(source, low, io, up, dbias, decay, skip, u, gate, state, moved)


SUM_MASKS = ((1, 2, 3), (8, 16, 24), (4,))


def mix_kernel(
    gated_ref, weight_hbm, residual_ref, gain_ref,
    out_ref,
    weight, snd, rcv, hidden, sums, got_sums,
    weight_sem, ss, rs, sum_ss, sum_rs,
):
    place = flips()
    me, delta = place
    weight_copy = pltpu.make_async_copy(weight_hbm, weight, weight_sem)
    weight_copy.start()
    barrier = pltpu.get_barrier_semaphore()
    masks = [mask for group in SUM_MASKS for mask in group]
    for mask in masks:
        pl.semaphore_signal(
            barrier, inc=1, device_id=tp_device(flipped(place, mask)), device_id_type=MESH
        )
    pl.semaphore_wait(barrier, len(masks))
    weight_copy.wait()

    starts = [sum(PART_ROWS[:p]) for p in range(5)]

    def copy_of(p, code, level):
        rows = PART_ROWS[p]
        return pltpu.make_async_remote_copy(
            snd.at[p, code, 0:rows], rcv.at[p, code, 0:rows], ss.at[p, code], rs.at[p, code],
            device_id=tp_device(flipped(place, pair_of(p, level))), device_id_type=MESH,
        )

    def summed(p, code, level, bits):
        flip = [0] * 5
        for j in range(LEVELS):
            for bit in range(5):
                if (pair_of(p, j) >> bit) & 1:
                    flip[bit] = flip[bit] + bits[j]
        owner = me
        for bit in range(5):
            owner = owner + (flip[bit] % 2) * delta[bit]
        columns = pl.ds(pl.multiple_of(owner * 256, 256), 256)
        rows = PART_ROWS[p]
        acc = dot_nn(gated_ref[starts[p] : starts[p] + rows, :], weight[:, columns])
        for j in range(level):
            copy_of(p, (1 << (4 - j)) + code, j).wait_recv()
            acc = acc + rcv[p, (1 << (4 - j)) + code, 0:rows].astype(F32)
        return acc

    for level in range(LEVELS):
        n = 1 << (4 - level)

        def send(i, carry):
            code = 2 * n - 1 - i
            bits = [0] * level + [1] + [(code // (1 << (4 - j))) % 2 for j in range(level + 1, LEVELS)]
            for p in range(5):
                acc = summed(p, code, level, bits)
                snd[p, code, 0 : PART_ROWS[p]] = acc.astype(BF16)
                copy_of(p, code, level).start()
            return carry

        lax.fori_loop(0, n, send, 0)

    for p in range(5):
        rows = PART_ROWS[p]
        acc = summed(p, 0, LEVELS, [0] * LEVELS)
        acc = acc + residual_ref[starts[p] : starts[p] + rows, :].astype(F32)
        hidden[starts[p] : starts[p] + rows, :] = acc
    sums[0] = jnp.zeros((8, 256), F32)
    which = lax.broadcasted_iota(jnp.int32, (8, 256), 0)
    for p in range(5):
        rows = PART_ROWS[p]
        acc = hidden[starts[p] : starts[p] + rows, :]
        pick = jnp.where(which == p, 1.0, 0.0)
        squares = lax.dot_general(
            pick, acc * acc, (((1,), (1,)), ((), ())), preferred_element_type=F32,
            precision=lax.Precision.HIGHEST,
        )
        sums[0, :, 0:rows] = sums[0, :, 0:rows] + squares
    slot = 0
    sum_copies = []
    for stage, group in enumerate(SUM_MASKS):
        here = []
        for mask in group:
            copy = pltpu.make_async_remote_copy(
                sums.at[stage], got_sums.at[slot], sum_ss.at[slot], sum_rs.at[slot],
                device_id=tp_device(flipped(place, mask)), device_id_type=MESH,
            )
            copy.start()
            here.append((copy, slot))
            slot += 1
        total = sums[stage]
        for copy, index in here:
            copy.wait_recv()
            total = total + got_sums[index]
            sum_copies.append(copy)
        sums[stage + 1] = total
    scale = lax.rsqrt(sums[len(SUM_MASKS)] * (1.0 / D) + EPSILON)
    gain = gain_ref[:, pl.ds(pl.multiple_of(me * 256, 256), 256)]
    for p in range(5):
        rows = PART_ROWS[p]
        pick = jnp.where(which == p, 1.0, 0.0)
        factor = lax.dot_general(
            scale[:, 0:rows], pick, (((0,), (0,)), ((), ())), preferred_element_type=F32,
            precision=lax.Precision.HIGHEST,
        )
        acc = hidden[starts[p] : starts[p] + rows, :]
        out_ref[starts[p] : starts[p] + rows, :] = (acc * factor * gain).astype(BF16)

    for copy in sum_copies:
        copy.wait_send()
    for level in range(LEVELS):
        n = 1 << (4 - level)

        def drain(i, carry):
            for p in range(5):
                copy_of(p, n + i, level).wait_send()
            return carry

        lax.fori_loop(0, n, drain, 0)


def mix(gated, weight, residual, gain):
    vmem = pl.BlockSpec(memory_space=pltpu.VMEM)
    hbm = pl.BlockSpec(memory_space=pl.ANY)
    return pl.pallas_call(
        mix_kernel,
        out_shape=jax.ShapeDtypeStruct((1024, 256), BF16),
        in_specs=[vmem, hbm, vmem, vmem],
        out_specs=vmem,
        scratch_shapes=[
            pltpu.VMEM((512, D), BF16),
            pltpu.VMEM((5, 32, 208, 256), BF16),
            pltpu.VMEM((5, 32, 208, 256), BF16),
            pltpu.VMEM((1024, 256), F32),
            pltpu.VMEM((4, 8, 256), F32),
            pltpu.VMEM((7, 8, 256), F32),
            pltpu.SemaphoreType.DMA,
            pltpu.SemaphoreType.DMA((5, 32)),
            pltpu.SemaphoreType.DMA((5, 32)),
            pltpu.SemaphoreType.DMA((7,)),
            pltpu.SemaphoreType.DMA((7,)),
        ],
        compiler_params=pltpu.CompilerParams(
            collective_id=1, has_side_effects=True, vmem_limit_bytes=60 << 20
        ),
        name="mix",
    )(gated, weight, residual, gain)


def on_device(
    mixer_input,
    gate_input,
    conv_state,
    scan_state,
    leave_slot,
    land_slot,
    move_count,
    conv_weight,
    conv_bias,
    delta_down,
    state_proj,
    delta_up,
    delta_bias,
    decay_log,
    skip_gain,
    out_weight,
    residual,
    norm_gain,
):
    low, io, conv_out, source, moved = project(
        leave_slot, land_slot, move_count, mixer_input, jnp.transpose(conv_state, (1, 0, 2)), scan_state,
        conv_weight, conv_bias.reshape(1, -1), delta_down, state_proj,
    )
    final_state, gated = recur(
        source, low.reshape(4, 2, 256, 256), io.reshape(256, 128), delta_up, delta_bias.reshape(1, -1),
        decay_log, skip_gain.reshape(1, -1), conv_out, gate_input, scan_state, moved.reshape(128, NS, 512),
    )
    normed = mix(
        gated.reshape(1024, 512), out_weight, residual.reshape(1024, 256), norm_gain.reshape(1, -1)
    )
    return (normed.reshape(STEPS, 256, 256), final_state)


def solution(mesh):
    in_specs = (
        P(None, "inst", "tp"),
        P(None, "inst", "tp"),
        P("inst", None, "tp"),
        P("inst", None, "tp"),
        P("inst", None, None),
        P(None, "inst", None),
        P(),
        P(None, "tp"),
        P("tp"),
        P("tp", None),
        P(None, "tp"),
        P(None, "tp"),
        P("tp"),
        P(None, "tp"),
        P("tp"),
        P("tp", None),
        P(None, "inst", "tp"),
        P(),
    )
    out_specs = (P(None, "inst", "tp"), P("inst", None, "tp"))
    return jax.shard_map(
        on_device, mesh=mesh, in_specs=in_specs, out_specs=out_specs, check_vma=False
    )
```

```python
import jax
import jax.numpy as jnp
from jax import lax
from jax.experimental import pallas as pl
from jax.experimental.pallas import tpu as pltpu
from jax.sharding import PartitionSpec as P

D = 8192
NS = 16
STEPS = 4
EPSILON = 1e-05
LOG2E = 1.4426950408889634
MESH = pl.DeviceIdType.MESH
F32 = jnp.float32
BF16 = jnp.bfloat16

PAIRS = (1, 8, 3, 24, 4)
LEVELS = 5
GROUP = 16
PART_ROWS = (208, 208, 208, 208, 192)


def flips():
    me = lax.axis_index("tp")
    return me, [(1 << bit) * (1 - 2 * ((me // (1 << bit)) % 2)) for bit in range(5)]


def flipped(place, mask):
    me, delta = place
    for bit in range(5):
        if (mask >> bit) & 1:
            me = me + delta[bit]
    return me


def pair_of(part, level):
    return PAIRS[(part + level) % LEVELS]


def mask_of(part, code):
    mask = 0
    for level in range(LEVELS):
        if (code >> (4 - level)) & 1:
            mask ^= pair_of(part, level)
    return mask


def tp_device(index):
    return (lax.axis_index("inst"), index)


def inst_partner(mask):
    inst = lax.axis_index("inst")
    core, low = inst % 2, inst // 2
    if mask & 1:
        core = 1 - core
    if mask & 2:
        low = 1 - low
    return low * 2 + core


def dot_nt(a, b):
    return lax.dot_general(a, b, (((1,), (1,)), ((), ())), preferred_element_type=F32)


def dot_tn(a, b):
    return lax.dot_general(a, b, (((0,), (0,)), ((), ())), preferred_element_type=F32)


def dot_nn(a, b):
    return jnp.dot(a, b, preferred_element_type=F32)


SIDES = ((0, 1, 2, 3), (0, 8, 16, 24))
PARTS = (3, 0, 1, 2, 4)
FIRST_STATES = 20


def sum_mask(part, code):
    first, second = SIDES[part % 2], SIDES[1 - part % 2]
    return first[code // 8] ^ second[(code // 2) % 4] ^ (4 * (code % 2))


def sum_moves(part, stage):
    first, second = SIDES[part % 2], SIDES[1 - part % 2]
    if stage == 0:
        return [(c - 1, 8 * c, 8, first[c]) for c in (2, 1, 3)]
    if stage == 1:
        return [(c + 2, 2 * c, 2, second[c]) for c in (2, 1, 3)]
    return [(6, 1, 1, 4)]


def project_kernel(
    leave_hbm, land_hbm, count_hbm, mix_hbm, conv_hbm, state_hbm, weight_hbm, bias_hbm, down_hbm, proj_hbm,
    low_out, io_out, u_out, map_out, moved_out,
    leave_smem, count_ref, leave_ref, land_ref, mix_ref, conv_ref, weight_ref, bias_ref, down_ref, proj_ref,
    state_v, pack_conv, got_conv, pack_state, got_state, low, io, snd, rcv, ag, snd_io, rcv_io, ag_io,
    in_sem, state_sem, conv_ss, conv_rs, mig_ss, mig_rs, out_sem, rs_ss, rs_rs, ag_ss, ag_rs,
):
    place = flips()
    inst = lax.axis_index("inst")
    loads = []
    for source, target in (
        (leave_hbm, leave_smem), (count_hbm, count_ref), (leave_hbm, leave_ref), (land_hbm, land_ref),
        (conv_hbm, conv_ref), (mix_hbm, mix_ref), (weight_hbm, weight_ref), (bias_hbm, bias_ref),
        (down_hbm, down_ref), (proj_hbm, proj_ref),
    ):
        copy = pltpu.make_async_copy(source, target, in_sem.at[len(loads)])
        copy.start()
        loads.append(copy)
    state_copy = pltpu.make_async_copy(state_hbm, state_v, state_sem)
    state_copy.start()
    barrier = pltpu.get_barrier_semaphore()
    masks = SIDES[0][1:] + SIDES[1][1:] + (4,)
    for mask in masks:
        pl.semaphore_signal(
            barrier, inc=1, device_id=tp_device(flipped(place, mask)), device_id_type=MESH
        )
    for mask in (1, 2, 3):
        pl.semaphore_signal(
            barrier, inc=1, device_id=(inst_partner(mask), place[0]), device_id_type=MESH
        )
    for copy in loads:
        copy.wait()

    lanes = lax.broadcasted_iota(jnp.int32, (1, 32), 1)
    leave_row = jnp.concatenate(
        [jnp.where(lanes < count_ref[inst, j], leave_ref[0, j : j + 1, :], -1) for j in range(4)], axis=1
    )
    land_row = jnp.concatenate(
        [jnp.where(lanes < count_ref[j, inst], land_ref[j], -1) for j in range(4)], axis=1
    )
    slots = lax.broadcasted_iota(jnp.int32, (256, 128), 0)
    leave_hot = jnp.where(slots == leave_row, 1.0, 0.0)
    land_hot = jnp.where(slots == land_row, 1.0, 0.0)
    keep = 1.0 - jnp.sum(leave_hot + land_hot, axis=1, keepdims=True)
    leave_hot = leave_hot.astype(BF16)
    land_hot = land_hot.astype(BF16)

    for k in range(3):
        pack_conv[:, k] = dot_tn(leave_hot, conv_ref[k]).astype(BF16).reshape(4, 32, 512)
    got_conv[inst] = jnp.zeros((3, 32, 512), BF16)

    pl.semaphore_wait(barrier, len(masks) + 3)
    conv_copies = []
    for mask in (2, 3, 1):
        other = inst_partner(mask)
        copy = pltpu.make_async_remote_copy(
            pack_conv.at[other], got_conv.at[inst], conv_ss.at[mask - 1], conv_rs.at[mask - 1],
            device_id=(other, place[0]), device_id_type=MESH,
        )
        copy.start()
        conv_copies.append(copy)

    taps = [weight_ref[k : k + 1, :] for k in range(4)]
    bias = bias_ref[...]

    def step(t, history):
        total = bias
        for k in range(4):
            source = history[t + k] if t + k < 3 else mix_ref[t + k - 3].astype(F32)
            total = total + taps[k] * source
        u = jax.nn.silu(total).astype(BF16)
        u_out[t] = u
        low[t, 0:16] = dot_nn(u, down_ref[:, 0:256]).reshape(16, 16, 256)
        low[t, 16:32] = dot_nn(u, down_ref[:, 256:512]).reshape(16, 16, 256)
        return u

    def rs_copy(p, move):
        index, start, size, mask = move
        s, r = (snd.at[p], rcv.at[p]) if p < 4 else (snd_io, rcv_io)
        return pltpu.make_async_remote_copy(
            s.at[start : start + size], r.at[start : start + size], rs_ss.at[p, index], rs_rs.at[p, index],
            device_id=tp_device(flipped(place, mask)), device_id_type=MESH,
        )

    def ag_copy(p, move):
        index, start, size, mask = move
        a = ag.at[p] if p < 4 else ag_io
        return pltpu.make_async_remote_copy(
            a.at[0:size], a.at[start : start + size], ag_ss.at[p, index], ag_rs.at[p, index],
            device_id=tp_device(flipped(place, mask)), device_id_type=MESH,
        )

    def summed(p, code):
        owner = flipped(place, sum_mask(p, code))
        acc = low[p, owner] if p < 4 else io[owner]
        sources = []
        if code < 8:
            sources += [8 * c + code for c in (1, 2, 3)]
        if code < 2:
            sources += [2 * c + code for c in (1, 2, 3)]
        if code == 0:
            sources += [1]
        for index in sources:
            acc = acc + (rcv[p, index] if p < 4 else rcv_io[index]).astype(F32)
        return acc

    def rs_stage(p, stage):
        if stage:
            for move in sum_moves(p, stage - 1):
                rs_copy(p, move).wait_recv()
        for move in sum_moves(p, stage):
            for code in range(move[1], move[1] + move[2]):
                acc = summed(p, code)
                if p < 4:
                    snd[p, code] = acc.astype(BF16)
                else:
                    snd_io[code] = acc
            rs_copy(p, move).start()

    us = [None] * 4
    us[3] = step(3, None)
    rs_stage(3, 0)

    state_copy.wait()
    state_copies = []
    for mask in (2, 3, 1):
        other = inst_partner(mask)

        def pack(i, carry):
            pack_state[other, i] = state_v[leave_smem[0, other, i]].astype(BF16)
            return carry

        lax.fori_loop(0, 32, pack, 0, unroll=4)
        for batch, (lo, hi) in enumerate(((0, FIRST_STATES), (FIRST_STATES, 32))):
            copy = pltpu.make_async_remote_copy(
                pack_state.at[other, lo:hi], got_state.at[inst, lo:hi],
                mig_ss.at[mask - 1, batch], mig_rs.at[mask - 1, batch],
                device_id=(other, place[0]), device_id_type=MESH,
            )
            if batch == 0:
                copy.start()
            state_copies.append((batch, copy))

    for copy in conv_copies:
        copy.wait_recv()
    history = []
    for k in range(3):
        moved = dot_nn(land_hot, got_conv[:, k].reshape(128, 512))
        history.append(conv_ref[k].astype(F32) * keep + moved)
    for t in range(3):
        us[t] = step(t, history)
        rs_stage(t, 0)
    proj = proj_ref[...]
    total = jnp.zeros((256, 128), F32)
    for t in range(4):
        pieces = [jnp.zeros_like(proj) if j != t else proj for j in range(4)]
        total = total + dot_nt(us[t], jnp.concatenate(pieces, axis=0))
    io[...] = total.reshape(32, 8, 128)
    rs_stage(4, 0)

    number = (lax.broadcasted_iota(jnp.int32, (8, 128), 1) + 1).astype(F32).astype(BF16)
    landed = dot_nt(number, land_hot)
    left = dot_nt(jnp.ones((8, 128), BF16), leave_hot)
    map_out[...] = (landed - left - 1.0).astype(jnp.int32)

    for stage in (1, 2):
        for p in PARTS:
            rs_stage(p, stage)
    for p in PARTS:
        for move in sum_moves(p, 2):
            rs_copy(p, move).wait_recv()
        acc = summed(p, 0)
        if p < 4:
            ag[p, 0] = acc.astype(BF16)
        else:
            ag_io[0] = acc
        for move in sum_moves(p, 2):
            ag_copy(p, move).start()
    for stage in (1, 0):
        for p in PARTS:
            for move in sum_moves(p, stage + 1):
                ag_copy(p, move).wait_recv()
            for move in sum_moves(p, stage):
                ag_copy(p, move).start()
        if stage == 1:
            for batch, copy in state_copies:
                if batch == 1:
                    copy.start()
    for p in PARTS:
        for move in sum_moves(p, 0):
            ag_copy(p, move).wait_recv()
        for code in range(32):
            owner = flipped(place, sum_mask(p, code))
            if p < 4:
                low_out[p, owner] = ag[p, code]
            else:
                io_out[owner] = ag_io[code]

    for batch, copy in state_copies:
        copy.wait_recv()
    outs = []
    for mask in (1, 2, 3):
        other = inst_partner(mask)
        copy = pltpu.make_async_copy(got_state.at[other], moved_out.at[other], out_sem.at[mask - 1])
        copy.start()
        outs.append(copy)
    for copy in conv_copies:
        copy.wait_send()
    for batch, copy in state_copies:
        copy.wait_send()
    for p in PARTS:
        for stage in range(3):
            for move in sum_moves(p, stage):
                rs_copy(p, move).wait_send()
                ag_copy(p, move).wait_send()
    for copy in outs:
        copy.wait()


def project(leave, land, count, mix, conv, state, weight, bias, down, proj):
    vmem = pl.BlockSpec(memory_space=pltpu.VMEM)
    hbm = pl.BlockSpec(memory_space=pltpu.HBM)
    return pl.pallas_call(
        project_kernel,
        out_shape=(
            jax.ShapeDtypeStruct((4, 32, 16, 256), BF16),
            jax.ShapeDtypeStruct((32, 8, 128), F32),
            jax.ShapeDtypeStruct((4, 256, 512), BF16),
            jax.ShapeDtypeStruct((8, 256), jnp.int32),
            jax.ShapeDtypeStruct((4, 32, 16, 512), BF16),
        ),
        in_specs=[hbm] * 10,
        out_specs=(vmem, vmem, vmem, vmem, vmem),
        scratch_shapes=[
            pltpu.SMEM((1, 4, 32), jnp.int32),
            pltpu.SMEM((4, 4), jnp.int32),
            pltpu.VMEM((1, 4, 32), jnp.int32),
            pltpu.VMEM((4, 1, 32), jnp.int32),
            pltpu.VMEM((4, 256, 512), BF16),
            pltpu.VMEM((3, 256, 512), BF16),
            pltpu.VMEM((4, 512), F32),
            pltpu.VMEM((1, 512), F32),
            pltpu.VMEM((512, 512), BF16),
            pltpu.VMEM((32, 512), BF16),
            pltpu.VMEM((256, 16, 512), F32),
            pltpu.VMEM((4, 3, 32, 512), BF16),
            pltpu.VMEM((4, 3, 32, 512), BF16),
            pltpu.VMEM((4, 32, 16, 512), BF16),
            pltpu.VMEM((4, 32, 16, 512), BF16),
            pltpu.VMEM((4, 32, 16, 256), F32),
            pltpu.VMEM((32, 8, 128), F32),
            pltpu.VMEM((4, 32, 16, 256), BF16),
            pltpu.VMEM((4, 32, 16, 256), BF16),
            pltpu.VMEM((4, 32, 16, 256), BF16),
            pltpu.VMEM((32, 8, 128), F32),
            pltpu.VMEM((32, 8, 128), F32),
            pltpu.VMEM((32, 8, 128), F32),
            pltpu.SemaphoreType.DMA((10,)),
            pltpu.SemaphoreType.DMA,
            pltpu.SemaphoreType.DMA((3,)),
            pltpu.SemaphoreType.DMA((3,)),
            pltpu.SemaphoreType.DMA((3, 2)),
            pltpu.SemaphoreType.DMA((3, 2)),
            pltpu.SemaphoreType.DMA((3,)),
            pltpu.SemaphoreType.DMA((5, 7)),
            pltpu.SemaphoreType.DMA((5, 7)),
            pltpu.SemaphoreType.DMA((5, 7)),
            pltpu.SemaphoreType.DMA((5, 7)),
        ],
        compiler_params=pltpu.CompilerParams(
            collective_id=0, has_side_effects=True, vmem_limit_bytes=60 << 20
        ),
        name="project",
    )(leave, land, count, mix, conv, state, weight, bias, down, proj)


def recur_kernel(
    map_ref, low_ref, io_ref, up_ref, dbias_ref, decay_ref, skip_ref, u_ref, gate_ref, state_ref, moved_ref,
    final_ref, gated_ref,
    delta, bbd, cbd, inject, held, decay,
):
    group = pl.program_id(0)

    @pl.when(group == 0)
    def _():
        decay[...] = jnp.exp(decay_ref[...]) * (-LOG2E)
        io = io_ref[...].astype(BF16)
        row = lax.broadcasted_iota(jnp.int32, (128, 256), 0)
        lane = lax.broadcasted_iota(jnp.int32, (128, 256), 1)
        slot = lax.broadcasted_iota(jnp.int32, (256, 256), 0)
        across = lax.broadcasted_iota(jnp.int32, (256, 256), 1)
        same = (slot % GROUP) == (across // NS)
        for t in range(STEPS):
            for offset, kept in ((0, bbd), (NS, cbd)):
                spread = jnp.where(row == (lane % NS) + (2 * NS * t + offset), 1.0, 0.0).astype(BF16)
                kept[t] = jnp.where(same, dot_nn(io, spread), 0.0).astype(BF16)
            rate = dot_nn(low_ref[t, 0], up_ref[0:256, :]) + dot_nn(low_ref[t, 1], up_ref[256:512, :])
            delta[t] = jax.nn.softplus(rate + dbias_ref[...])

    base = pl.multiple_of(group * GROUP, GROUP)
    for s in range(GROUP):
        source = map_ref[0, base + s]
        moved = moved_ref[jnp.maximum(source, 0)].astype(F32)
        final_ref[s] = jnp.where(source >= 0, moved, jnp.where(source == -1, state_ref[s], 0.0))
    for t in range(STEPS):
        u = u_ref[t].astype(F32)
        here = delta[t, pl.ds(base, GROUP), :]
        inject[...] = dot_tn(bbd[t, pl.ds(base, GROUP), :], (here * u).astype(BF16))
        for s in range(GROUP):
            rate = delta[t, pl.ds(base + s, 1), :]
            carried = final_ref[s] * jnp.exp2(rate * decay[...]) + inject[NS * s : NS * s + NS, :]
            final_ref[s] = carried
            held[NS * s : NS * s + NS, :] = carried.astype(BF16)
        readout = dot_nn(cbd[t, pl.ds(base, GROUP), :], held[...]) + skip_ref[...] * u
        gated_ref[t] = (readout * jax.nn.silu(gate_ref[t].astype(F32))).astype(BF16)


def recur(source, low, io, up, dbias, decay, skip, u, gate, state, moved):
    smem = pl.BlockSpec(memory_space=pltpu.SMEM)
    vmem = pl.BlockSpec(memory_space=pltpu.VMEM)
    steps = pl.BlockSpec((STEPS, GROUP, 512), lambda g: (0, g, 0))
    slots = pl.BlockSpec((GROUP, NS, 512), lambda g: (g, 0, 0))
    return pl.pallas_call(
        recur_kernel,
        grid=(256 // GROUP,),
        out_shape=(
            jax.ShapeDtypeStruct((256, NS, 512), F32),
            jax.ShapeDtypeStruct((STEPS, 256, 512), BF16),
        ),
        in_specs=[smem, vmem, vmem, vmem, vmem, vmem, vmem, steps, steps, slots, vmem],
        out_specs=(slots, steps),
        scratch_shapes=[
            pltpu.VMEM((STEPS, 256, 512), F32),
            pltpu.VMEM((STEPS, 256, 256), BF16),
            pltpu.VMEM((STEPS, 256, 256), BF16),
            pltpu.VMEM((NS * GROUP, 512), F32),
            pltpu.VMEM((NS * GROUP, 512), BF16),
            pltpu.VMEM((NS, 512), F32),
        ],
        compiler_params=pltpu.CompilerParams(vmem_limit_bytes=60 << 20),
        name="recur",
    )(source, low, io, up, dbias, decay, skip, u, gate, state, moved)


SUM_MASKS = (tuple(a + b for b in SIDES[1] for a in SIDES[0] if a + b), (4,))


def mix_kernel(
    gated_hbm, weight_hbm, residual_hbm, gain_hbm,
    out_ref,
    gated_ref, weight, residual_ref, gain_ref, snd, rcv, hidden, sums, got_sums,
    in_sem, ss, rs, sum_ss, sum_rs,
):
    place = flips()
    me, delta = place
    gain_here = gain_hbm.at[:, pl.ds(pl.multiple_of(me * 256, 256), 256)]
    loads = []
    for source, target in (
        (gated_hbm, gated_ref), (weight_hbm, weight), (residual_hbm, residual_ref), (gain_here, gain_ref)
    ):
        copy = pltpu.make_async_copy(source, target, in_sem.at[len(loads)])
        copy.start()
        loads.append(copy)
    barrier = pltpu.get_barrier_semaphore()
    masks = [mask for group in SUM_MASKS for mask in group]
    for mask in masks:
        pl.semaphore_signal(
            barrier, inc=1, device_id=tp_device(flipped(place, mask)), device_id_type=MESH
        )
    pl.semaphore_wait(barrier, len(masks))
    for copy in loads:
        copy.wait()

    starts = [sum(PART_ROWS[:p]) for p in range(5)]

    def copy_of(p, code, level):
        rows = PART_ROWS[p]
        return pltpu.make_async_remote_copy(
            snd.at[p, code, 0:rows], rcv.at[p, code, 0:rows], ss.at[p, code], rs.at[p, code],
            device_id=tp_device(flipped(place, pair_of(p, level))), device_id_type=MESH,
        )

    def summed(p, code, level, bits):
        flip = [0] * 5
        for j in range(LEVELS):
            for bit in range(5):
                if (pair_of(p, j) >> bit) & 1:
                    flip[bit] = flip[bit] + bits[j]
        owner = me
        for bit in range(5):
            owner = owner + (flip[bit] % 2) * delta[bit]
        columns = pl.ds(pl.multiple_of(owner * 256, 256), 256)
        rows = PART_ROWS[p]
        acc = dot_nn(gated_ref[starts[p] : starts[p] + rows, :], weight[:, columns])
        for j in range(level):
            copy_of(p, (1 << (4 - j)) + code, j).wait_recv()
            acc = acc + rcv[p, (1 << (4 - j)) + code, 0:rows].astype(F32)
        return acc

    for level in range(LEVELS):
        n = 1 << (4 - level)

        def send(i, carry):
            code = 2 * n - 1 - i
            bits = [0] * level + [1] + [(code // (1 << (4 - j))) % 2 for j in range(level + 1, LEVELS)]
            for p in range(5):
                acc = summed(p, code, level, bits)
                snd[p, code, 0 : PART_ROWS[p]] = acc.astype(BF16)
                copy_of(p, code, level).start()
            return carry

        lax.fori_loop(0, n, send, 0)

    for p in range(5):
        rows = PART_ROWS[p]
        acc = summed(p, 0, LEVELS, [0] * LEVELS)
        acc = acc + residual_ref[starts[p] : starts[p] + rows, :].astype(F32)
        hidden[starts[p] : starts[p] + rows, :] = acc
    sums[0] = jnp.zeros((8, 256), F32)
    which = lax.broadcasted_iota(jnp.int32, (8, 256), 0)
    for p in range(5):
        rows = PART_ROWS[p]
        acc = hidden[starts[p] : starts[p] + rows, :]
        pick = jnp.where(which == p, 1.0, 0.0)
        squares = lax.dot_general(
            pick, acc * acc, (((1,), (1,)), ((), ())), preferred_element_type=F32,
            precision=lax.Precision.HIGHEST,
        )
        sums[0, :, 0:rows] = sums[0, :, 0:rows] + squares
    slot = 0
    sum_copies = []
    for stage, group in enumerate(SUM_MASKS):
        here = []
        for mask in group:
            copy = pltpu.make_async_remote_copy(
                sums.at[stage], got_sums.at[slot], sum_ss.at[slot], sum_rs.at[slot],
                device_id=tp_device(flipped(place, mask)), device_id_type=MESH,
            )
            copy.start()
            here.append((copy, slot))
            slot += 1
        total = sums[stage]
        for copy, index in here:
            copy.wait_recv()
            total = total + got_sums[index]
            sum_copies.append(copy)
        sums[stage + 1] = total
    scale = lax.rsqrt(sums[len(SUM_MASKS)] * (1.0 / D) + EPSILON)
    gain = gain_ref[...]
    for p in range(5):
        rows = PART_ROWS[p]
        pick = jnp.where(which == p, 1.0, 0.0)
        factor = lax.dot_general(
            scale[:, 0:rows], pick, (((0,), (0,)), ((), ())), preferred_element_type=F32,
            precision=lax.Precision.HIGHEST,
        )
        acc = hidden[starts[p] : starts[p] + rows, :]
        out_ref[starts[p] : starts[p] + rows, :] = (acc * factor * gain).astype(BF16)

    for copy in sum_copies:
        copy.wait_send()
    for level in range(LEVELS):
        n = 1 << (4 - level)

        def drain(i, carry):
            for p in range(5):
                copy_of(p, n + i, level).wait_send()
            return carry

        lax.fori_loop(0, n, drain, 0)


def mix(gated, weight, residual, gain):
    vmem = pl.BlockSpec(memory_space=pltpu.VMEM)
    hbm = pl.BlockSpec(memory_space=pltpu.HBM)
    return pl.pallas_call(
        mix_kernel,
        out_shape=jax.ShapeDtypeStruct((1024, 256), BF16),
        in_specs=[hbm] * 4,
        out_specs=vmem,
        scratch_shapes=[
            pltpu.VMEM((1024, 512), BF16),
            pltpu.VMEM((512, D), BF16),
            pltpu.VMEM((1024, 256), BF16),
            pltpu.VMEM((1, 256), F32),
            pltpu.VMEM((5, 32, 208, 256), BF16),
            pltpu.VMEM((5, 32, 208, 256), BF16),
            pltpu.VMEM((1024, 256), F32),
            pltpu.VMEM((3, 8, 256), F32),
            pltpu.VMEM((16, 8, 256), F32),
            pltpu.SemaphoreType.DMA((4,)),
            pltpu.SemaphoreType.DMA((5, 32)),
            pltpu.SemaphoreType.DMA((5, 32)),
            pltpu.SemaphoreType.DMA((16,)),
            pltpu.SemaphoreType.DMA((16,)),
        ],
        compiler_params=pltpu.CompilerParams(
            collective_id=1, has_side_effects=True, vmem_limit_bytes=60 << 20
        ),
        name="mix",
    )(gated, weight, residual, gain)


def on_device(
    mixer_input,
    gate_input,
    conv_state,
    scan_state,
    leave_slot,
    land_slot,
    move_count,
    conv_weight,
    conv_bias,
    delta_down,
    state_proj,
    delta_up,
    delta_bias,
    decay_log,
    skip_gain,
    out_weight,
    residual,
    norm_gain,
):
    low, io, conv_out, source, moved = project(
        leave_slot, land_slot, move_count, mixer_input, jnp.transpose(conv_state, (1, 0, 2)), scan_state,
        conv_weight, conv_bias.reshape(1, -1), delta_down, state_proj,
    )
    final_state, gated = recur(
        source, low.reshape(4, 2, 256, 256), io.reshape(256, 128), delta_up, delta_bias.reshape(1, -1),
        decay_log, skip_gain.reshape(1, -1), conv_out, gate_input, scan_state, moved.reshape(128, NS, 512),
    )
    normed = mix(
        gated.reshape(1024, 512), out_weight, residual.reshape(1024, 256), norm_gain.reshape(1, -1)
    )
    return (normed.reshape(STEPS, 256, 256), final_state)


def solution(mesh):
    in_specs = (
        P(None, "inst", "tp"),
        P(None, "inst", "tp"),
        P("inst", None, "tp"),
        P("inst", None, "tp"),
        P("inst", None, None),
        P(None, "inst", None),
        P(),
        P(None, "tp"),
        P("tp"),
        P("tp", None),
        P(None, "tp"),
        P(None, "tp"),
        P("tp"),
        P(None, "tp"),
        P("tp"),
        P("tp", None),
        P(None, "inst", "tp"),
        P(),
    )
    out_specs = (P(None, "inst", "tp"), P("inst", None, "tp"))
    return jax.shard_map(
        on_device, mesh=mesh, in_specs=in_specs, out_specs=out_specs, check_vma=False
    )
```

```python
import functools

import jax
import jax.numpy as jnp
from jax import lax
from jax.experimental import pallas as pl
from jax.experimental.pallas import tpu as pltpu
from jax.sharding import PartitionSpec as P

D = 8192
NS = 16
STEPS = 4
EPSILON = 1e-05
LOG2E = 1.4426950408889634
MESH = pl.DeviceIdType.MESH
F32 = jnp.float32
BF16 = jnp.bfloat16

PAIRS = (1, 8, 3, 24)
LEVELS = 4
GROUP = 16
CHUNKS = ((0, 128), (128, 128))
ORDER = ((0, 0), (0, 1), (1, 0), (0, 2), (0, 3), (0, 4), (1, 1), (1, 2), (1, 3), (1, 4))
HALF = 128


def flips():
    me = lax.axis_index("tp")
    return me, [(1 << bit) * (1 - 2 * ((me // (1 << bit)) % 2)) for bit in range(5)]


def flipped(place, mask):
    me, delta = place
    for bit in range(5):
        if (mask >> bit) & 1:
            me = me + delta[bit]
    return me


def pair_of(part, level):
    return PAIRS[(part + level) % LEVELS]


def tp_device(index):
    return (lax.axis_index("inst"), index)


def inst_partner(mask):
    inst = lax.axis_index("inst")
    core, low = inst % 2, inst // 2
    if mask & 1:
        core = 1 - core
    if mask & 2:
        low = 1 - low
    return low * 2 + core


def dot_nt(a, b):
    return lax.dot_general(a, b, (((1,), (1,)), ((), ())), preferred_element_type=F32)


def dot_tn(a, b):
    return lax.dot_general(a, b, (((0,), (0,)), ((), ())), preferred_element_type=F32)


def dot_nn(a, b):
    return jnp.dot(a, b, preferred_element_type=F32)


SIDES = ((0, 1, 2, 3), (0, 8, 16, 24))
PARTS = (3, 0, 1, 2, 4)
FIRST_STATES = 20


def sum_mask(part, code):
    first, second = SIDES[part % 2], SIDES[1 - part % 2]
    return first[code // 8] ^ second[(code // 2) % 4] ^ (4 * (code % 2))


def sum_moves(part, stage):
    first, second = SIDES[part % 2], SIDES[1 - part % 2]
    if stage == 0:
        return [(c - 1, 8 * c, 8, first[c]) for c in (2, 1, 3)]
    if stage == 1:
        return [(c + 2, 2 * c, 2, second[c]) for c in (2, 1, 3)]
    return [(6, 1, 1, 4)]


def project_kernel(
    leave_hbm, land_hbm, count_hbm, mix_hbm, conv_hbm, state_hbm, weight_hbm, bias_hbm, down_hbm, proj_hbm,
    low_out, io_out, u_out, map_out, moved_out,
    leave_smem, count_ref, leave_ref, land_ref, mix_ref, conv_ref, weight_ref, bias_ref, down_ref, proj_ref,
    state_v, pack_conv, got_conv, pack_state, got_state, low, io, snd, rcv, ag, snd_io, rcv_io, ag_io,
    in_sem, state_sem, conv_ss, conv_rs, mig_ss, mig_rs, out_sem, rs_ss, rs_rs, ag_ss, ag_rs,
):
    place = flips()
    inst = lax.axis_index("inst")
    loads = []
    for source, target in (
        (leave_hbm, leave_smem), (count_hbm, count_ref), (leave_hbm, leave_ref), (land_hbm, land_ref),
        (conv_hbm, conv_ref), (mix_hbm, mix_ref), (weight_hbm, weight_ref), (bias_hbm, bias_ref),
        (down_hbm, down_ref), (proj_hbm, proj_ref),
    ):
        copy = pltpu.make_async_copy(source, target, in_sem.at[len(loads)])
        copy.start()
        loads.append(copy)
    state_copy = pltpu.make_async_copy(state_hbm, state_v, state_sem)
    state_copy.start()
    barrier = pltpu.get_barrier_semaphore()
    masks = SIDES[0][1:] + SIDES[1][1:] + (4,)
    for mask in masks:
        pl.semaphore_signal(
            barrier, inc=1, device_id=tp_device(flipped(place, mask)), device_id_type=MESH
        )
    for mask in (1, 2, 3):
        pl.semaphore_signal(
            barrier, inc=1, device_id=(inst_partner(mask), place[0]), device_id_type=MESH
        )
    for copy in loads:
        copy.wait()

    lanes = lax.broadcasted_iota(jnp.int32, (1, 32), 1)
    leave_row = jnp.concatenate(
        [jnp.where(lanes < count_ref[inst, j], leave_ref[0, j : j + 1, :], -1) for j in range(4)], axis=1
    )
    land_row = jnp.concatenate(
        [jnp.where(lanes < count_ref[j, inst], land_ref[j], -1) for j in range(4)], axis=1
    )
    slots = lax.broadcasted_iota(jnp.int32, (256, 128), 0)
    leave_hot = jnp.where(slots == leave_row, 1.0, 0.0)
    land_hot = jnp.where(slots == land_row, 1.0, 0.0)
    keep = 1.0 - jnp.sum(leave_hot + land_hot, axis=1, keepdims=True)
    leave_hot = leave_hot.astype(BF16)
    land_hot = land_hot.astype(BF16)

    for k in range(3):
        pack_conv[:, k] = dot_tn(leave_hot, conv_ref[k]).astype(BF16).reshape(4, 32, 512)
    got_conv[inst] = jnp.zeros((3, 32, 512), BF16)

    pl.semaphore_wait(barrier, len(masks) + 3)
    conv_copies = []
    for mask in (2, 3, 1):
        other = inst_partner(mask)
        copy = pltpu.make_async_remote_copy(
            pack_conv.at[other], got_conv.at[inst], conv_ss.at[mask - 1], conv_rs.at[mask - 1],
            device_id=(other, place[0]), device_id_type=MESH,
        )
        copy.start()
        conv_copies.append(copy)

    taps = [weight_ref[k : k + 1, :] for k in range(4)]
    bias = bias_ref[...]

    def step(t, history):
        total = bias
        for k in range(4):
            source = history[t + k] if t + k < 3 else mix_ref[t + k - 3].astype(F32)
            total = total + taps[k] * source
        u = jax.nn.silu(total).astype(BF16)
        u_out[t] = u
        low[t, 0:16] = dot_nn(u, down_ref[:, 0:256]).reshape(16, 16, 256)
        low[t, 16:32] = dot_nn(u, down_ref[:, 256:512]).reshape(16, 16, 256)
        return u

    def rs_copy(p, move):
        index, start, size, mask = move
        s, r = (snd.at[p], rcv.at[p]) if p < 4 else (snd_io, rcv_io)
        return pltpu.make_async_remote_copy(
            s.at[start : start + size], r.at[start : start + size], rs_ss.at[p, index], rs_rs.at[p, index],
            device_id=tp_device(flipped(place, mask)), device_id_type=MESH,
        )

    def ag_copy(p, move):
        index, start, size, mask = move
        a = ag.at[p] if p < 4 else ag_io
        return pltpu.make_async_remote_copy(
            a.at[0:size], a.at[start : start + size], ag_ss.at[p, index], ag_rs.at[p, index],
            device_id=tp_device(flipped(place, mask)), device_id_type=MESH,
        )

    def summed(p, code):
        owner = flipped(place, sum_mask(p, code))
        acc = low[p, owner] if p < 4 else io[owner]
        sources = []
        if code < 8:
            sources += [8 * c + code for c in (1, 2, 3)]
        if code < 2:
            sources += [2 * c + code for c in (1, 2, 3)]
        if code == 0:
            sources += [1]
        for index in sources:
            acc = acc + (rcv[p, index] if p < 4 else rcv_io[index]).astype(F32)
        return acc

    def rs_stage(p, stage):
        if stage:
            for move in sum_moves(p, stage - 1):
                rs_copy(p, move).wait_recv()
        for move in sum_moves(p, stage):
            for code in range(move[1], move[1] + move[2]):
                acc = summed(p, code)
                if p < 4:
                    snd[p, code] = acc.astype(BF16)
                else:
                    snd_io[code] = acc
            rs_copy(p, move).start()

    us = [None] * 4
    us[3] = step(3, None)
    rs_stage(3, 0)

    state_copy.wait()
    state_copies = []
    for mask in (2, 3, 1):
        other = inst_partner(mask)

        def pack(i, carry):
            pack_state[other, i] = state_v[leave_smem[0, other, i]].astype(BF16)
            return carry

        lax.fori_loop(0, 32, pack, 0, unroll=4)
        for batch, (lo, hi) in enumerate(((0, FIRST_STATES), (FIRST_STATES, 32))):
            copy = pltpu.make_async_remote_copy(
                pack_state.at[other, lo:hi], got_state.at[inst, lo:hi],
                mig_ss.at[mask - 1, batch], mig_rs.at[mask - 1, batch],
                device_id=(other, place[0]), device_id_type=MESH,
            )
            if batch == 0:
                copy.start()
            state_copies.append((batch, copy))

    for copy in conv_copies:
        copy.wait_recv()
    history = []
    for k in range(3):
        moved = dot_nn(land_hot, got_conv[:, k].reshape(128, 512))
        history.append(conv_ref[k].astype(F32) * keep + moved)
    for t in range(3):
        us[t] = step(t, history)
        rs_stage(t, 0)
    proj = proj_ref[...]
    total = jnp.zeros((256, 128), F32)
    for t in range(4):
        pieces = [jnp.zeros_like(proj) if j != t else proj for j in range(4)]
        total = total + dot_nt(us[t], jnp.concatenate(pieces, axis=0))
    io[...] = total.reshape(32, 8, 128)
    rs_stage(4, 0)

    number = (lax.broadcasted_iota(jnp.int32, (8, 128), 1) + 1).astype(F32).astype(BF16)
    landed = dot_nt(number, land_hot)
    left = dot_nt(jnp.ones((8, 128), BF16), leave_hot)
    map_out[...] = (landed - left - 1.0).astype(jnp.int32)

    for stage in (1, 2):
        for p in PARTS:
            rs_stage(p, stage)
    for p in PARTS:
        for move in sum_moves(p, 2):
            rs_copy(p, move).wait_recv()
        acc = summed(p, 0)
        if p < 4:
            ag[p, 0] = acc.astype(BF16)
        else:
            ag_io[0] = acc
        for move in sum_moves(p, 2):
            ag_copy(p, move).start()
    for stage in (1, 0):
        for p in PARTS:
            for move in sum_moves(p, stage + 1):
                ag_copy(p, move).wait_recv()
            for move in sum_moves(p, stage):
                ag_copy(p, move).start()
        if stage == 1:
            for batch, copy in state_copies:
                if batch == 1:
                    copy.start()
    for p in PARTS:
        for move in sum_moves(p, 0):
            ag_copy(p, move).wait_recv()
        for code in range(32):
            owner = flipped(place, sum_mask(p, code))
            if p < 4:
                low_out[p, owner] = ag[p, code]
            else:
                io_out[owner] = ag_io[code]

    for batch, copy in state_copies:
        copy.wait_recv()
    outs = []
    for mask in (1, 2, 3):
        other = inst_partner(mask)
        copy = pltpu.make_async_copy(got_state.at[other], moved_out.at[other], out_sem.at[mask - 1])
        copy.start()
        outs.append(copy)
    for copy in conv_copies:
        copy.wait_send()
    for batch, copy in state_copies:
        copy.wait_send()
    for p in PARTS:
        for stage in range(3):
            for move in sum_moves(p, stage):
                rs_copy(p, move).wait_send()
                ag_copy(p, move).wait_send()
    for copy in outs:
        copy.wait()


def project(leave, land, count, mix, conv, state, weight, bias, down, proj):
    vmem = pl.BlockSpec(memory_space=pltpu.VMEM)
    hbm = pl.BlockSpec(memory_space=pltpu.HBM)
    return pl.pallas_call(
        project_kernel,
        out_shape=(
            jax.ShapeDtypeStruct((4, 32, 16, 256), BF16),
            jax.ShapeDtypeStruct((32, 8, 128), F32),
            jax.ShapeDtypeStruct((4, 256, 512), BF16),
            jax.ShapeDtypeStruct((8, 256), jnp.int32),
            jax.ShapeDtypeStruct((4, 32, 16, 512), BF16),
        ),
        in_specs=[hbm] * 10,
        out_specs=(vmem, vmem, vmem, vmem, vmem),
        scratch_shapes=[
            pltpu.SMEM((1, 4, 32), jnp.int32),
            pltpu.SMEM((4, 4), jnp.int32),
            pltpu.VMEM((1, 4, 32), jnp.int32),
            pltpu.VMEM((4, 1, 32), jnp.int32),
            pltpu.VMEM((4, 256, 512), BF16),
            pltpu.VMEM((3, 256, 512), BF16),
            pltpu.VMEM((4, 512), F32),
            pltpu.VMEM((1, 512), F32),
            pltpu.VMEM((512, 512), BF16),
            pltpu.VMEM((32, 512), BF16),
            pltpu.VMEM((256, 16, 512), F32),
            pltpu.VMEM((4, 3, 32, 512), BF16),
            pltpu.VMEM((4, 3, 32, 512), BF16),
            pltpu.VMEM((4, 32, 16, 512), BF16),
            pltpu.VMEM((4, 32, 16, 512), BF16),
            pltpu.VMEM((4, 32, 16, 256), F32),
            pltpu.VMEM((32, 8, 128), F32),
            pltpu.VMEM((4, 32, 16, 256), BF16),
            pltpu.VMEM((4, 32, 16, 256), BF16),
            pltpu.VMEM((4, 32, 16, 256), BF16),
            pltpu.VMEM((32, 8, 128), F32),
            pltpu.VMEM((32, 8, 128), F32),
            pltpu.VMEM((32, 8, 128), F32),
            pltpu.SemaphoreType.DMA((10,)),
            pltpu.SemaphoreType.DMA,
            pltpu.SemaphoreType.DMA((3,)),
            pltpu.SemaphoreType.DMA((3,)),
            pltpu.SemaphoreType.DMA((3, 2)),
            pltpu.SemaphoreType.DMA((3, 2)),
            pltpu.SemaphoreType.DMA((3,)),
            pltpu.SemaphoreType.DMA((5, 7)),
            pltpu.SemaphoreType.DMA((5, 7)),
            pltpu.SemaphoreType.DMA((5, 7)),
            pltpu.SemaphoreType.DMA((5, 7)),
        ],
        compiler_params=pltpu.CompilerParams(
            collective_id=0, has_side_effects=True, vmem_limit_bytes=60 << 20
        ),
        cost_estimate=pl.CostEstimate(flops=60_000_000_000, bytes_accessed=40_000_000, transcendentals=0),
        name="project",
    )(leave, land, count, mix, conv, state, weight, bias, down, proj)


def recur_kernel(half, *refs):
    map_ref, low_ref, io_ref, up_ref, dbias_ref, decay_ref, skip_ref, u_ref, gate_ref, state_ref, moved_ref = refs[:11]
    final_ref, gated_ref, delta, cbd, held, decay = refs[-6:]
    group = pl.program_id(0)

    @pl.when(group == 0)
    def _():
        decay[...] = jnp.exp(decay_ref[...]) * (-LOG2E)
        io = io_ref[...].astype(BF16)
        row = lax.broadcasted_iota(jnp.int32, (128, 256), 0)
        lane = lax.broadcasted_iota(jnp.int32, (128, 256), 1)
        slot = lax.broadcasted_iota(jnp.int32, (HALF, 256), 0)
        across = lax.broadcasted_iota(jnp.int32, (HALF, 256), 1)
        same = (slot % GROUP) == (across // NS)
        for t in range(STEPS):
            spread = jnp.where(row == (lane % NS) + (2 * NS * t + NS), 1.0, 0.0).astype(BF16)
            cbd[t] = jnp.where(same, dot_nn(io, spread), 0.0).astype(BF16)
            rate = dot_nn(low_ref[t, 0], up_ref[0:256, :]) + dot_nn(low_ref[t, 1], up_ref[256:512, :])
            delta[t] = jax.nn.softplus(rate + dbias_ref[...])

    base = pl.multiple_of(group * GROUP, GROUP)
    terms = jnp.transpose(io_ref[pl.ds(base, GROUP), :])
    rates = [delta[t, pl.ds(base, GROUP), :] for t in range(STEPS)]
    signals = [u_ref[t].astype(F32) for t in range(STEPS)]
    driven = [rates[t] * signals[t] for t in range(STEPS)]
    for s in range(GROUP):
        source = map_ref[0, half * HALF + base + s]
        moved = moved_ref[jnp.maximum(source, 0)].astype(F32)
        carried = jnp.where(source >= 0, moved, jnp.where(source == -1, state_ref[s], 0.0))
        for t in range(STEPS):
            decayed = carried * jnp.exp2(rates[t][s : s + 1, :] * decay[...])
            carried = decayed + terms[2 * NS * t : 2 * NS * t + NS, s : s + 1] * driven[t][s : s + 1, :]
            held[t, NS * s : NS * s + NS, :] = carried.astype(BF16)
        final_ref[s] = carried
    for t in range(STEPS):
        readout = dot_nn(cbd[t, pl.ds(base, GROUP), :], held[t]) + skip_ref[...] * signals[t]
        gated_ref[t] = (readout * jax.nn.silu(gate_ref[t].astype(F32))).astype(BF16)


def recur(half, source, low, io, up, dbias, decay, skip, u, gate, state, moved, final=None):
    smem = pl.BlockSpec(memory_space=pltpu.SMEM)
    vmem = pl.BlockSpec(memory_space=pltpu.VMEM)
    groups = HALF // GROUP
    steps = pl.BlockSpec((STEPS, GROUP, 512), lambda g: (0, half * groups + g, 0))
    slots = pl.BlockSpec((GROUP, NS, 512), lambda g: (half * groups + g, 0, 0))
    rows = pl.BlockSpec((STEPS, 2, HALF, 256), lambda g: (0, 0, half, 0))
    terms = pl.BlockSpec((HALF, 128), lambda g: (half, 0))
    extra = [] if final is None else [final]
    return pl.pallas_call(
        functools.partial(recur_kernel, half),
        grid=(groups,),
        out_shape=(
            jax.ShapeDtypeStruct((256, NS, 512), F32),
            jax.ShapeDtypeStruct((STEPS, HALF, 512), BF16),
        ),
        in_specs=[smem, rows, terms, vmem, vmem, vmem, vmem, steps, steps, slots, vmem]
        + [pl.BlockSpec(memory_space=pltpu.HBM)] * len(extra),
        out_specs=(slots, pl.BlockSpec((STEPS, GROUP, 512), lambda g: (0, g, 0))),
        scratch_shapes=[
            pltpu.VMEM((STEPS, HALF, 512), F32),
            pltpu.VMEM((STEPS, HALF, 256), BF16),
            pltpu.VMEM((STEPS, NS * GROUP, 512), BF16),
            pltpu.VMEM((NS, 512), F32),
        ],
        input_output_aliases={11: 0} if extra else {},
        compiler_params=pltpu.CompilerParams(vmem_limit_bytes=60 << 20),
        cost_estimate=pl.CostEstimate(flops=15_000_000_000, bytes_accessed=20_000_000, transcendentals=0),
        name="recur",
    )(source, low, io, up, dbias, decay, skip, u, gate, state, moved, *extra)


SUM_MASKS = (tuple(a + b for b in SIDES[1] for a in SIDES[0] if a + b), (4,))


def mix_kernel(
    first_hbm, second_hbm, other_hbm, weight_hbm, got_a, got_b, swap_a, swap_b, residual_hbm, gain_hbm,
    out_ref,
    gated, weight, residual_ref, gain_ref, own, snd, rcv, hidden, sums, got_sums,
    in_sem, gate_sem, pair_ss, pair_rs, ss, rs, sum_ss, sum_rs,
):
    place = flips()
    me, delta = place
    core = lax.axis_index("inst") % 2
    half = (me // 4) % 2
    gated_copy = pltpu.make_async_copy(second_hbm, gated.at[:, HALF:, 0:512], gate_sem)
    gated_copy.start()
    loads = []

    def load(source, target):
        copy = pltpu.make_async_copy(source, target, in_sem.at[len(loads)])
        copy.start()
        loads.append(copy)

    load(first_hbm, gated.at[:, 0:HALF, 0:512])
    load(other_hbm, gated.at[:, 0:HALF, 512:1024])
    for z in range(4):
        columns = pl.ds(pl.multiple_of(z * 2048 + half * 1024, 1024), 1024)
        load(weight_hbm.at[:, columns], weight.at[z, 0:512])
    load(got_a, weight.at[2 * core, 512:1024])
    load(got_b, weight.at[2 * core + 1, 512:1024])
    load(swap_a, weight.at[2 - 2 * core, 512:1024])
    load(swap_b, weight.at[3 - 2 * core, 512:1024])
    load(residual_hbm, residual_ref)
    load(gain_hbm.at[:, pl.ds(pl.multiple_of(me * 256, 256), 256)], gain_ref)
    barrier = pltpu.get_barrier_semaphore()
    masks = [mask for group in SUM_MASKS for mask in group]
    for mask in masks:
        pl.semaphore_signal(
            barrier, inc=1, device_id=tp_device(flipped(place, mask)), device_id_type=MESH
        )
    gated_copy.wait()
    pl.semaphore_wait(barrier, len(masks))
    pair_copy = pltpu.make_async_remote_copy(
        gated.at[:, HALF:, 0:512], gated.at[:, HALF:, 512:1024], pair_ss, pair_rs,
        device_id=tp_device(flipped(place, 4)), device_id_type=MESH,
    )
    pair_copy.start()
    for copy in loads:
        copy.wait()

    def copy_of(chunk, p, code, level):
        start, size = CHUNKS[chunk]
        return pltpu.make_async_remote_copy(
            snd.at[p, code, start : start + size], rcv.at[p, code, start : start + size],
            ss.at[chunk, p, code], rs.at[chunk, p, code],
            device_id=tp_device(flipped(place, pair_of(p, level))), device_id_type=MESH,
        )

    def products(chunk):
        start, size = CHUNKS[chunk]

        def product(i, carry):
            bits = [((15 - i) // (1 << (3 - j))) % 2 for j in range(LEVELS)]
            flip = [0] * 5
            for j in range(LEVELS):
                for bit in range(5):
                    if (PAIRS[j] >> bit) & 1:
                        flip[bit] = flip[bit] + bits[j]
            owner = me
            for bit in range(5):
                owner = owner + (flip[bit] % 2) * delta[bit]
            columns = pl.ds(pl.multiple_of((owner % 4) * 256, 256), 256)
            rows = gated[:, start : start + size, :].reshape(STEPS * size, 1024)
            acc = dot_nn(rows, weight[owner // 8, :, columns]).reshape(STEPS, size, 256)
            for p in range(4):
                code = sum(bits[(p + j) % 4] * (1 << (3 - j)) for j in range(LEVELS))

                @pl.when(bits[p] == 1)
                def _():
                    snd[p, code, start : start + size] = acc[p].astype(BF16)
                    copy_of(chunk, p, code, 0).start()

                @pl.when(bits[p] == 0)
                def _():
                    own[p, code, start : start + size] = acc[p]

            return carry

        lax.fori_loop(0, 16, product, 0)

    def summed(chunk, p, code, level):
        start, size = CHUNKS[chunk]
        acc = own[p, code, start : start + size]
        for j in range(level):
            copy_of(chunk, p, (1 << (3 - j)) + code, j).wait_recv()
            acc = acc + rcv[p, (1 << (3 - j)) + code, start : start + size].astype(F32)
        return acc

    for chunk, level in ORDER:
        start, size = CHUNKS[chunk]
        if level == 0:
            if chunk == 1:
                pair_copy.wait_recv()
            products(chunk)
        elif level < LEVELS:
            n = 1 << (3 - level)

            def send(i, carry):
                code = 2 * n - 1 - i
                for p in range(4):
                    acc = summed(chunk, p, code, level)
                    snd[p, code, start : start + size] = acc.astype(BF16)
                    copy_of(chunk, p, code, level).start()
                return carry

            lax.fori_loop(0, n, send, 0)
        else:
            for p in range(4):
                acc = summed(chunk, p, 0, LEVELS)
                hidden[p, start : start + size] = acc + residual_ref[p, start : start + size].astype(F32)

    which = lax.broadcasted_iota(jnp.int32, (8, 256), 0)
    squares = jnp.zeros((8, 256), F32)
    for p in range(4):
        acc = hidden[p]
        pick = jnp.where(which == p, 1.0, 0.0)
        squares = squares + lax.dot_general(
            pick, acc * acc, (((1,), (1,)), ((), ())), preferred_element_type=F32,
            precision=lax.Precision.HIGHEST,
        )
    sums[0] = squares
    slot = 0
    sum_copies = []
    for stage, group in enumerate(SUM_MASKS):
        here = []
        for mask in group:
            copy = pltpu.make_async_remote_copy(
                sums.at[stage], got_sums.at[slot], sum_ss.at[slot], sum_rs.at[slot],
                device_id=tp_device(flipped(place, mask)), device_id_type=MESH,
            )
            copy.start()
            here.append((copy, slot))
            slot += 1
        total = sums[stage]
        for copy, index in here:
            copy.wait_recv()
            total = total + got_sums[index]
            sum_copies.append(copy)
        sums[stage + 1] = total
    scale = lax.rsqrt(sums[len(SUM_MASKS)] * (1.0 / D) + EPSILON)
    gain = gain_ref[...]
    for p in range(4):
        pick = jnp.where(which == p, 1.0, 0.0)
        factor = lax.dot_general(
            scale, pick, (((0,), (0,)), ((), ())), preferred_element_type=F32,
            precision=lax.Precision.HIGHEST,
        )
        out_ref[p] = (hidden[p] * factor * gain).astype(BF16)

    for copy in sum_copies + [pair_copy]:
        copy.wait_send()
    for chunk in range(len(CHUNKS)):
        for level in range(LEVELS):
            n = 1 << (3 - level)

            def drain(i, carry):
                for p in range(4):
                    copy_of(chunk, p, n + i, level).wait_send()
                return carry

            lax.fori_loop(0, n, drain, 0)


def mix(first, second, other, weight, received, residual, gain):
    vmem = pl.BlockSpec(memory_space=pltpu.VMEM)
    hbm = pl.BlockSpec(memory_space=pltpu.HBM)
    return pl.pallas_call(
        mix_kernel,
        out_shape=jax.ShapeDtypeStruct((STEPS, 256, 256), BF16),
        in_specs=[hbm] * 10,
        out_specs=vmem,
        scratch_shapes=[
            pltpu.VMEM((STEPS, 256, 1024), BF16),
            pltpu.VMEM((4, 1024, 1024), BF16),
            pltpu.VMEM((STEPS, 256, 256), BF16),
            pltpu.VMEM((1, 256), F32),
            pltpu.VMEM((4, 8, 256, 256), F32),
            pltpu.VMEM((4, 16, 256, 256), BF16),
            pltpu.VMEM((4, 16, 256, 256), BF16),
            pltpu.VMEM((STEPS, 256, 256), F32),
            pltpu.VMEM((3, 8, 256), F32),
            pltpu.VMEM((16, 8, 256), F32),
            pltpu.SemaphoreType.DMA((12,)),
            pltpu.SemaphoreType.DMA,
            pltpu.SemaphoreType.DMA,
            pltpu.SemaphoreType.DMA,
            pltpu.SemaphoreType.DMA((2, 4, 16)),
            pltpu.SemaphoreType.DMA((2, 4, 16)),
            pltpu.SemaphoreType.DMA((16,)),
            pltpu.SemaphoreType.DMA((16,)),
        ],
        compiler_params=pltpu.CompilerParams(
            collective_id=1, has_side_effects=True, vmem_limit_bytes=60 << 20
        ),
        name="mix",
    )(first, second, other, weight, *received, residual, gain)


def permuted(value, inst_mask, tp_mask):
    places = [(i, t) for i in range(4) for t in range(32)]
    pairs = [(i * 32 + t, (i ^ inst_mask) * 32 + (t ^ tp_mask)) for i, t in places]
    return lax.ppermute(value, ("inst", "tp"), pairs)


def on_device(
    mixer_input,
    gate_input,
    conv_state,
    scan_state,
    leave_slot,
    land_slot,
    move_count,
    conv_weight,
    conv_bias,
    delta_down,
    state_proj,
    delta_up,
    delta_bias,
    decay_log,
    skip_gain,
    out_weight,
    residual,
    norm_gain,
):
    core = lax.axis_index("inst") % 2
    far = 1 - (lax.axis_index("tp") // 4) % 2
    received = []
    for piece in range(2):
        column = (2 * core + piece) * 2048 + far * 1024
        received.append(permuted(lax.dynamic_slice(out_weight, (0, column), (512, 1024)), 2, 4))
    low, io, conv_out, source, moved = project(
        leave_slot, land_slot, move_count, mixer_input, jnp.transpose(conv_state, (1, 0, 2)), scan_state,
        conv_weight, conv_bias.reshape(1, -1), delta_down, state_proj,
    )
    low, received[0] = lax.optimization_barrier((low, received[0]))
    operands = (
        source, low.reshape(4, 2, 256, 256), io.reshape(256, 128), delta_up, delta_bias.reshape(1, -1),
        decay_log, skip_gain.reshape(1, -1), conv_out, gate_input, scan_state, moved.reshape(128, NS, 512),
    )
    final_state, first = recur(0, *operands)
    first, received[1] = lax.optimization_barrier((first, received[1]))
    received = received + [permuted(piece, 1, 0) for piece in received]
    other = permuted(first, 0, 4)
    final_state, second = recur(1, *operands, final_state)
    normed = mix(first, second, other, out_weight, received, residual, norm_gain.reshape(1, -1))
    return (normed, final_state)


def solution(mesh):
    in_specs = (
        P(None, "inst", "tp"),
        P(None, "inst", "tp"),
        P("inst", None, "tp"),
        P("inst", None, "tp"),
        P("inst", None, None),
        P(None, "inst", None),
        P(),
        P(None, "tp"),
        P("tp"),
        P("tp", None),
        P(None, "tp"),
        P(None, "tp"),
        P("tp"),
        P(None, "tp"),
        P("tp"),
        P("tp", None),
        P(None, "inst", "tp"),
        P(),
    )
    out_specs = (P(None, "inst", "tp"), P("inst", None, "tp"))
    return jax.shard_map(
        on_device, mesh=mesh, in_specs=in_specs, out_specs=out_specs, check_vma=False
    )
```

```python
import functools

import jax
import jax.numpy as jnp
from jax import lax
from jax.experimental import pallas as pl
from jax.experimental.pallas import tpu as pltpu
from jax.sharding import PartitionSpec as P

D = 8192
NS = 16
STEPS = 4
EPSILON = 1e-05
LOG2E = 1.4426950408889634
MESH = pl.DeviceIdType.MESH
F32 = jnp.float32
BF16 = jnp.bfloat16

PAIRS = (1, 8, 3, 24)
LEVELS = 4
GROUP = 16
BLOCK = 64
CHUNKS = ((0, 128), (128, 128))
ORDER = ((0, 0), (0, 1), (1, 0), (1, 1), (0, 2), (1, 2), (0, 3), (1, 3), (0, 4), (1, 4))
HALF = 128


def flips():
    me = lax.axis_index("tp")
    return me, [(1 << bit) * (1 - 2 * ((me // (1 << bit)) % 2)) for bit in range(5)]


def flipped(place, mask):
    me, delta = place
    for bit in range(5):
        if (mask >> bit) & 1:
            me = me + delta[bit]
    return me


def pair_of(part, level):
    return PAIRS[(part + level) % LEVELS]


def tp_device(index):
    return (lax.axis_index("inst"), index)


def inst_partner(mask):
    inst = lax.axis_index("inst")
    core, low = inst % 2, inst // 2
    if mask & 1:
        core = 1 - core
    if mask & 2:
        low = 1 - low
    return low * 2 + core


def dot_nt(a, b):
    return lax.dot_general(a, b, (((1,), (1,)), ((), ())), preferred_element_type=F32)


def dot_tn(a, b):
    return lax.dot_general(a, b, (((0,), (0,)), ((), ())), preferred_element_type=F32)


def dot_nn(a, b):
    return jnp.dot(a, b, preferred_element_type=F32)


SIDES = ((0, 1, 2, 3), (0, 8, 16, 24))
PARTS = (3, 0, 1, 2, 4)
FIRST_STATES = 20


def sum_mask(part, code):
    first, second = SIDES[part % 2], SIDES[1 - part % 2]
    return first[code // 8] ^ second[(code // 2) % 4] ^ (4 * (code % 2))


def sum_moves(part, stage):
    first, second = SIDES[part % 2], SIDES[1 - part % 2]
    if stage == 0:
        return [(c - 1, 8 * c, 8, first[c]) for c in (2, 1, 3)]
    if stage == 1:
        return [(c + 2, 2 * c, 2, second[c]) for c in (2, 1, 3)]
    return [(6, 1, 1, 4)]


def project_kernel(
    leave_hbm, land_hbm, count_hbm, mix_hbm, conv_hbm, state_hbm, weight_hbm, bias_hbm, down_hbm, proj_hbm,
    low_out, io_out, u_out, map_out, moved_out,
    leave_smem, count_ref, leave_ref, land_ref, mix_ref, conv_ref, weight_ref, bias_ref, down_ref, proj_ref,
    state_v, pack_conv, got_conv, pack_state, got_state, low, io, snd, rcv, ag, snd_io, rcv_io, ag_io,
    in_sem, state_sem, conv_ss, conv_rs, mig_ss, mig_rs, out_sem, rs_ss, rs_rs, ag_ss, ag_rs,
):
    place = flips()
    inst = lax.axis_index("inst")
    loads = []
    for source, target in (
        (leave_hbm, leave_smem), (count_hbm, count_ref), (leave_hbm, leave_ref), (land_hbm, land_ref),
        (conv_hbm, conv_ref), (mix_hbm, mix_ref), (weight_hbm, weight_ref), (bias_hbm, bias_ref),
        (down_hbm, down_ref), (proj_hbm, proj_ref),
    ):
        copy = pltpu.make_async_copy(source, target, in_sem.at[len(loads)])
        copy.start()
        loads.append(copy)
    state_copy = pltpu.make_async_copy(state_hbm, state_v, state_sem)
    state_copy.start()
    barrier = pltpu.get_barrier_semaphore()
    masks = SIDES[0][1:] + SIDES[1][1:] + (4,)
    for mask in masks:
        pl.semaphore_signal(
            barrier, inc=1, device_id=tp_device(flipped(place, mask)), device_id_type=MESH
        )
    for mask in (1, 2, 3):
        pl.semaphore_signal(
            barrier, inc=1, device_id=(inst_partner(mask), place[0]), device_id_type=MESH
        )
    for copy in loads:
        copy.wait()

    lanes = lax.broadcasted_iota(jnp.int32, (1, 32), 1)
    leave_row = jnp.concatenate(
        [jnp.where(lanes < count_ref[inst, j], leave_ref[0, j : j + 1, :], -1) for j in range(4)], axis=1
    )
    land_row = jnp.concatenate(
        [jnp.where(lanes < count_ref[j, inst], land_ref[j], -1) for j in range(4)], axis=1
    )
    slots = lax.broadcasted_iota(jnp.int32, (256, 128), 0)
    leave_hot = jnp.where(slots == leave_row, 1.0, 0.0)
    land_hot = jnp.where(slots == land_row, 1.0, 0.0)
    keep = 1.0 - jnp.sum(leave_hot + land_hot, axis=1, keepdims=True)
    leave_hot = leave_hot.astype(BF16)
    land_hot = land_hot.astype(BF16)

    for k in range(3):
        pack_conv[:, k] = dot_tn(leave_hot, conv_ref[k]).astype(BF16).reshape(4, 32, 512)
    got_conv[inst] = jnp.zeros((3, 32, 512), BF16)

    pl.semaphore_wait(barrier, len(masks) + 3)
    conv_copies = []
    for mask in (2, 3, 1):
        other = inst_partner(mask)
        copy = pltpu.make_async_remote_copy(
            pack_conv.at[other], got_conv.at[inst], conv_ss.at[mask - 1], conv_rs.at[mask - 1],
            device_id=(other, place[0]), device_id_type=MESH,
        )
        copy.start()
        conv_copies.append(copy)

    taps = [weight_ref[k : k + 1, :] for k in range(4)]
    bias = bias_ref[...]

    def step(t, history):
        total = bias
        for k in range(4):
            source = history[t + k] if t + k < 3 else mix_ref[t + k - 3].astype(F32)
            total = total + taps[k] * source
        u = jax.nn.silu(total).astype(BF16)
        u_out[t] = u
        low[t, 0:16] = dot_nn(u, down_ref[:, 0:256]).reshape(16, 16, 256)
        low[t, 16:32] = dot_nn(u, down_ref[:, 256:512]).reshape(16, 16, 256)
        return u

    def rs_copy(p, move):
        index, start, size, mask = move
        s, r = (snd.at[p], rcv.at[p]) if p < 4 else (snd_io, rcv_io)
        return pltpu.make_async_remote_copy(
            s.at[start : start + size], r.at[start : start + size], rs_ss.at[p, index], rs_rs.at[p, index],
            device_id=tp_device(flipped(place, mask)), device_id_type=MESH,
        )

    def ag_copy(p, move):
        index, start, size, mask = move
        a = ag.at[p] if p < 4 else ag_io
        return pltpu.make_async_remote_copy(
            a.at[0:size], a.at[start : start + size], ag_ss.at[p, index], ag_rs.at[p, index],
            device_id=tp_device(flipped(place, mask)), device_id_type=MESH,
        )

    def summed(p, code):
        owner = flipped(place, sum_mask(p, code))
        acc = low[p, owner] if p < 4 else io[owner]
        sources = []
        if code < 8:
            sources += [8 * c + code for c in (1, 2, 3)]
        if code < 2:
            sources += [2 * c + code for c in (1, 2, 3)]
        if code == 0:
            sources += [1]
        for index in sources:
            acc = acc + (rcv[p, index] if p < 4 else rcv_io[index]).astype(F32)
        return acc

    def rs_stage(p, stage):
        if stage:
            for move in sum_moves(p, stage - 1):
                rs_copy(p, move).wait_recv()
        for move in sum_moves(p, stage):
            for code in range(move[1], move[1] + move[2]):
                acc = summed(p, code)
                if p < 4:
                    snd[p, code] = acc.astype(BF16)
                else:
                    snd_io[code] = acc
            rs_copy(p, move).start()

    us = [None] * 4
    us[3] = step(3, None)
    rs_stage(3, 0)

    state_copy.wait()
    state_copies = []
    for mask in (2, 3, 1):
        other = inst_partner(mask)

        def pack(i, carry):
            pack_state[other, i] = state_v[leave_smem[0, other, i]].astype(BF16)
            return carry

        lax.fori_loop(0, 32, pack, 0, unroll=4)
        for batch, (lo, hi) in enumerate(((0, FIRST_STATES), (FIRST_STATES, 32))):
            copy = pltpu.make_async_remote_copy(
                pack_state.at[other, lo:hi], got_state.at[inst, lo:hi],
                mig_ss.at[mask - 1, batch], mig_rs.at[mask - 1, batch],
                device_id=(other, place[0]), device_id_type=MESH,
            )
            if batch == 0:
                copy.start()
            state_copies.append((batch, copy))

    for copy in conv_copies:
        copy.wait_recv()
    history = []
    for k in range(3):
        moved = dot_nn(land_hot, got_conv[:, k].reshape(128, 512))
        history.append(conv_ref[k].astype(F32) * keep + moved)
    for t in range(3):
        us[t] = step(t, history)
        rs_stage(t, 0)
    proj = proj_ref[...]
    total = jnp.zeros((256, 128), F32)
    for t in range(4):
        pieces = [jnp.zeros_like(proj) if j != t else proj for j in range(4)]
        total = total + dot_nt(us[t], jnp.concatenate(pieces, axis=0))
    io[...] = total.reshape(32, 8, 128)
    rs_stage(4, 0)

    number = (lax.broadcasted_iota(jnp.int32, (8, 128), 1) + 1).astype(F32).astype(BF16)
    landed = dot_nt(number, land_hot)
    left = dot_nt(jnp.ones((8, 128), BF16), leave_hot)
    map_out[...] = (landed - left - 1.0).astype(jnp.int32)

    for stage in (1, 2):
        for p in PARTS:
            rs_stage(p, stage)
    for p in PARTS:
        for move in sum_moves(p, 2):
            rs_copy(p, move).wait_recv()
        acc = summed(p, 0)
        if p < 4:
            ag[p, 0] = acc.astype(BF16)
        else:
            ag_io[0] = acc
        for move in sum_moves(p, 2):
            ag_copy(p, move).start()
    for stage in (1, 0):
        for p in PARTS:
            for move in sum_moves(p, stage + 1):
                ag_copy(p, move).wait_recv()
            for move in sum_moves(p, stage):
                ag_copy(p, move).start()
        if stage == 1:
            for batch, copy in state_copies:
                if batch == 1:
                    copy.start()
    for p in PARTS:
        for move in sum_moves(p, 0):
            ag_copy(p, move).wait_recv()
        for code in range(32):
            owner = flipped(place, sum_mask(p, code))
            if p < 4:
                low_out[p, owner] = ag[p, code]
            else:
                io_out[owner] = ag_io[code]

    for batch, copy in state_copies:
        copy.wait_recv()
    outs = []
    for mask in (1, 2, 3):
        other = inst_partner(mask)
        copy = pltpu.make_async_copy(got_state.at[other], moved_out.at[other], out_sem.at[mask - 1])
        copy.start()
        outs.append(copy)
    for copy in conv_copies:
        copy.wait_send()
    for batch, copy in state_copies:
        copy.wait_send()
    for p in PARTS:
        for stage in range(3):
            for move in sum_moves(p, stage):
                rs_copy(p, move).wait_send()
                ag_copy(p, move).wait_send()
    for copy in outs:
        copy.wait()


def project(leave, land, count, mix, conv, state, weight, bias, down, proj):
    vmem = pl.BlockSpec(memory_space=pltpu.VMEM)
    hbm = pl.BlockSpec(memory_space=pltpu.HBM)
    return pl.pallas_call(
        project_kernel,
        out_shape=(
            jax.ShapeDtypeStruct((4, 32, 16, 256), BF16),
            jax.ShapeDtypeStruct((32, 8, 128), F32),
            jax.ShapeDtypeStruct((4, 256, 512), BF16),
            jax.ShapeDtypeStruct((8, 256), jnp.int32),
            jax.ShapeDtypeStruct((4, 32, 16, 512), BF16),
        ),
        in_specs=[hbm] * 10,
        out_specs=(vmem, vmem, vmem, vmem, vmem),
        scratch_shapes=[
            pltpu.SMEM((1, 4, 32), jnp.int32),
            pltpu.SMEM((4, 4), jnp.int32),
            pltpu.VMEM((1, 4, 32), jnp.int32),
            pltpu.VMEM((4, 1, 32), jnp.int32),
            pltpu.VMEM((4, 256, 512), BF16),
            pltpu.VMEM((3, 256, 512), BF16),
            pltpu.VMEM((4, 512), F32),
            pltpu.VMEM((1, 512), F32),
            pltpu.VMEM((512, 512), BF16),
            pltpu.VMEM((32, 512), BF16),
            pltpu.VMEM((256, 16, 512), F32),
            pltpu.VMEM((4, 3, 32, 512), BF16),
            pltpu.VMEM((4, 3, 32, 512), BF16),
            pltpu.VMEM((4, 32, 16, 512), BF16),
            pltpu.VMEM((4, 32, 16, 512), BF16),
            pltpu.VMEM((4, 32, 16, 256), F32),
            pltpu.VMEM((32, 8, 128), F32),
            pltpu.VMEM((4, 32, 16, 256), BF16),
            pltpu.VMEM((4, 32, 16, 256), BF16),
            pltpu.VMEM((4, 32, 16, 256), BF16),
            pltpu.VMEM((32, 8, 128), F32),
            pltpu.VMEM((32, 8, 128), F32),
            pltpu.VMEM((32, 8, 128), F32),
            pltpu.SemaphoreType.DMA((10,)),
            pltpu.SemaphoreType.DMA,
            pltpu.SemaphoreType.DMA((3,)),
            pltpu.SemaphoreType.DMA((3,)),
            pltpu.SemaphoreType.DMA((3, 2)),
            pltpu.SemaphoreType.DMA((3, 2)),
            pltpu.SemaphoreType.DMA((3,)),
            pltpu.SemaphoreType.DMA((5, 7)),
            pltpu.SemaphoreType.DMA((5, 7)),
            pltpu.SemaphoreType.DMA((5, 7)),
            pltpu.SemaphoreType.DMA((5, 7)),
        ],
        compiler_params=pltpu.CompilerParams(
            collective_id=0, has_side_effects=True, vmem_limit_bytes=60 << 20
        ),
        cost_estimate=pl.CostEstimate(flops=60_000_000_000, bytes_accessed=40_000_000, transcendentals=0),
        name="project",
    )(leave, land, count, mix, conv, state, weight, bias, down, proj)


def recur_kernel(half, *refs):
    map_ref, low_ref, io_ref, up_ref, dbias_ref, decay_ref, skip_ref, u_ref, gate_ref, state_ref, moved_ref = refs[:11]
    final_ref, gated_ref, delta, cbd, held, decay = refs[-6:]
    group = pl.program_id(0)

    @pl.when(group == 0)
    def _():
        decay[...] = jnp.exp(decay_ref[...]) * (-LOG2E)
        io = io_ref[...].astype(BF16)
        row = lax.broadcasted_iota(jnp.int32, (128, 256), 0)
        lane = lax.broadcasted_iota(jnp.int32, (128, 256), 1)
        slot = lax.broadcasted_iota(jnp.int32, (HALF, 256), 0)
        across = lax.broadcasted_iota(jnp.int32, (HALF, 256), 1)
        same = (slot % GROUP) == (across // NS)
        for t in range(STEPS):
            spread = jnp.where(row == (lane % NS) + (2 * NS * t + NS), 1.0, 0.0).astype(BF16)
            cbd[t] = jnp.where(same, dot_nn(io, spread), 0.0).astype(BF16)
            rate = dot_nn(low_ref[t, 0], up_ref[0:256, :]) + dot_nn(low_ref[t, 1], up_ref[256:512, :])
            delta[t] = jax.nn.softplus(rate + dbias_ref[...])

    for part in range(BLOCK // GROUP):
        inner = part * GROUP
        base = pl.multiple_of(group * BLOCK + inner, GROUP)
        terms = jnp.transpose(io_ref[pl.ds(base, GROUP), :])
        rates = [delta[t, pl.ds(base, GROUP), :] for t in range(STEPS)]
        signals = [u_ref[t, inner : inner + GROUP, :].astype(F32) for t in range(STEPS)]
        driven = [rates[t] * signals[t] for t in range(STEPS)]
        for s in range(GROUP):
            source = map_ref[0, half * HALF + base + s]
            moved = moved_ref[jnp.maximum(source, 0)].astype(F32)
            carried = jnp.where(source >= 0, moved, jnp.where(source == -1, state_ref[inner + s], 0.0))
            for t in range(STEPS):
                decayed = carried * jnp.exp2(rates[t][s : s + 1, :] * decay[...])
                carried = decayed + terms[2 * NS * t : 2 * NS * t + NS, s : s + 1] * driven[t][s : s + 1, :]
                held[part, t, NS * s : NS * s + NS, :] = carried.astype(BF16)
            final_ref[inner + s] = carried
        for t in range(STEPS):
            readout = dot_nn(cbd[t, pl.ds(base, GROUP), :], held[part, t]) + skip_ref[...] * signals[t]
            gate = jax.nn.silu(gate_ref[t, inner : inner + GROUP, :].astype(F32))
            gated_ref[t, inner : inner + GROUP, :] = (readout * gate).astype(BF16)


def recur(half, source, low, io, up, dbias, decay, skip, u, gate, state, moved, final=None):
    smem = pl.BlockSpec(memory_space=pltpu.SMEM)
    vmem = pl.BlockSpec(memory_space=pltpu.VMEM)
    groups = HALF // BLOCK
    steps = pl.BlockSpec((STEPS, BLOCK, 512), lambda g: (0, half * groups + g, 0))
    slots = pl.BlockSpec((BLOCK, NS, 512), lambda g: (half * groups + g, 0, 0))
    rows = pl.BlockSpec((STEPS, 2, HALF, 256), lambda g: (0, 0, half, 0))
    terms = pl.BlockSpec((HALF, 128), lambda g: (half, 0))
    extra = [] if final is None else [final]
    return pl.pallas_call(
        functools.partial(recur_kernel, half),
        grid=(groups,),
        out_shape=(
            jax.ShapeDtypeStruct((256, NS, 512), F32),
            jax.ShapeDtypeStruct((STEPS, HALF, 512), BF16),
        ),
        in_specs=[smem, rows, terms, vmem, vmem, vmem, vmem, steps, steps, slots, vmem]
        + [pl.BlockSpec(memory_space=pltpu.HBM)] * len(extra),
        out_specs=(slots, pl.BlockSpec((STEPS, BLOCK, 512), lambda g: (0, g, 0))),
        scratch_shapes=[
            pltpu.VMEM((STEPS, HALF, 512), F32),
            pltpu.VMEM((STEPS, HALF, 256), BF16),
            pltpu.VMEM((BLOCK // GROUP, STEPS, NS * GROUP, 512), BF16),
            pltpu.VMEM((NS, 512), F32),
        ],
        input_output_aliases={11: 0} if extra else {},
        compiler_params=pltpu.CompilerParams(vmem_limit_bytes=60 << 20),
        cost_estimate=pl.CostEstimate(flops=15_000_000_000, bytes_accessed=20_000_000, transcendentals=0),
        name="recur",
    )(source, low, io, up, dbias, decay, skip, u, gate, state, moved, *extra)


SUM_MASKS = (tuple(a + b for b in SIDES[1] for a in SIDES[0] if a + b), (4,))


def mix_kernel(
    first_hbm, second_hbm, other_hbm, weight_hbm, got_a, got_b, swap_a, swap_b, residual_hbm, gain_hbm,
    out_ref,
    gated, weight, residual_ref, gain_ref, own, snd, rcv, hidden, sums, got_sums,
    in_sem, weight_sem, gate_sem, pair_ss, pair_rs, ss, rs, sum_ss, sum_rs,
):
    place = flips()
    me, delta = place
    core = lax.axis_index("inst") % 2
    half = (me // 4) % 2
    gated_copy = pltpu.make_async_copy(second_hbm, gated.at[:, HALF:, 0:512], gate_sem)
    gated_copy.start()
    loads = []

    def load(source, target):
        copy = pltpu.make_async_copy(source, target, in_sem.at[len(loads)])
        copy.start()
        loads.append(copy)

    load(first_hbm, gated.at[:, 0:HALF, 0:512])
    load(other_hbm, gated.at[:, 0:HALF, 512:1024])

    z_here = me // 8
    z_order = [flipped(place, mask) // 8 for mask in (16, 8, 24)] + [z_here]
    for index, z in enumerate(z_order):
        columns = pl.ds(pl.multiple_of(z * 2048 + half * 1024, 1024), 1024)
        load(weight_hbm.at[:, columns], weight.at[z, 0:512])
        sem = weight_sem.at[index]
        low_part = (z % 2) == 0
        mine = (z // 2) == core

        @pl.when(mine & low_part)
        def _():
            pltpu.make_async_copy(got_a, weight.at[z, 512:1024], sem).start()

        @pl.when(mine & ~low_part)
        def _():
            pltpu.make_async_copy(got_b, weight.at[z, 512:1024], sem).start()

        @pl.when(~mine & low_part)
        def _():
            pltpu.make_async_copy(swap_a, weight.at[z, 512:1024], sem).start()

        @pl.when(~mine & ~low_part)
        def _():
            pltpu.make_async_copy(swap_b, weight.at[z, 512:1024], sem).start()

    load(residual_hbm, residual_ref)
    load(gain_hbm.at[:, pl.ds(pl.multiple_of(me * 256, 256), 256)], gain_ref)
    barrier = pltpu.get_barrier_semaphore()
    masks = [mask for group in SUM_MASKS for mask in group]
    for mask in masks:
        pl.semaphore_signal(
            barrier, inc=1, device_id=tp_device(flipped(place, mask)), device_id_type=MESH
        )
    gated_copy.wait()
    pl.semaphore_wait(barrier, len(masks))
    pair_copy = pltpu.make_async_remote_copy(
        gated.at[:, HALF:, 0:512], gated.at[:, HALF:, 512:1024], pair_ss, pair_rs,
        device_id=tp_device(flipped(place, 4)), device_id_type=MESH,
    )
    pair_copy.start()
    loads[0].wait()
    loads[1].wait()

    def copy_of(chunk, p, code, level):
        start, size = CHUNKS[chunk]
        return pltpu.make_async_remote_copy(
            snd.at[p, code, start : start + size], rcv.at[p, code, start : start + size],
            ss.at[chunk, p, code], rs.at[chunk, p, code],
            device_id=tp_device(flipped(place, pair_of(p, level))), device_id_type=MESH,
        )

    def products(chunk):
        start, size = CHUNKS[chunk]

        def product(i, carry):
            if chunk == 0:
                for index, z in enumerate(z_order):

                    @pl.when(i == index)
                    def _():
                        loads[2 + index].wait()
                        pltpu.make_async_copy(got_a, weight.at[z, 512:1024], weight_sem.at[index]).wait()

            bits = [((15 - i) // (1 << (3 - j))) % 2 for j in range(LEVELS)]
            flip = [0] * 5
            for j in range(LEVELS):
                for bit in range(5):
                    if (PAIRS[j] >> bit) & 1:
                        flip[bit] = flip[bit] + bits[j]
            owner = me
            for bit in range(5):
                owner = owner + (flip[bit] % 2) * delta[bit]
            columns = pl.ds(pl.multiple_of((owner % 4) * 256, 256), 256)
            rows = gated[:, start : start + size, :].reshape(STEPS * size, 1024)
            acc = dot_nn(rows, weight[owner // 8, :, columns]).reshape(STEPS, size, 256)
            for p in range(4):
                code = sum(bits[(p + j) % 4] * (1 << (3 - j)) for j in range(LEVELS))

                @pl.when(bits[p] == 1)
                def _():
                    snd[p, code, start : start + size] = acc[p].astype(BF16)
                    copy_of(chunk, p, code, 0).start()

                @pl.when(bits[p] == 0)
                def _():
                    own[p, code, start : start + size] = acc[p]

            return carry

        lax.fori_loop(0, 16, product, 0)

    def summed(chunk, p, code, level):
        start, size = CHUNKS[chunk]
        acc = own[p, code, start : start + size]
        for j in range(level):
            copy_of(chunk, p, (1 << (3 - j)) + code, j).wait_recv()
            acc = acc + rcv[p, (1 << (3 - j)) + code, start : start + size].astype(F32)
        return acc

    for chunk, level in ORDER:
        if (chunk, level) == (0, LEVELS):
            loads[6].wait()
            loads[7].wait()
        start, size = CHUNKS[chunk]
        if level == 0:
            if chunk == 1:
                pair_copy.wait_recv()
            products(chunk)
        elif level < LEVELS:
            n = 1 << (3 - level)

            def send(i, carry):
                code = 2 * n - 1 - i
                for p in range(4):
                    acc = summed(chunk, p, code, level)
                    snd[p, code, start : start + size] = acc.astype(BF16)
                    copy_of(chunk, p, code, level).start()
                return carry

            lax.fori_loop(0, n, send, 0)
        else:
            for p in range(4):
                acc = summed(chunk, p, 0, LEVELS)
                hidden[p, start : start + size] = acc + residual_ref[p, start : start + size].astype(F32)

    which = lax.broadcasted_iota(jnp.int32, (8, 256), 0)
    squares = jnp.zeros((8, 256), F32)
    for p in range(4):
        acc = hidden[p]
        pick = jnp.where(which == p, 1.0, 0.0).astype(BF16)
        squares = squares + dot_nt(pick, (acc * acc).astype(BF16))
    sums[0] = squares
    slot = 0
    sum_copies = []
    for stage, group in enumerate(SUM_MASKS):
        here = []
        for mask in group:
            copy = pltpu.make_async_remote_copy(
                sums.at[stage], got_sums.at[slot], sum_ss.at[slot], sum_rs.at[slot],
                device_id=tp_device(flipped(place, mask)), device_id_type=MESH,
            )
            copy.start()
            here.append((copy, slot))
            slot += 1
        total = sums[stage]
        for copy, index in here:
            copy.wait_recv()
            total = total + got_sums[index]
            sum_copies.append(copy)
        sums[stage + 1] = total
    scale = lax.rsqrt(sums[len(SUM_MASKS)] * (1.0 / D) + EPSILON)
    gain = gain_ref[...]
    coarse = scale.astype(BF16)
    fine = (scale - coarse.astype(F32)).astype(BF16)
    for p in range(4):
        pick = jnp.where(which == p, 1.0, 0.0).astype(BF16)
        factor = dot_tn(coarse, pick) + dot_tn(fine, pick)
        out_ref[p] = (hidden[p] * factor * gain).astype(BF16)

    for copy in sum_copies + [pair_copy]:
        copy.wait_send()
    for chunk in range(len(CHUNKS)):
        for level in range(LEVELS):
            n = 1 << (3 - level)

            def drain(i, carry):
                for p in range(4):
                    copy_of(chunk, p, n + i, level).wait_send()
                return carry

            lax.fori_loop(0, n, drain, 0)


def mix(first, second, other, weight, received, residual, gain):
    vmem = pl.BlockSpec(memory_space=pltpu.VMEM)
    hbm = pl.BlockSpec(memory_space=pltpu.HBM)
    return pl.pallas_call(
        mix_kernel,
        out_shape=jax.ShapeDtypeStruct((STEPS, 256, 256), BF16),
        in_specs=[hbm] * 10,
        out_specs=vmem,
        scratch_shapes=[
            pltpu.VMEM((STEPS, 256, 1024), BF16),
            pltpu.VMEM((4, 1024, 1024), BF16),
            pltpu.VMEM((STEPS, 256, 256), BF16),
            pltpu.VMEM((1, 256), F32),
            pltpu.VMEM((4, 8, 256, 256), F32),
            pltpu.VMEM((4, 16, 256, 256), BF16),
            pltpu.VMEM((4, 16, 256, 256), BF16),
            pltpu.VMEM((STEPS, 256, 256), F32),
            pltpu.VMEM((3, 8, 256), F32),
            pltpu.VMEM((16, 8, 256), F32),
            pltpu.SemaphoreType.DMA((8,)),
            pltpu.SemaphoreType.DMA((4,)),
            pltpu.SemaphoreType.DMA,
            pltpu.SemaphoreType.DMA,
            pltpu.SemaphoreType.DMA,
            pltpu.SemaphoreType.DMA((2, 4, 16)),
            pltpu.SemaphoreType.DMA((2, 4, 16)),
            pltpu.SemaphoreType.DMA((16,)),
            pltpu.SemaphoreType.DMA((16,)),
        ],
        compiler_params=pltpu.CompilerParams(
            collective_id=1, has_side_effects=True, vmem_limit_bytes=60 << 20
        ),
        name="mix",
    )(first, second, other, weight, *received, residual, gain)


def permuted(value, inst_mask, tp_mask):
    places = [(i, t) for i in range(4) for t in range(32)]
    pairs = [(i * 32 + t, (i ^ inst_mask) * 32 + (t ^ tp_mask)) for i, t in places]
    return lax.ppermute(value, ("inst", "tp"), pairs)


def on_device(
    mixer_input,
    gate_input,
    conv_state,
    scan_state,
    leave_slot,
    land_slot,
    move_count,
    conv_weight,
    conv_bias,
    delta_down,
    state_proj,
    delta_up,
    delta_bias,
    decay_log,
    skip_gain,
    out_weight,
    residual,
    norm_gain,
):
    core = lax.axis_index("inst") % 2
    far = 1 - (lax.axis_index("tp") // 4) % 2
    received = []
    for piece in range(2):
        column = (2 * core + piece) * 2048 + far * 1024
        received.append(permuted(lax.dynamic_slice(out_weight, (0, column), (512, 1024)), 2, 4))
    low, io, conv_out, source, moved = project(
        leave_slot, land_slot, move_count, mixer_input, jnp.transpose(conv_state, (1, 0, 2)), scan_state,
        conv_weight, conv_bias.reshape(1, -1), delta_down, state_proj,
    )
    low, received[0] = lax.optimization_barrier((low, received[0]))
    operands = (
        source, low.reshape(4, 2, 256, 256), io.reshape(256, 128), delta_up, delta_bias.reshape(1, -1),
        decay_log, skip_gain.reshape(1, -1), conv_out, gate_input, scan_state, moved.reshape(128, NS, 512),
    )
    final_state, first = recur(0, *operands)
    first, received[1] = lax.optimization_barrier((first, received[1]))
    received = received + [permuted(piece, 1, 0) for piece in received]
    other = permuted(first, 0, 4)
    final_state, second = recur(1, *operands, final_state)
    normed = mix(first, second, other, out_weight, received, residual, norm_gain.reshape(1, -1))
    return (normed, final_state)


def solution(mesh):
    in_specs = (
        P(None, "inst", "tp"),
        P(None, "inst", "tp"),
        P("inst", None, "tp"),
        P("inst", None, "tp"),
        P("inst", None, None),
        P(None, "inst", None),
        P(),
        P(None, "tp"),
        P("tp"),
        P("tp", None),
        P(None, "tp"),
        P(None, "tp"),
        P("tp"),
        P(None, "tp"),
        P("tp"),
        P("tp", None),
        P(None, "inst", "tp"),
        P(),
    )
    out_specs = (P(None, "inst", "tp"), P("inst", None, "tp"))
    return jax.shard_map(
        on_device, mesh=mesh, in_specs=in_specs, out_specs=out_specs, check_vma=False
    )
```

```python
import functools

import jax
import jax.numpy as jnp
from jax import lax
from jax.experimental import pallas as pl
from jax.experimental.pallas import tpu as pltpu
from jax.sharding import PartitionSpec as P

D = 8192
NS = 16
STEPS = 4
EPSILON = 1e-05
LOG2E = 1.4426950408889634
MESH = pl.DeviceIdType.MESH
F32 = jnp.float32
BF16 = jnp.bfloat16

PAIRS = (1, 8, 3, 24)
LEVELS = 4
GROUP = 16
BLOCK = 64
CHUNKS = ((0, 128), (128, 128))
ORDER = ((0, 0), (0, 1), (1, 0), (1, 1), (0, 2), (1, 2), (0, 3), (1, 3), (0, 4), (1, 4))
HALF = 128


def flips():
    me = lax.axis_index("tp")
    return me, [(1 << bit) * (1 - 2 * ((me // (1 << bit)) % 2)) for bit in range(5)]


def flipped(place, mask):
    me, delta = place
    for bit in range(5):
        if (mask >> bit) & 1:
            me = me + delta[bit]
    return me


def pair_of(part, level):
    return PAIRS[(part + level) % LEVELS]


def tp_device(index):
    return (lax.axis_index("inst"), index)


def inst_partner(mask):
    inst = lax.axis_index("inst")
    core, low = inst % 2, inst // 2
    if mask & 1:
        core = 1 - core
    if mask & 2:
        low = 1 - low
    return low * 2 + core


def dot_nt(a, b):
    return lax.dot_general(a, b, (((1,), (1,)), ((), ())), preferred_element_type=F32)


def dot_tn(a, b):
    return lax.dot_general(a, b, (((0,), (0,)), ((), ())), preferred_element_type=F32)


def dot_nn(a, b):
    return jnp.dot(a, b, preferred_element_type=F32)


SIDES = ((0, 1, 2, 3), (0, 8, 16, 24))
PARTS = (3, 0, 1, 2, 4)
FIRST_STATES = 20


def sum_mask(part, code):
    first, second = SIDES[part % 2], SIDES[1 - part % 2]
    return first[code // 4] ^ second[code % 4]


def sum_moves(part, stage):
    first, second = SIDES[part % 2], SIDES[1 - part % 2]
    if stage == 0:
        return [(c - 1, 4 * c, 4, first[c]) for c in (2, 1, 3)]
    if stage == 1:
        return [(c + 2, c, 1, second[c]) for c in (2, 1, 3)]
    return [(6, 0, 1, 4)]


def project_kernel(
    leave_hbm, land_hbm, count_hbm, mix_hbm, conv_hbm, state_hbm, weight_hbm, bias_hbm, down_hbm, proj_hbm,
    low_out, io_out, u_out, map_out, moved_out,
    leave_smem, count_ref, leave_ref, land_ref, mix_ref, conv_ref, weight_ref, bias_ref, down_ref, proj_ref,
    state_v, pack_conv, got_conv, pack_state, got_state, low, io, snd, rcv, ag, snd_io, rcv_io, ag_io,
    in_sem, state_sem, conv_ss, conv_rs, mig_ss, mig_rs, out_sem, rs_ss, rs_rs, ag_ss, ag_rs,
):
    place = flips()
    inst = lax.axis_index("inst")
    loads = []
    for source, target in (
        (leave_hbm, leave_smem), (count_hbm, count_ref), (leave_hbm, leave_ref), (land_hbm, land_ref),
        (conv_hbm, conv_ref), (mix_hbm, mix_ref), (weight_hbm, weight_ref), (bias_hbm, bias_ref),
        (down_hbm, down_ref), (proj_hbm, proj_ref),
    ):
        copy = pltpu.make_async_copy(source, target, in_sem.at[len(loads)])
        copy.start()
        loads.append(copy)
    state_copy = pltpu.make_async_copy(state_hbm, state_v, state_sem)
    state_copy.start()
    barrier = pltpu.get_barrier_semaphore()
    masks = SIDES[0][1:] + SIDES[1][1:] + (4,)
    for mask in masks:
        pl.semaphore_signal(
            barrier, inc=1, device_id=tp_device(flipped(place, mask)), device_id_type=MESH
        )
    for mask in (1, 2, 3):
        pl.semaphore_signal(
            barrier, inc=1, device_id=(inst_partner(mask), place[0]), device_id_type=MESH
        )
    for copy in loads:
        copy.wait()

    lanes = lax.broadcasted_iota(jnp.int32, (1, 32), 1)
    leave_row = jnp.concatenate(
        [jnp.where(lanes < count_ref[inst, j], leave_ref[0, j : j + 1, :], -1) for j in range(4)], axis=1
    )
    land_row = jnp.concatenate(
        [jnp.where(lanes < count_ref[j, inst], land_ref[j], -1) for j in range(4)], axis=1
    )
    slots = lax.broadcasted_iota(jnp.int32, (256, 128), 0)
    leave_hot = jnp.where(slots == leave_row, 1.0, 0.0)
    land_hot = jnp.where(slots == land_row, 1.0, 0.0)
    keep = 1.0 - jnp.sum(leave_hot + land_hot, axis=1, keepdims=True)
    leave_hot = leave_hot.astype(BF16)
    land_hot = land_hot.astype(BF16)

    for k in range(3):
        pack_conv[:, k] = dot_tn(leave_hot, conv_ref[k]).astype(BF16).reshape(4, 32, 512)
    got_conv[inst] = jnp.zeros((3, 32, 512), BF16)

    pl.semaphore_wait(barrier, len(masks) + 3)
    conv_copies = []
    for mask in (2, 3, 1):
        other = inst_partner(mask)
        copy = pltpu.make_async_remote_copy(
            pack_conv.at[other], got_conv.at[inst], conv_ss.at[mask - 1], conv_rs.at[mask - 1],
            device_id=(other, place[0]), device_id_type=MESH,
        )
        copy.start()
        conv_copies.append(copy)

    taps = [weight_ref[k : k + 1, :] for k in range(4)]
    bias = bias_ref[...]

    def step(t, history):
        total = bias
        for k in range(4):
            source = history[t + k] if t + k < 3 else mix_ref[t + k - 3].astype(F32)
            total = total + taps[k] * source
        u = jax.nn.silu(total).astype(BF16)
        u_out[t] = u
        low[t, 0:8] = dot_nn(u, down_ref[:, 0:256]).reshape(8, 32, 256)
        low[t, 8:16] = dot_nn(u, down_ref[:, 256:512]).reshape(8, 32, 256)
        return u

    def rs_copy(p, move):
        index, start, size, mask = move
        s, r = (snd.at[p], rcv.at[p]) if p < 4 else (snd_io, rcv_io)
        return pltpu.make_async_remote_copy(
            s.at[start : start + size], r.at[start : start + size], rs_ss.at[p, index], rs_rs.at[p, index],
            device_id=tp_device(flipped(place, mask)), device_id_type=MESH,
        )

    def ag_copy(p, move):
        index, start, size, mask = move
        a = ag.at[p] if p < 4 else ag_io
        return pltpu.make_async_remote_copy(
            a.at[0:size], a.at[start : start + size], ag_ss.at[p, index], ag_rs.at[p, index],
            device_id=tp_device(flipped(place, mask)), device_id_type=MESH,
        )

    def block(p, code):
        there = flipped(place, sum_mask(p, code))
        return (there // 8) * 4 + there % 4

    def summed(p, code):
        acc = low[p, block(p, code)] if p < 4 else io[block(p, code)]
        sources = []
        if code < 4:
            sources += [4 * c + code for c in (1, 2, 3)]
        if code == 0:
            sources += [1, 2, 3]
        for index in sources:
            acc = acc + (rcv[p, index] if p < 4 else rcv_io[index]).astype(F32)
        return acc

    def rs_stage(p, stage):
        if stage:
            for move in sum_moves(p, stage - 1):
                rs_copy(p, move).wait_recv()
        for move in sum_moves(p, stage):
            for code in range(move[1], move[1] + move[2]):
                value = summed(p, code).astype(BF16)
                if p < 4:
                    snd[p, code] = value
                else:
                    snd_io[code] = value
            rs_copy(p, move).start()

    us = [None] * 4
    us[3] = step(3, None)
    rs_stage(3, 0)

    state_copy.wait()
    state_copies = []
    for mask in (2, 3, 1):
        other = inst_partner(mask)

        def pack(i, carry):
            pack_state[other, i] = state_v[leave_smem[0, other, i]].astype(BF16)
            return carry

        lax.fori_loop(0, 32, pack, 0, unroll=4)
        for batch, (lo, hi) in enumerate(((0, FIRST_STATES), (FIRST_STATES, 32))):
            copy = pltpu.make_async_remote_copy(
                pack_state.at[other, lo:hi], got_state.at[inst, lo:hi],
                mig_ss.at[mask - 1, batch], mig_rs.at[mask - 1, batch],
                device_id=(other, place[0]), device_id_type=MESH,
            )
            if batch == 0:
                copy.start()
            state_copies.append((batch, copy))

    for copy in conv_copies:
        copy.wait_recv()
    history = []
    for k in range(3):
        moved = dot_nn(land_hot, got_conv[:, k].reshape(128, 512))
        history.append(conv_ref[k].astype(F32) * keep + moved)
    for t in range(3):
        us[t] = step(t, history)
        rs_stage(t, 0)
    proj = proj_ref[...]
    total = jnp.zeros((256, 128), F32)
    for t in range(4):
        pieces = [jnp.zeros_like(proj) if j != t else proj for j in range(4)]
        total = total + dot_nt(us[t], jnp.concatenate(pieces, axis=0))
    io[...] = total.reshape(16, 16, 128)
    rs_stage(4, 0)

    number = (lax.broadcasted_iota(jnp.int32, (8, 128), 1) + 1).astype(F32).astype(BF16)
    landed = dot_nt(number, land_hot)
    left = dot_nt(jnp.ones((8, 128), BF16), leave_hot)
    map_out[...] = (landed - left - 1.0).astype(jnp.int32)

    for stage in (1, 2):
        for p in PARTS:
            rs_stage(p, stage)
    for p in PARTS:
        for move in sum_moves(p, 2):
            rs_copy(p, move).wait_recv()
        if p < 4:
            ag[p, 0] = (snd[p, 0].astype(F32) + rcv[p, 0].astype(F32)).astype(BF16)
        else:
            ag_io[0] = (snd_io[0].astype(F32) + rcv_io[0].astype(F32)).astype(BF16)
        for move in sum_moves(p, 1):
            ag_copy(p, move).start()
    for batch, copy in state_copies:
        if batch == 1:
            copy.start()
    for p in PARTS:
        for move in sum_moves(p, 1):
            ag_copy(p, move).wait_recv()
        for move in sum_moves(p, 0):
            ag_copy(p, move).start()
    for p in PARTS:
        for move in sum_moves(p, 0):
            ag_copy(p, move).wait_recv()
        for code in range(16):
            if p < 4:
                low_out[p, block(p, code)] = ag[p, code]
            else:
                io_out[block(p, code)] = ag_io[code]

    for batch, copy in state_copies:
        copy.wait_recv()
    outs = []
    for mask in (1, 2, 3):
        other = inst_partner(mask)
        copy = pltpu.make_async_copy(got_state.at[other], moved_out.at[other], out_sem.at[mask - 1])
        copy.start()
        outs.append(copy)
    for copy in conv_copies:
        copy.wait_send()
    for batch, copy in state_copies:
        copy.wait_send()
    for p in PARTS:
        for stage in range(3):
            for move in sum_moves(p, stage):
                rs_copy(p, move).wait_send()
                if stage < 2:
                    ag_copy(p, move).wait_send()
    for copy in outs:
        copy.wait()


def project(leave, land, count, mix, conv, state, weight, bias, down, proj):
    vmem = pl.BlockSpec(memory_space=pltpu.VMEM)
    hbm = pl.BlockSpec(memory_space=pltpu.HBM)
    return pl.pallas_call(
        project_kernel,
        out_shape=(
            jax.ShapeDtypeStruct((4, 16, 32, 256), BF16),
            jax.ShapeDtypeStruct((16, 16, 128), BF16),
            jax.ShapeDtypeStruct((4, 256, 512), BF16),
            jax.ShapeDtypeStruct((8, 256), jnp.int32),
            jax.ShapeDtypeStruct((4, 32, 16, 512), BF16),
        ),
        in_specs=[hbm] * 10,
        out_specs=(vmem, vmem, vmem, vmem, vmem),
        scratch_shapes=[
            pltpu.SMEM((1, 4, 32), jnp.int32),
            pltpu.SMEM((4, 4), jnp.int32),
            pltpu.VMEM((1, 4, 32), jnp.int32),
            pltpu.VMEM((4, 1, 32), jnp.int32),
            pltpu.VMEM((4, 256, 512), BF16),
            pltpu.VMEM((3, 256, 512), BF16),
            pltpu.VMEM((4, 512), F32),
            pltpu.VMEM((1, 512), F32),
            pltpu.VMEM((512, 512), BF16),
            pltpu.VMEM((32, 512), BF16),
            pltpu.VMEM((256, 16, 512), F32),
            pltpu.VMEM((4, 3, 32, 512), BF16),
            pltpu.VMEM((4, 3, 32, 512), BF16),
            pltpu.VMEM((4, 32, 16, 512), BF16),
            pltpu.VMEM((4, 32, 16, 512), BF16),
            pltpu.VMEM((4, 16, 32, 256), F32),
            pltpu.VMEM((16, 16, 128), F32),
            pltpu.VMEM((4, 16, 32, 256), BF16),
            pltpu.VMEM((4, 16, 32, 256), BF16),
            pltpu.VMEM((4, 16, 32, 256), BF16),
            pltpu.VMEM((16, 16, 128), BF16),
            pltpu.VMEM((16, 16, 128), BF16),
            pltpu.VMEM((16, 16, 128), BF16),
            pltpu.SemaphoreType.DMA((10,)),
            pltpu.SemaphoreType.DMA,
            pltpu.SemaphoreType.DMA((3,)),
            pltpu.SemaphoreType.DMA((3,)),
            pltpu.SemaphoreType.DMA((3, 2)),
            pltpu.SemaphoreType.DMA((3, 2)),
            pltpu.SemaphoreType.DMA((3,)),
            pltpu.SemaphoreType.DMA((5, 7)),
            pltpu.SemaphoreType.DMA((5, 7)),
            pltpu.SemaphoreType.DMA((5, 7)),
            pltpu.SemaphoreType.DMA((5, 7)),
        ],
        compiler_params=pltpu.CompilerParams(
            collective_id=0, has_side_effects=True, vmem_limit_bytes=60 << 20
        ),
        cost_estimate=pl.CostEstimate(flops=60_000_000_000, bytes_accessed=40_000_000, transcendentals=0),
        name="project",
    )(leave, land, count, mix, conv, state, weight, bias, down, proj)


def recur_kernel(half, *refs):
    map_ref, low_ref, io_ref, up_ref, dbias_ref, decay_ref, skip_ref, u_ref, gate_ref, state_ref, moved_ref = refs[:11]
    final_ref, gated_ref, delta, cbd, held, decay = refs[-6:]
    group = pl.program_id(0)

    @pl.when(group == 0)
    def _():
        decay[...] = jnp.exp(decay_ref[...]) * (-LOG2E)
        io = io_ref[...]
        row = lax.broadcasted_iota(jnp.int32, (128, 256), 0)
        lane = lax.broadcasted_iota(jnp.int32, (128, 256), 1)
        slot = lax.broadcasted_iota(jnp.int32, (HALF, 256), 0)
        across = lax.broadcasted_iota(jnp.int32, (HALF, 256), 1)
        same = (slot % GROUP) == (across // NS)
        for t in range(STEPS):
            spread = jnp.where(row == (lane % NS) + (2 * NS * t + NS), 1.0, 0.0).astype(BF16)
            cbd[t] = jnp.where(same, dot_nn(io, spread), 0.0).astype(BF16)
            rate = dot_nn(low_ref[t, 0], up_ref[0:256, :]) + dot_nn(low_ref[t, 1], up_ref[256:512, :])
            delta[t] = jax.nn.softplus(rate + dbias_ref[...])

    for part in range(BLOCK // GROUP):
        inner = part * GROUP
        base = pl.multiple_of(group * BLOCK + inner, GROUP)
        terms = jnp.transpose(io_ref[pl.ds(base, GROUP), :].astype(F32))
        rates = [delta[t, pl.ds(base, GROUP), :] for t in range(STEPS)]
        signals = [u_ref[t, inner : inner + GROUP, :].astype(F32) for t in range(STEPS)]
        driven = [rates[t] * signals[t] for t in range(STEPS)]
        for s in range(GROUP):
            source = map_ref[0, half * HALF + base + s]
            moved = moved_ref[jnp.maximum(source, 0)].astype(F32)
            carried = jnp.where(source >= 0, moved, jnp.where(source == -1, state_ref[inner + s], 0.0))
            for t in range(STEPS):
                decayed = carried * jnp.exp2(rates[t][s : s + 1, :] * decay[...])
                carried = decayed + terms[2 * NS * t : 2 * NS * t + NS, s : s + 1] * driven[t][s : s + 1, :]
                held[part, t, NS * s : NS * s + NS, :] = carried.astype(BF16)
            final_ref[inner + s] = carried
        for t in range(STEPS):
            readout = dot_nn(cbd[t, pl.ds(base, GROUP), :], held[part, t]) + skip_ref[...] * signals[t]
            gate = jax.nn.silu(gate_ref[t, inner : inner + GROUP, :].astype(F32))
            gated_ref[t, inner : inner + GROUP, :] = (readout * gate).astype(BF16)


def recur(half, source, low, io, up, dbias, decay, skip, u, gate, state, moved, final=None):
    smem = pl.BlockSpec(memory_space=pltpu.SMEM)
    vmem = pl.BlockSpec(memory_space=pltpu.VMEM)
    groups = HALF // BLOCK
    steps = pl.BlockSpec((STEPS, BLOCK, 512), lambda g: (0, half * groups + g, 0))
    slots = pl.BlockSpec((BLOCK, NS, 512), lambda g: (half * groups + g, 0, 0))
    rows = pl.BlockSpec((STEPS, 2, HALF, 256), lambda g: (0, 0, half, 0))
    terms = pl.BlockSpec((HALF, 128), lambda g: (half, 0))
    extra = [] if final is None else [final]
    return pl.pallas_call(
        functools.partial(recur_kernel, half),
        grid=(groups,),
        out_shape=(
            jax.ShapeDtypeStruct((256, NS, 512), F32),
            jax.ShapeDtypeStruct((STEPS, HALF, 512), BF16),
        ),
        in_specs=[smem, rows, terms, vmem, vmem, vmem, vmem, steps, steps, slots, vmem]
        + [pl.BlockSpec(memory_space=pltpu.HBM)] * len(extra),
        out_specs=(slots, pl.BlockSpec((STEPS, BLOCK, 512), lambda g: (0, g, 0))),
        scratch_shapes=[
            pltpu.VMEM((STEPS, HALF, 512), F32),
            pltpu.VMEM((STEPS, HALF, 256), BF16),
            pltpu.VMEM((BLOCK // GROUP, STEPS, NS * GROUP, 512), BF16),
            pltpu.VMEM((NS, 512), F32),
        ],
        input_output_aliases={11: 0} if extra else {},
        compiler_params=pltpu.CompilerParams(vmem_limit_bytes=60 << 20),
        cost_estimate=pl.CostEstimate(flops=15_000_000_000, bytes_accessed=20_000_000, transcendentals=0),
        name="recur",
    )(source, low, io, up, dbias, decay, skip, u, gate, state, moved, *extra)


SUM_MASKS = (tuple(a + b for b in SIDES[1] for a in SIDES[0] if a + b), (4,))


def mix_kernel(
    first_hbm, second_hbm, other_hbm, weight_hbm, got_a, got_b, swap_a, swap_b, residual_hbm, gain_hbm,
    out_ref,
    gated, weight, residual_ref, gain_ref, own, snd, rcv, hidden, sums, got_sums,
    in_sem, weight_sem, gate_sem, pair_ss, pair_rs, ss, rs, sum_ss, sum_rs,
):
    place = flips()
    me, delta = place
    core = lax.axis_index("inst") % 2
    half = (me // 4) % 2
    gated_copy = pltpu.make_async_copy(second_hbm, gated.at[:, HALF:, 0:512], gate_sem)
    gated_copy.start()
    loads = []

    def load(source, target):
        copy = pltpu.make_async_copy(source, target, in_sem.at[len(loads)])
        copy.start()
        loads.append(copy)

    load(first_hbm, gated.at[:, 0:HALF, 0:512])
    load(other_hbm, gated.at[:, 0:HALF, 512:1024])

    z_here = me // 8
    z_order = [flipped(place, mask) // 8 for mask in (16, 8, 24)] + [z_here]
    for index, z in enumerate(z_order):
        columns = pl.ds(pl.multiple_of(z * 2048 + half * 1024, 1024), 1024)
        load(weight_hbm.at[:, columns], weight.at[z, 0:512])
        sem = weight_sem.at[index]
        low_part = (z % 2) == 0
        mine = (z // 2) == core

        @pl.when(mine & low_part)
        def _():
            pltpu.make_async_copy(got_a, weight.at[z, 512:1024], sem).start()

        @pl.when(mine & ~low_part)
        def _():
            pltpu.make_async_copy(got_b, weight.at[z, 512:1024], sem).start()

        @pl.when(~mine & low_part)
        def _():
            pltpu.make_async_copy(swap_a, weight.at[z, 512:1024], sem).start()

        @pl.when(~mine & ~low_part)
        def _():
            pltpu.make_async_copy(swap_b, weight.at[z, 512:1024], sem).start()

    load(residual_hbm, residual_ref)
    load(gain_hbm.at[:, pl.ds(pl.multiple_of(me * 256, 256), 256)], gain_ref)
    barrier = pltpu.get_barrier_semaphore()
    masks = [mask for group in SUM_MASKS for mask in group]
    for mask in masks:
        pl.semaphore_signal(
            barrier, inc=1, device_id=tp_device(flipped(place, mask)), device_id_type=MESH
        )
    gated_copy.wait()
    pl.semaphore_wait(barrier, len(masks))
    pair_copy = pltpu.make_async_remote_copy(
        gated.at[:, HALF:, 0:512], gated.at[:, HALF:, 512:1024], pair_ss, pair_rs,
        device_id=tp_device(flipped(place, 4)), device_id_type=MESH,
    )
    pair_copy.start()
    loads[0].wait()
    loads[1].wait()

    def copy_of(chunk, p, code, level):
        start, size = CHUNKS[chunk]
        return pltpu.make_async_remote_copy(
            snd.at[p, code, start : start + size], rcv.at[p, code, start : start + size],
            ss.at[chunk, p, code], rs.at[chunk, p, code],
            device_id=tp_device(flipped(place, pair_of(p, level))), device_id_type=MESH,
        )

    def products(chunk):
        start, size = CHUNKS[chunk]

        def product(i, carry):
            if chunk == 0:
                for index, z in enumerate(z_order):

                    @pl.when(i == index)
                    def _():
                        loads[2 + index].wait()
                        pltpu.make_async_copy(got_a, weight.at[z, 512:1024], weight_sem.at[index]).wait()

            bits = [((15 - i) // (1 << (3 - j))) % 2 for j in range(LEVELS)]
            flip = [0] * 5
            for j in range(LEVELS):
                for bit in range(5):
                    if (PAIRS[j] >> bit) & 1:
                        flip[bit] = flip[bit] + bits[j]
            owner = me
            for bit in range(5):
                owner = owner + (flip[bit] % 2) * delta[bit]
            columns = pl.ds(pl.multiple_of((owner % 4) * 256, 256), 256)
            rows = gated[:, start : start + size, :].reshape(STEPS * size, 1024)
            acc = dot_nn(rows, weight[owner // 8, :, columns]).reshape(STEPS, size, 256)
            for p in range(4):
                code = sum(bits[(p + j) % 4] * (1 << (3 - j)) for j in range(LEVELS))

                @pl.when(bits[p] == 1)
                def _():
                    snd[p, code, start : start + size] = acc[p].astype(BF16)
                    copy_of(chunk, p, code, 0).start()

                @pl.when(bits[p] == 0)
                def _():
                    own[p, code, start : start + size] = acc[p]

            return carry

        lax.fori_loop(0, 16, product, 0)

    def summed(chunk, p, code, level):
        start, size = CHUNKS[chunk]
        acc = own[p, code, start : start + size]
        for j in range(level):
            copy_of(chunk, p, (1 << (3 - j)) + code, j).wait_recv()
            acc = acc + rcv[p, (1 << (3 - j)) + code, start : start + size].astype(F32)
        return acc

    for chunk, level in ORDER:
        if (chunk, level) == (0, LEVELS):
            loads[6].wait()
            loads[7].wait()
        start, size = CHUNKS[chunk]
        if level == 0:
            if chunk == 1:
                pair_copy.wait_recv()
            products(chunk)
        elif level < LEVELS:
            n = 1 << (3 - level)

            def send(i, carry):
                code = 2 * n - 1 - i
                for p in range(4):
                    acc = summed(chunk, p, code, level)
                    snd[p, code, start : start + size] = acc.astype(BF16)
                    copy_of(chunk, p, code, level).start()
                return carry

            lax.fori_loop(0, n, send, 0)
        else:
            for p in range(4):
                acc = summed(chunk, p, 0, LEVELS)
                hidden[p, start : start + size] = acc + residual_ref[p, start : start + size].astype(F32)

    which = lax.broadcasted_iota(jnp.int32, (8, 256), 0)
    squares = jnp.zeros((8, 256), F32)
    for p in range(4):
        acc = hidden[p]
        pick = jnp.where(which == p, 1.0, 0.0).astype(BF16)
        squares = squares + dot_nt(pick, (acc * acc).astype(BF16))
    sums[0] = squares
    slot = 0
    sum_copies = []
    for stage, group in enumerate(SUM_MASKS):
        here = []
        for mask in group:
            copy = pltpu.make_async_remote_copy(
                sums.at[stage], got_sums.at[slot], sum_ss.at[slot], sum_rs.at[slot],
                device_id=tp_device(flipped(place, mask)), device_id_type=MESH,
            )
            copy.start()
            here.append((copy, slot))
            slot += 1
        total = sums[stage]
        for copy, index in here:
            copy.wait_recv()
            total = total + got_sums[index]
            sum_copies.append(copy)
        sums[stage + 1] = total
    scale = lax.rsqrt(sums[len(SUM_MASKS)] * (1.0 / D) + EPSILON)
    gain = gain_ref[...]
    coarse = scale.astype(BF16)
    fine = (scale - coarse.astype(F32)).astype(BF16)
    for p in range(4):
        pick = jnp.where(which == p, 1.0, 0.0).astype(BF16)
        factor = dot_tn(coarse, pick) + dot_tn(fine, pick)
        out_ref[p] = (hidden[p] * factor * gain).astype(BF16)

    for copy in sum_copies + [pair_copy]:
        copy.wait_send()
    for chunk in range(len(CHUNKS)):
        for level in range(LEVELS):
            n = 1 << (3 - level)

            def drain(i, carry):
                for p in range(4):
                    copy_of(chunk, p, n + i, level).wait_send()
                return carry

            lax.fori_loop(0, n, drain, 0)


def mix(first, second, other, weight, received, residual, gain):
    vmem = pl.BlockSpec(memory_space=pltpu.VMEM)
    hbm = pl.BlockSpec(memory_space=pltpu.HBM)
    return pl.pallas_call(
        mix_kernel,
        out_shape=jax.ShapeDtypeStruct((STEPS, 256, 256), BF16),
        in_specs=[hbm] * 10,
        out_specs=vmem,
        scratch_shapes=[
            pltpu.VMEM((STEPS, 256, 1024), BF16),
            pltpu.VMEM((4, 1024, 1024), BF16),
            pltpu.VMEM((STEPS, 256, 256), BF16),
            pltpu.VMEM((1, 256), F32),
            pltpu.VMEM((4, 8, 256, 256), F32),
            pltpu.VMEM((4, 16, 256, 256), BF16),
            pltpu.VMEM((4, 16, 256, 256), BF16),
            pltpu.VMEM((STEPS, 256, 256), F32),
            pltpu.VMEM((3, 8, 256), F32),
            pltpu.VMEM((16, 8, 256), F32),
            pltpu.SemaphoreType.DMA((8,)),
            pltpu.SemaphoreType.DMA((4,)),
            pltpu.SemaphoreType.DMA,
            pltpu.SemaphoreType.DMA,
            pltpu.SemaphoreType.DMA,
            pltpu.SemaphoreType.DMA((2, 4, 16)),
            pltpu.SemaphoreType.DMA((2, 4, 16)),
            pltpu.SemaphoreType.DMA((16,)),
            pltpu.SemaphoreType.DMA((16,)),
        ],
        compiler_params=pltpu.CompilerParams(
            collective_id=1, has_side_effects=True, vmem_limit_bytes=60 << 20
        ),
        name="mix",
    )(first, second, other, weight, *received, residual, gain)


def permuted(value, inst_mask, tp_mask):
    places = [(i, t) for i in range(4) for t in range(32)]
    pairs = [(i * 32 + t, (i ^ inst_mask) * 32 + (t ^ tp_mask)) for i, t in places]
    return lax.ppermute(value, ("inst", "tp"), pairs)


def on_device(
    mixer_input,
    gate_input,
    conv_state,
    scan_state,
    leave_slot,
    land_slot,
    move_count,
    conv_weight,
    conv_bias,
    delta_down,
    state_proj,
    delta_up,
    delta_bias,
    decay_log,
    skip_gain,
    out_weight,
    residual,
    norm_gain,
):
    core = lax.axis_index("inst") % 2
    far = 1 - (lax.axis_index("tp") // 4) % 2
    received = []
    for piece in range(2):
        column = (2 * core + piece) * 2048 + far * 1024
        received.append(permuted(lax.dynamic_slice(out_weight, (0, column), (512, 1024)), 2, 4))
    low, io, conv_out, source, moved = project(
        leave_slot, land_slot, move_count, mixer_input, jnp.transpose(conv_state, (1, 0, 2)), scan_state,
        conv_weight, conv_bias.reshape(1, -1), delta_down, state_proj,
    )
    low, received[0] = lax.optimization_barrier((low, received[0]))
    operands = (
        source, low.reshape(4, 2, 256, 256), io.reshape(256, 128), delta_up, delta_bias.reshape(1, -1),
        decay_log, skip_gain.reshape(1, -1), conv_out, gate_input, scan_state, moved.reshape(128, NS, 512),
    )
    final_state, first = recur(0, *operands)
    first, received[1] = lax.optimization_barrier((first, received[1]))
    received = received + [permuted(piece, 1, 0) for piece in received]
    other = permuted(first, 0, 4)
    final_state, second = recur(1, *operands, final_state)
    normed = mix(first, second, other, out_weight, received, residual, norm_gain.reshape(1, -1))
    return (normed, final_state)


def solution(mesh):
    in_specs = (
        P(None, "inst", "tp"),
        P(None, "inst", "tp"),
        P("inst", None, "tp"),
        P("inst", None, "tp"),
        P("inst", None, None),
        P(None, "inst", None),
        P(),
        P(None, "tp"),
        P("tp"),
        P("tp", None),
        P(None, "tp"),
        P(None, "tp"),
        P("tp"),
        P(None, "tp"),
        P("tp"),
        P("tp", None),
        P(None, "inst", "tp"),
        P(),
    )
    out_specs = (P(None, "inst", "tp"), P("inst", None, "tp"))
    return jax.shard_map(
        on_device, mesh=mesh, in_specs=in_specs, out_specs=out_specs, check_vma=False
    )
```

```python
import functools

import jax
import jax.numpy as jnp
from jax import lax
from jax.experimental import pallas as pl
from jax.experimental.pallas import tpu as pltpu
from jax.sharding import PartitionSpec as P

D = 8192
NS = 16
STEPS = 4
EPSILON = 1e-05
LOG2E = 1.4426950408889634
MESH = pl.DeviceIdType.MESH
F32 = jnp.float32
BF16 = jnp.bfloat16

PAIRS = (1, 8, 3, 24)
LEVELS = 4
GROUP = 16
BLOCK = 64
CHUNKS = ((0, 128), (128, 128))
ORDER = ((0, 0), (0, 1), (1, 0), (1, 1), (0, 2), (1, 2), (0, 3), (1, 3), (0, 4), (1, 4))
EARLY = 128


def flips():
    me = lax.axis_index("tp")
    return me, [(1 << bit) * (1 - 2 * ((me // (1 << bit)) % 2)) for bit in range(5)]


def flipped(place, mask):
    me, delta = place
    for bit in range(5):
        if (mask >> bit) & 1:
            me = me + delta[bit]
    return me


def pair_of(part, level):
    return PAIRS[(part + level) % LEVELS]


def tp_device(index):
    return (lax.axis_index("inst"), index)


def inst_partner(mask):
    inst = lax.axis_index("inst")
    core, low = inst % 2, inst // 2
    if mask & 1:
        core = 1 - core
    if mask & 2:
        low = 1 - low
    return low * 2 + core


def dot_nt(a, b):
    return lax.dot_general(a, b, (((1,), (1,)), ((), ())), preferred_element_type=F32)


def dot_tn(a, b):
    return lax.dot_general(a, b, (((0,), (0,)), ((), ())), preferred_element_type=F32)


def dot_nn(a, b):
    return jnp.dot(a, b, preferred_element_type=F32)


SIDES = ((0, 1, 2, 3), (0, 8, 16, 24))
PARTS = (3, 0, 1, 2, 4)
FIRST_STATES = 20


def sum_mask(part, code):
    first, second = SIDES[part % 2], SIDES[1 - part % 2]
    return first[code // 4] ^ second[code % 4]


def sum_moves(part, stage):
    first, second = SIDES[part % 2], SIDES[1 - part % 2]
    if stage == 0:
        return [(c - 1, 4 * c, 4, first[c]) for c in (2, 1, 3)]
    if stage == 1:
        return [(c + 2, c, 1, second[c]) for c in (2, 1, 3)]
    return [(6, 0, 1, 4)]


def project_kernel(
    leave_hbm, land_hbm, count_hbm, mix_hbm, conv_hbm, state_hbm, weight_hbm, bias_hbm, down_hbm, proj_hbm,
    low_out, io_out, u_hbm, map_out, moved_out,
    u_out, leave_smem, count_ref, leave_ref, land_ref, mix_ref, conv_ref, weight_ref, bias_ref, down_ref, proj_ref,
    state_v, pack_conv, got_conv, pack_state, got_state, low, io, snd, rcv, ag, snd_io, rcv_io, ag_io,
    in_sem, state_sem, conv_ss, conv_rs, mig_ss, mig_rs, out_sem, rs_ss, rs_rs, ag_ss, ag_rs,
):
    place = flips()
    inst = lax.axis_index("inst")
    loads = []
    for source, target in (
        (leave_hbm, leave_smem), (count_hbm, count_ref), (leave_hbm, leave_ref), (land_hbm, land_ref),
        (conv_hbm, conv_ref), (mix_hbm, mix_ref), (weight_hbm, weight_ref), (bias_hbm, bias_ref),
        (down_hbm, down_ref), (proj_hbm, proj_ref),
    ):
        copy = pltpu.make_async_copy(source, target, in_sem.at[len(loads)])
        copy.start()
        loads.append(copy)
    state_copy = pltpu.make_async_copy(state_hbm, state_v, state_sem)
    state_copy.start()
    barrier = pltpu.get_barrier_semaphore()
    masks = SIDES[0][1:] + SIDES[1][1:] + (4,)
    for mask in masks:
        pl.semaphore_signal(
            barrier, inc=1, device_id=tp_device(flipped(place, mask)), device_id_type=MESH
        )
    for mask in (1, 2, 3):
        pl.semaphore_signal(
            barrier, inc=1, device_id=(inst_partner(mask), place[0]), device_id_type=MESH
        )
    for copy in loads:
        copy.wait()

    lanes = lax.broadcasted_iota(jnp.int32, (1, 32), 1)
    leave_row = jnp.concatenate(
        [jnp.where(lanes < count_ref[inst, j], leave_ref[0, j : j + 1, :], -1) for j in range(4)], axis=1
    )
    land_row = jnp.concatenate(
        [jnp.where(lanes < count_ref[j, inst], land_ref[j], -1) for j in range(4)], axis=1
    )
    slots = lax.broadcasted_iota(jnp.int32, (256, 128), 0)
    leave_hot = jnp.where(slots == leave_row, 1.0, 0.0)
    land_hot = jnp.where(slots == land_row, 1.0, 0.0)
    keep = 1.0 - jnp.sum(leave_hot + land_hot, axis=1, keepdims=True)
    leave_hot = leave_hot.astype(BF16)
    land_hot = land_hot.astype(BF16)

    for k in range(3):
        pack_conv[:, k] = dot_tn(leave_hot, conv_ref[k]).astype(BF16).reshape(4, 32, 512)
    got_conv[inst] = jnp.zeros((3, 32, 512), BF16)

    pl.semaphore_wait(barrier, len(masks) + 3)
    conv_copies = []
    for mask in (2, 3, 1):
        other = inst_partner(mask)
        copy = pltpu.make_async_remote_copy(
            pack_conv.at[other], got_conv.at[inst], conv_ss.at[mask - 1], conv_rs.at[mask - 1],
            device_id=(other, place[0]), device_id_type=MESH,
        )
        copy.start()
        conv_copies.append(copy)

    taps = [weight_ref[k : k + 1, :] for k in range(4)]
    bias = bias_ref[...]

    def step(t, history):
        total = bias
        for k in range(4):
            source = history[t + k] if t + k < 3 else mix_ref[t + k - 3].astype(F32)
            total = total + taps[k] * source
        u = jax.nn.silu(total).astype(BF16)
        u_out[t] = u
        low[t, 0:8] = dot_nn(u, down_ref[:, 0:256]).reshape(8, 32, 256)
        low[t, 8:16] = dot_nn(u, down_ref[:, 256:512]).reshape(8, 32, 256)
        return u

    def rs_copy(p, move):
        index, start, size, mask = move
        s, r = (snd.at[p], rcv.at[p]) if p < 4 else (snd_io, rcv_io)
        return pltpu.make_async_remote_copy(
            s.at[start : start + size], r.at[start : start + size], rs_ss.at[p, index], rs_rs.at[p, index],
            device_id=tp_device(flipped(place, mask)), device_id_type=MESH,
        )

    def ag_copy(p, move):
        index, start, size, mask = move
        a = ag.at[p] if p < 4 else ag_io
        return pltpu.make_async_remote_copy(
            a.at[0:size], a.at[start : start + size], ag_ss.at[p, index], ag_rs.at[p, index],
            device_id=tp_device(flipped(place, mask)), device_id_type=MESH,
        )

    def block(p, code):
        there = flipped(place, sum_mask(p, code))
        return (there // 8) * 4 + there % 4

    def summed(p, code):
        acc = low[p, block(p, code)] if p < 4 else io[block(p, code)]
        sources = []
        if code < 4:
            sources += [4 * c + code for c in (1, 2, 3)]
        if code == 0:
            sources += [1, 2, 3]
        for index in sources:
            acc = acc + (rcv[p, index] if p < 4 else rcv_io[index]).astype(F32)
        return acc

    def rs_stage(p, stage):
        if stage:
            for move in sum_moves(p, stage - 1):
                rs_copy(p, move).wait_recv()
        for move in sum_moves(p, stage):
            for code in range(move[1], move[1] + move[2]):
                value = summed(p, code).astype(BF16)
                if p < 4:
                    snd[p, code] = value
                else:
                    snd_io[code] = value
            rs_copy(p, move).start()

    us = [None] * 4
    us[3] = step(3, None)
    rs_stage(3, 0)

    state_copy.wait()
    state_copies = []
    for mask in (2, 3, 1):
        other = inst_partner(mask)

        def pack(i, carry):
            pack_state[other, i] = state_v[leave_smem[0, other, i]].astype(BF16)
            return carry

        lax.fori_loop(0, 32, pack, 0, unroll=4)
        for batch, (lo, hi) in enumerate(((0, FIRST_STATES), (FIRST_STATES, 32))):
            copy = pltpu.make_async_remote_copy(
                pack_state.at[other, lo:hi], got_state.at[inst, lo:hi],
                mig_ss.at[mask - 1, batch], mig_rs.at[mask - 1, batch],
                device_id=(other, place[0]), device_id_type=MESH,
            )
            if batch == 0:
                copy.start()
            state_copies.append((batch, copy))

    for copy in conv_copies:
        copy.wait_recv()
    history = []
    for k in range(3):
        moved = dot_nn(land_hot, got_conv[:, k].reshape(128, 512))
        history.append(conv_ref[k].astype(F32) * keep + moved)
    for t in range(3):
        us[t] = step(t, history)
        rs_stage(t, 0)
    proj = proj_ref[...]
    total = jnp.zeros((256, 128), F32)
    for t in range(4):
        pieces = [jnp.zeros_like(proj) if j != t else proj for j in range(4)]
        total = total + dot_nt(us[t], jnp.concatenate(pieces, axis=0))
    io[...] = total.reshape(16, 16, 128)
    rs_stage(4, 0)

    u_copy = pltpu.make_async_copy(u_out, u_hbm, out_sem.at[3])
    u_copy.start()
    number = (lax.broadcasted_iota(jnp.int32, (8, 128), 1) + 1).astype(F32).astype(BF16)
    landed = dot_nt(number, land_hot)
    left = dot_nt(jnp.ones((8, 128), BF16), leave_hot)
    map_out[...] = (landed - left - 1.0).astype(jnp.int32)

    for stage in (1, 2):
        for p in PARTS:
            rs_stage(p, stage)
    for p in PARTS:
        for move in sum_moves(p, 2):
            rs_copy(p, move).wait_recv()
        if p < 4:
            ag[p, 0] = (snd[p, 0].astype(F32) + rcv[p, 0].astype(F32)).astype(BF16)
        else:
            ag_io[0] = (snd_io[0].astype(F32) + rcv_io[0].astype(F32)).astype(BF16)
        for move in sum_moves(p, 1):
            ag_copy(p, move).start()
    for batch, copy in state_copies:
        if batch == 1:
            copy.start()
    for p in PARTS:
        for move in sum_moves(p, 1):
            ag_copy(p, move).wait_recv()
        for move in sum_moves(p, 0):
            ag_copy(p, move).start()
    for p in PARTS:
        for move in sum_moves(p, 0):
            ag_copy(p, move).wait_recv()
        for code in range(16):
            if p < 4:
                low_out[p, block(p, code)] = ag[p, code]
            else:
                io_out[block(p, code)] = ag_io[code]

    for batch, copy in state_copies:
        copy.wait_recv()
    outs = []
    for mask in (1, 2, 3):
        other = inst_partner(mask)
        copy = pltpu.make_async_copy(got_state.at[other], moved_out.at[other], out_sem.at[mask - 1])
        copy.start()
        outs.append(copy)
    for copy in conv_copies:
        copy.wait_send()
    for batch, copy in state_copies:
        copy.wait_send()
    for p in PARTS:
        for stage in range(3):
            for move in sum_moves(p, stage):
                rs_copy(p, move).wait_send()
                if stage < 2:
                    ag_copy(p, move).wait_send()
    for copy in outs + [u_copy]:
        copy.wait()


def project(leave, land, count, mix, conv, state, weight, bias, down, proj):
    vmem = pl.BlockSpec(memory_space=pltpu.VMEM)
    hbm = pl.BlockSpec(memory_space=pltpu.HBM)
    return pl.pallas_call(
        project_kernel,
        out_shape=(
            jax.ShapeDtypeStruct((4, 16, 32, 256), BF16),
            jax.ShapeDtypeStruct((16, 16, 128), BF16),
            jax.ShapeDtypeStruct((4, 256, 512), BF16),
            jax.ShapeDtypeStruct((8, 256), jnp.int32),
            jax.ShapeDtypeStruct((4, 32, 16, 512), BF16),
        ),
        in_specs=[hbm] * 10,
        out_specs=(vmem, vmem, hbm, vmem, hbm),
        scratch_shapes=[
            pltpu.VMEM((4, 256, 512), BF16),
            pltpu.SMEM((1, 4, 32), jnp.int32),
            pltpu.SMEM((4, 4), jnp.int32),
            pltpu.VMEM((1, 4, 32), jnp.int32),
            pltpu.VMEM((4, 1, 32), jnp.int32),
            pltpu.VMEM((4, 256, 512), BF16),
            pltpu.VMEM((3, 256, 512), BF16),
            pltpu.VMEM((4, 512), F32),
            pltpu.VMEM((1, 512), F32),
            pltpu.VMEM((512, 512), BF16),
            pltpu.VMEM((32, 512), BF16),
            pltpu.VMEM((256, 16, 512), F32),
            pltpu.VMEM((4, 3, 32, 512), BF16),
            pltpu.VMEM((4, 3, 32, 512), BF16),
            pltpu.VMEM((4, 32, 16, 512), BF16),
            pltpu.VMEM((4, 32, 16, 512), BF16),
            pltpu.VMEM((4, 16, 32, 256), F32),
            pltpu.VMEM((16, 16, 128), F32),
            pltpu.VMEM((4, 16, 32, 256), BF16),
            pltpu.VMEM((4, 16, 32, 256), BF16),
            pltpu.VMEM((4, 16, 32, 256), BF16),
            pltpu.VMEM((16, 16, 128), BF16),
            pltpu.VMEM((16, 16, 128), BF16),
            pltpu.VMEM((16, 16, 128), BF16),
            pltpu.SemaphoreType.DMA((10,)),
            pltpu.SemaphoreType.DMA,
            pltpu.SemaphoreType.DMA((3,)),
            pltpu.SemaphoreType.DMA((3,)),
            pltpu.SemaphoreType.DMA((3, 2)),
            pltpu.SemaphoreType.DMA((3, 2)),
            pltpu.SemaphoreType.DMA((4,)),
            pltpu.SemaphoreType.DMA((5, 7)),
            pltpu.SemaphoreType.DMA((5, 7)),
            pltpu.SemaphoreType.DMA((5, 7)),
            pltpu.SemaphoreType.DMA((5, 7)),
        ],
        compiler_params=pltpu.CompilerParams(
            collective_id=0, has_side_effects=True, vmem_limit_bytes=60 << 20
        ),
        cost_estimate=pl.CostEstimate(flops=60_000_000_000, bytes_accessed=40_000_000, transcendentals=0),
        name="project",
    )(leave, land, count, mix, conv, state, weight, bias, down, proj)


def recur_kernel(start, size, *refs):
    map_ref, low_ref, io_ref, up_ref, dbias_ref, decay_ref, skip_ref, u_ref, gate_ref, state_ref, moved_ref = refs[:11]
    final_ref, gated_ref, delta, cbd, held, decay = refs[-6:]
    group = pl.program_id(0)

    @pl.when(group == 0)
    def _():
        decay[...] = jnp.exp(decay_ref[...]) * (-LOG2E)
        io = io_ref[start : start + size, :]
        row = lax.broadcasted_iota(jnp.int32, (128, 256), 0)
        lane = lax.broadcasted_iota(jnp.int32, (128, 256), 1)
        slot = lax.broadcasted_iota(jnp.int32, (size, 256), 0)
        across = lax.broadcasted_iota(jnp.int32, (size, 256), 1)
        same = (slot % GROUP) == (across // NS)
        for t in range(STEPS):
            spread = jnp.where(row == (lane % NS) + (2 * NS * t + NS), 1.0, 0.0).astype(BF16)
            cbd[t] = jnp.where(same, dot_nn(io, spread), 0.0).astype(BF16)
            rate = dot_nn(low_ref[t, 0, start : start + size], up_ref[0:256, :])
            rate = rate + dot_nn(low_ref[t, 1, start : start + size], up_ref[256:512, :])
            delta[t] = jax.nn.softplus(rate + dbias_ref[...])

    for part in range(BLOCK // GROUP):
        inner = part * GROUP
        base = pl.multiple_of(group * BLOCK + inner, GROUP)
        terms = jnp.transpose(io_ref[pl.ds(start + base, GROUP), :].astype(F32))
        rates = [delta[t, pl.ds(base, GROUP), :] for t in range(STEPS)]
        signals = [u_ref[t, inner : inner + GROUP, :].astype(F32) for t in range(STEPS)]
        driven = [rates[t] * signals[t] for t in range(STEPS)]
        for s in range(GROUP):
            source = map_ref[0, start + base + s]
            moved = moved_ref[jnp.maximum(source, 0)].astype(F32)
            carried = jnp.where(source >= 0, moved, jnp.where(source == -1, state_ref[inner + s], 0.0))
            for t in range(STEPS):
                decayed = carried * jnp.exp2(rates[t][s : s + 1, :] * decay[...])
                carried = decayed + terms[2 * NS * t : 2 * NS * t + NS, s : s + 1] * driven[t][s : s + 1, :]
                held[part, t, NS * s : NS * s + NS, :] = carried.astype(BF16)
            final_ref[inner + s] = carried
        for t in range(STEPS):
            readout = dot_nn(cbd[t, pl.ds(base, GROUP), :], held[part, t]) + skip_ref[...] * signals[t]
            gate = jax.nn.silu(gate_ref[t, inner : inner + GROUP, :].astype(F32))
            gated_ref[t, inner : inner + GROUP, :] = (readout * gate).astype(BF16)


def recur(start, size, source, low, io, up, dbias, decay, skip, u, gate, state, moved, final=None):
    smem = pl.BlockSpec(memory_space=pltpu.SMEM)
    vmem = pl.BlockSpec(memory_space=pltpu.VMEM)
    groups, lead = size // BLOCK, start // BLOCK
    steps = pl.BlockSpec((STEPS, BLOCK, 512), lambda g: (0, lead + g, 0))
    slots = pl.BlockSpec((BLOCK, NS, 512), lambda g: (lead + g, 0, 0))
    rows = pl.BlockSpec((STEPS, 2, start + size, 256), lambda g: (0, 0, 0, 0))
    terms = pl.BlockSpec((start + size, 128), lambda g: (0, 0))
    extra = [] if final is None else [final]
    return pl.pallas_call(
        functools.partial(recur_kernel, start, size),
        grid=(groups,),
        out_shape=(
            jax.ShapeDtypeStruct((256, NS, 512), F32),
            jax.ShapeDtypeStruct((STEPS, size, 512), BF16),
        ),
        in_specs=[smem, rows, terms, vmem, vmem, vmem, vmem, steps, steps, slots, vmem]
        + [pl.BlockSpec(memory_space=pltpu.HBM)] * len(extra),
        out_specs=(slots, pl.BlockSpec((STEPS, BLOCK, 512), lambda g: (0, g, 0))),
        scratch_shapes=[
            pltpu.VMEM((STEPS, size, 512), F32),
            pltpu.VMEM((STEPS, size, 256), BF16),
            pltpu.VMEM((BLOCK // GROUP, STEPS, NS * GROUP, 512), BF16),
            pltpu.VMEM((NS, 512), F32),
        ],
        input_output_aliases={11: 0} if extra else {},
        compiler_params=pltpu.CompilerParams(vmem_limit_bytes=60 << 20),
        cost_estimate=pl.CostEstimate(flops=15_000_000_000, bytes_accessed=20_000_000, transcendentals=0),
        name="recur",
    )(source, low, io, up, dbias, decay, skip, u, gate, state, moved, *extra)


SUM_MASKS = ((1, 2, 3, 4, 5, 6, 7), (8, 16, 24))


def mix_kernel(
    first_hbm, second_hbm, other_hbm, weight_hbm, got_a, got_b, swap_a, swap_b, residual_hbm, gain_hbm,
    out_ref,
    gated, weight, residual_ref, gain_ref, own, snd, rcv, hidden, sums, got_sums,
    in_sem, weight_sem, gate_sem, pair_ss, pair_rs, ss, rs, sum_ss, sum_rs,
):
    place = flips()
    me, delta = place
    core = lax.axis_index("inst") % 2
    half = (me // 4) % 2
    gated_copy = pltpu.make_async_copy(second_hbm, gated.at[:, EARLY:, 0:512], gate_sem)
    gated_copy.start()
    loads = []

    def load(source, target):
        copy = pltpu.make_async_copy(source, target, in_sem.at[len(loads)])
        copy.start()
        loads.append(copy)

    load(first_hbm, gated.at[:, 0:EARLY, 0:512])
    load(other_hbm, gated.at[:, 0:EARLY, 512:1024])

    z_here = me // 8
    z_order = [flipped(place, mask) // 8 for mask in (16, 8, 24)] + [z_here]
    for index, z in enumerate(z_order):
        columns = pl.ds(pl.multiple_of(z * 2048 + half * 1024, 1024), 1024)
        load(weight_hbm.at[:, columns], weight.at[z, 0:512])
        sem = weight_sem.at[index]
        low_part = (z % 2) == 0
        mine = (z // 2) == core

        @pl.when(mine & low_part)
        def _():
            pltpu.make_async_copy(got_a, weight.at[z, 512:1024], sem).start()

        @pl.when(mine & ~low_part)
        def _():
            pltpu.make_async_copy(got_b, weight.at[z, 512:1024], sem).start()

        @pl.when(~mine & low_part)
        def _():
            pltpu.make_async_copy(swap_a, weight.at[z, 512:1024], sem).start()

        @pl.when(~mine & ~low_part)
        def _():
            pltpu.make_async_copy(swap_b, weight.at[z, 512:1024], sem).start()

    load(residual_hbm, residual_ref)
    load(gain_hbm.at[:, pl.ds(pl.multiple_of(me * 256, 256), 256)], gain_ref)
    barrier = pltpu.get_barrier_semaphore()
    masks = [mask for group in SUM_MASKS for mask in group]
    for mask in masks:
        pl.semaphore_signal(
            barrier, inc=1, device_id=tp_device(flipped(place, mask)), device_id_type=MESH
        )
    gated_copy.wait()
    pl.semaphore_wait(barrier, len(masks))
    pair_copies = []
    for start, size in CHUNKS[1:]:
        copy = pltpu.make_async_remote_copy(
            gated.at[:, start : start + size, 0:512], gated.at[:, start : start + size, 512:1024],
            pair_ss.at[len(pair_copies)], pair_rs.at[len(pair_copies)],
            device_id=tp_device(flipped(place, 4)), device_id_type=MESH,
        )
        copy.start()
        pair_copies.append(copy)
    loads[0].wait()
    loads[1].wait()

    def copy_of(chunk, p, code, level):
        start, size = CHUNKS[chunk]
        return pltpu.make_async_remote_copy(
            snd.at[p, code, start : start + size], rcv.at[p, code, start : start + size],
            ss.at[chunk, p, code], rs.at[chunk, p, code],
            device_id=tp_device(flipped(place, pair_of(p, level))), device_id_type=MESH,
        )

    def products(chunk):
        start, size = CHUNKS[chunk]

        def product(i, carry):
            if chunk == 0:
                for index, z in enumerate(z_order):

                    @pl.when(i == index)
                    def _():
                        loads[2 + index].wait()
                        pltpu.make_async_copy(got_a, weight.at[z, 512:1024], weight_sem.at[index]).wait()

            bits = [((15 - i) // (1 << (3 - j))) % 2 for j in range(LEVELS)]
            flip = [0] * 5
            for j in range(LEVELS):
                for bit in range(5):
                    if (PAIRS[j] >> bit) & 1:
                        flip[bit] = flip[bit] + bits[j]
            owner = me
            for bit in range(5):
                owner = owner + (flip[bit] % 2) * delta[bit]
            columns = pl.ds(pl.multiple_of((owner % 4) * 256, 256), 256)
            rows = gated[:, start : start + size, :].reshape(STEPS * size, 1024)
            acc = dot_nn(rows, weight[owner // 8, :, columns]).reshape(STEPS, size, 256)
            for p in range(4):
                code = sum(bits[(p + j) % 4] * (1 << (3 - j)) for j in range(LEVELS))

                @pl.when(bits[p] == 1)
                def _():
                    snd[p, code, start : start + size] = acc[p].astype(BF16)
                    copy_of(chunk, p, code, 0).start()

                @pl.when(bits[p] == 0)
                def _():
                    own[p, code, start : start + size] = acc[p]

            return carry

        lax.fori_loop(0, 16, product, 0)

    def summed(chunk, p, code, level):
        start, size = CHUNKS[chunk]
        acc = own[p, code, start : start + size]
        for j in range(level):
            copy_of(chunk, p, (1 << (3 - j)) + code, j).wait_recv()
            acc = acc + rcv[p, (1 << (3 - j)) + code, start : start + size].astype(F32)
        return acc

    for chunk, level in ORDER:
        if (chunk, level) == (0, LEVELS):
            loads[6].wait()
            loads[7].wait()
        start, size = CHUNKS[chunk]
        if level == 0:
            if chunk:
                pair_copies[chunk - 1].wait_recv()
            products(chunk)
        elif level < LEVELS:
            n = 1 << (3 - level)

            def send(i, carry):
                code = 2 * n - 1 - i
                for p in range(4):
                    acc = summed(chunk, p, code, level)
                    snd[p, code, start : start + size] = acc.astype(BF16)
                    copy_of(chunk, p, code, level).start()
                return carry

            lax.fori_loop(0, n, send, 0)
        else:
            for p in range(4):
                acc = summed(chunk, p, 0, LEVELS)
                hidden[p, start : start + size] = acc + residual_ref[p, start : start + size].astype(F32)

    which = lax.broadcasted_iota(jnp.int32, (8, 256), 0)
    squares = jnp.zeros((8, 256), F32)
    for p in range(4):
        acc = hidden[p]
        pick = jnp.where(which == p, 1.0, 0.0).astype(BF16)
        squares = squares + dot_nt(pick, (acc * acc).astype(BF16))
    sums[0] = squares
    slot = 0
    sum_copies = []
    for stage, group in enumerate(SUM_MASKS):
        here = []
        for mask in group:
            copy = pltpu.make_async_remote_copy(
                sums.at[stage], got_sums.at[slot], sum_ss.at[slot], sum_rs.at[slot],
                device_id=tp_device(flipped(place, mask)), device_id_type=MESH,
            )
            copy.start()
            here.append((copy, slot))
            slot += 1
        total = sums[stage]
        for copy, index in here:
            copy.wait_recv()
            total = total + got_sums[index]
            sum_copies.append(copy)
        sums[stage + 1] = total
    scale = lax.rsqrt(sums[len(SUM_MASKS)] * (1.0 / D) + EPSILON)
    gain = gain_ref[...]
    coarse = scale.astype(BF16)
    fine = (scale - coarse.astype(F32)).astype(BF16)
    for p in range(4):
        pick = jnp.where(which == p, 1.0, 0.0).astype(BF16)
        factor = dot_tn(coarse, pick) + dot_tn(fine, pick)
        out_ref[p] = (hidden[p] * factor * gain).astype(BF16)

    for copy in sum_copies + pair_copies:
        copy.wait_send()
    for chunk in range(len(CHUNKS)):
        for level in range(LEVELS):
            n = 1 << (3 - level)

            def drain(i, carry):
                for p in range(4):
                    copy_of(chunk, p, n + i, level).wait_send()
                return carry

            lax.fori_loop(0, n, drain, 0)


def mix(first, second, other, weight, received, residual, gain):
    vmem = pl.BlockSpec(memory_space=pltpu.VMEM)
    hbm = pl.BlockSpec(memory_space=pltpu.HBM)
    return pl.pallas_call(
        mix_kernel,
        out_shape=jax.ShapeDtypeStruct((STEPS, 256, 256), BF16),
        in_specs=[hbm] * 10,
        out_specs=vmem,
        scratch_shapes=[
            pltpu.VMEM((STEPS, 256, 1024), BF16),
            pltpu.VMEM((4, 1024, 1024), BF16),
            pltpu.VMEM((STEPS, 256, 256), BF16),
            pltpu.VMEM((1, 256), F32),
            pltpu.VMEM((4, 8, 256, 256), F32),
            pltpu.VMEM((4, 16, 256, 256), BF16),
            pltpu.VMEM((4, 16, 256, 256), BF16),
            pltpu.VMEM((STEPS, 256, 256), F32),
            pltpu.VMEM((3, 8, 256), F32),
            pltpu.VMEM((10, 8, 256), F32),
            pltpu.SemaphoreType.DMA((8,)),
            pltpu.SemaphoreType.DMA((4,)),
            pltpu.SemaphoreType.DMA,
            pltpu.SemaphoreType.DMA((2,)),
            pltpu.SemaphoreType.DMA((2,)),
            pltpu.SemaphoreType.DMA((2, 4, 16)),
            pltpu.SemaphoreType.DMA((2, 4, 16)),
            pltpu.SemaphoreType.DMA((10,)),
            pltpu.SemaphoreType.DMA((10,)),
        ],
        compiler_params=pltpu.CompilerParams(
            collective_id=1, has_side_effects=True, vmem_limit_bytes=60 << 20
        ),
        name="mix",
    )(first, second, other, weight, *received, residual, gain)


def permuted(value, inst_mask, tp_mask):
    places = [(i, t) for i in range(4) for t in range(32)]
    pairs = [(i * 32 + t, (i ^ inst_mask) * 32 + (t ^ tp_mask)) for i, t in places]
    return lax.ppermute(value, ("inst", "tp"), pairs)


def on_device(
    mixer_input,
    gate_input,
    conv_state,
    scan_state,
    leave_slot,
    land_slot,
    move_count,
    conv_weight,
    conv_bias,
    delta_down,
    state_proj,
    delta_up,
    delta_bias,
    decay_log,
    skip_gain,
    out_weight,
    residual,
    norm_gain,
):
    core = lax.axis_index("inst") % 2
    far = 1 - (lax.axis_index("tp") // 4) % 2
    received = []
    for piece in range(2):
        column = (2 * core + piece) * 2048 + far * 1024
        received.append(permuted(lax.dynamic_slice(out_weight, (0, column), (512, 1024)), 2, 4))
    low, io, conv_out, source, moved = project(
        leave_slot, land_slot, move_count, mixer_input, jnp.transpose(conv_state, (1, 0, 2)), scan_state,
        conv_weight, conv_bias.reshape(1, -1), delta_down, state_proj,
    )
    low, received[0] = lax.optimization_barrier((low, received[0]))
    operands = (
        source, low.reshape(4, 2, 256, 256), io.reshape(256, 128), delta_up, delta_bias.reshape(1, -1),
        decay_log, skip_gain.reshape(1, -1), conv_out, gate_input, scan_state, moved.reshape(128, NS, 512),
    )
    final_state, first = recur(0, EARLY, *operands)
    first, received[1] = lax.optimization_barrier((first, received[1]))
    received = received + [permuted(piece, 1, 0) for piece in received]
    other = permuted(first, 0, 4)
    final_state, second = recur(EARLY, 256 - EARLY, *operands, final_state)
    normed = mix(first, second, other, out_weight, received, residual, norm_gain.reshape(1, -1))
    return (normed, final_state)


def solution(mesh):
    in_specs = (
        P(None, "inst", "tp"),
        P(None, "inst", "tp"),
        P("inst", None, "tp"),
        P("inst", None, "tp"),
        P("inst", None, None),
        P(None, "inst", None),
        P(),
        P(None, "tp"),
        P("tp"),
        P("tp", None),
        P(None, "tp"),
        P(None, "tp"),
        P("tp"),
        P(None, "tp"),
        P("tp"),
        P("tp", None),
        P(None, "inst", "tp"),
        P(),
    )
    out_specs = (P(None, "inst", "tp"), P("inst", None, "tp"))
    return jax.shard_map(
        on_device, mesh=mesh, in_specs=in_specs, out_specs=out_specs, check_vma=False
    )
```

```python
import functools

import jax
import jax.numpy as jnp
from jax import lax
from jax.experimental import pallas as pl
from jax.experimental.pallas import tpu as pltpu
from jax.sharding import PartitionSpec as P

D = 8192
NS = 16
STEPS = 4
EPSILON = 1e-05
LOG2E = 1.4426950408889634
MESH = pl.DeviceIdType.MESH
F32 = jnp.float32
BF16 = jnp.bfloat16

PAIRS = (1, 8, 3, 24)
LEVELS = 4
GROUP = 16
BLOCK = 64
CHUNKS = ((0, 128), (128, 128))
ORDER = ((0, 0), (0, 1), (1, 0), (1, 1), (0, 2), (1, 2), (0, 3), (1, 3), (0, 4), (1, 4))
EARLY = 128


def flips():
    me = lax.axis_index("tp")
    return me, [(1 << bit) * (1 - 2 * ((me // (1 << bit)) % 2)) for bit in range(5)]


def flipped(place, mask):
    me, delta = place
    for bit in range(5):
        if (mask >> bit) & 1:
            me = me + delta[bit]
    return me


def pair_of(part, level):
    return PAIRS[(part + level) % LEVELS]


def tp_device(index):
    return (lax.axis_index("inst"), index)


def inst_partner(mask):
    inst = lax.axis_index("inst")
    core, low = inst % 2, inst // 2
    if mask & 1:
        core = 1 - core
    if mask & 2:
        low = 1 - low
    return low * 2 + core


def dot_nt(a, b):
    return lax.dot_general(a, b, (((1,), (1,)), ((), ())), preferred_element_type=F32)


def dot_tn(a, b):
    return lax.dot_general(a, b, (((0,), (0,)), ((), ())), preferred_element_type=F32)


def dot_nn(a, b):
    return jnp.dot(a, b, preferred_element_type=F32)


SIDES = ((0, 1, 2, 3), (0, 8, 16, 24))
PARTS = (3, 0, 1, 2, 4)
FIRST_STATES = 20


def sum_mask(part, code):
    first, second = SIDES[part % 2], SIDES[1 - part % 2]
    return first[code // 4] ^ second[code % 4]


def sum_moves(part, stage):
    first, second = SIDES[part % 2], SIDES[1 - part % 2]
    if stage == 0:
        return [(c - 1, 4 * c, 4, first[c]) for c in (2, 1, 3)]
    if stage == 1:
        return [(c + 2, c, 1, second[c]) for c in (2, 1, 3)]
    return [(6, 0, 1, 4)]


def project_kernel(
    leave_hbm, land_hbm, count_hbm, mix_hbm, conv_hbm, state_hbm, weight_hbm, bias_hbm, down_hbm, proj_hbm,
    low_out, io_out, u_hbm, map_out, moved_out,
    u_out, leave_smem, count_ref, leave_ref, land_ref, mix_ref, conv_ref, weight_ref, bias_ref, down_ref, proj_ref,
    state_v, pack_conv, got_conv, pack_state, got_state, low, io, snd, rcv, ag, snd_io, rcv_io, ag_io,
    in_sem, state_sem, conv_ss, conv_rs, mig_ss, mig_rs, out_sem, rs_ss, rs_rs, ag_ss, ag_rs,
):
    place = flips()
    inst = lax.axis_index("inst")
    loads = []
    for source, target in (
        (leave_hbm, leave_smem), (count_hbm, count_ref), (leave_hbm, leave_ref), (land_hbm, land_ref),
        (conv_hbm, conv_ref), (mix_hbm, mix_ref), (weight_hbm, weight_ref), (bias_hbm, bias_ref),
        (down_hbm, down_ref), (proj_hbm, proj_ref),
    ):
        copy = pltpu.make_async_copy(source, target, in_sem.at[len(loads)])
        copy.start()
        loads.append(copy)
    state_copy = pltpu.make_async_copy(state_hbm, state_v, state_sem)
    state_copy.start()
    barrier = pltpu.get_barrier_semaphore()
    masks = SIDES[0][1:] + SIDES[1][1:] + (4,)
    for mask in masks:
        pl.semaphore_signal(
            barrier, inc=1, device_id=tp_device(flipped(place, mask)), device_id_type=MESH
        )
    for mask in (1, 2, 3):
        pl.semaphore_signal(
            barrier, inc=1, device_id=(inst_partner(mask), place[0]), device_id_type=MESH
        )
    for copy in loads:
        copy.wait()

    lanes = lax.broadcasted_iota(jnp.int32, (1, 32), 1)
    leave_row = jnp.concatenate(
        [jnp.where(lanes < count_ref[inst, j], leave_ref[0, j : j + 1, :], -1) for j in range(4)], axis=1
    )
    land_row = jnp.concatenate(
        [jnp.where(lanes < count_ref[j, inst], land_ref[j], -1) for j in range(4)], axis=1
    )
    slots = lax.broadcasted_iota(jnp.int32, (256, 128), 0)
    leave_hot = jnp.where(slots == leave_row, 1.0, 0.0)
    land_hot = jnp.where(slots == land_row, 1.0, 0.0)
    keep = 1.0 - jnp.sum(leave_hot + land_hot, axis=1, keepdims=True)
    leave_hot = leave_hot.astype(BF16)
    land_hot = land_hot.astype(BF16)

    for k in range(3):
        pack_conv[:, k] = dot_tn(leave_hot, conv_ref[k]).astype(BF16).reshape(4, 32, 512)
    got_conv[inst] = jnp.zeros((3, 32, 512), BF16)

    pl.semaphore_wait(barrier, len(masks) + 3)
    conv_copies = []
    for mask in (2, 3, 1):
        other = inst_partner(mask)
        copy = pltpu.make_async_remote_copy(
            pack_conv.at[other], got_conv.at[inst], conv_ss.at[mask - 1], conv_rs.at[mask - 1],
            device_id=(other, place[0]), device_id_type=MESH,
        )
        copy.start()
        conv_copies.append(copy)

    taps = [weight_ref[k : k + 1, :] for k in range(4)]
    bias = bias_ref[...]

    def step(t, history):
        total = bias
        for k in range(4):
            source = history[t + k] if t + k < 3 else mix_ref[t + k - 3].astype(F32)
            total = total + taps[k] * source
        u = jax.nn.silu(total).astype(BF16)
        u_out[t] = u
        low[t, 0:8] = dot_nn(u, down_ref[:, 0:256]).reshape(8, 32, 256)
        low[t, 8:16] = dot_nn(u, down_ref[:, 256:512]).reshape(8, 32, 256)
        return u

    def rs_copy(p, move):
        index, start, size, mask = move
        s, r = (snd.at[p], rcv.at[p]) if p < 4 else (snd_io, rcv_io)
        return pltpu.make_async_remote_copy(
            s.at[start : start + size], r.at[start : start + size], rs_ss.at[p, index], rs_rs.at[p, index],
            device_id=tp_device(flipped(place, mask)), device_id_type=MESH,
        )

    def ag_copy(p, move):
        index, start, size, mask = move
        a = ag.at[p] if p < 4 else ag_io
        return pltpu.make_async_remote_copy(
            a.at[0:size], a.at[start : start + size], ag_ss.at[p, index], ag_rs.at[p, index],
            device_id=tp_device(flipped(place, mask)), device_id_type=MESH,
        )

    def block(p, code):
        there = flipped(place, sum_mask(p, code))
        return (there // 8) * 4 + there % 4

    def summed(p, code):
        acc = low[p, block(p, code)] if p < 4 else io[block(p, code)]
        sources = []
        if code < 4:
            sources += [4 * c + code for c in (1, 2, 3)]
        if code == 0:
            sources += [1, 2, 3]
        for index in sources:
            acc = acc + (rcv[p, index] if p < 4 else rcv_io[index]).astype(F32)
        return acc

    def rs_stage(p, stage):
        if stage:
            for move in sum_moves(p, stage - 1):
                rs_copy(p, move).wait_recv()
        for move in sum_moves(p, stage):
            for code in range(move[1], move[1] + move[2]):
                value = summed(p, code).astype(BF16)
                if p < 4:
                    snd[p, code] = value
                else:
                    snd_io[code] = value
            rs_copy(p, move).start()

    us = [None] * 4
    us[3] = step(3, None)
    rs_stage(3, 0)

    state_copy.wait()
    state_copies = []
    for mask in (2, 3, 1):
        other = inst_partner(mask)

        def pack(i, carry):
            pack_state[other, i] = state_v[leave_smem[0, other, i]].astype(BF16)
            return carry

        lax.fori_loop(0, 32, pack, 0, unroll=4)
        for batch, (lo, hi) in enumerate(((0, FIRST_STATES), (FIRST_STATES, 32))):
            copy = pltpu.make_async_remote_copy(
                pack_state.at[other, lo:hi], got_state.at[inst, lo:hi],
                mig_ss.at[mask - 1, batch], mig_rs.at[mask - 1, batch],
                device_id=(other, place[0]), device_id_type=MESH,
            )
            if batch == 0:
                copy.start()
            state_copies.append((batch, copy))

    for copy in conv_copies:
        copy.wait_recv()
    history = []
    for k in range(3):
        moved = dot_nn(land_hot, got_conv[:, k].reshape(128, 512))
        history.append(conv_ref[k].astype(F32) * keep + moved)
    for t in range(3):
        us[t] = step(t, history)
        rs_stage(t, 0)
    proj = proj_ref[...]
    total = jnp.zeros((256, 128), F32)
    for t in range(4):
        pieces = [jnp.zeros_like(proj) if j != t else proj for j in range(4)]
        total = total + dot_nt(us[t], jnp.concatenate(pieces, axis=0))
    io[...] = total.reshape(16, 16, 128)
    rs_stage(4, 0)

    u_copy = pltpu.make_async_copy(u_out, u_hbm, out_sem.at[3])
    u_copy.start()
    number = (lax.broadcasted_iota(jnp.int32, (8, 128), 1) + 1).astype(F32).astype(BF16)
    landed = dot_nt(number, land_hot)
    left = dot_nt(jnp.ones((8, 128), BF16), leave_hot)
    map_out[...] = (landed - left - 1.0).astype(jnp.int32)

    for stage in (1, 2):
        for p in PARTS:
            rs_stage(p, stage)
    for p in PARTS:
        for move in sum_moves(p, 2):
            rs_copy(p, move).wait_recv()
        if p < 4:
            ag[p, 0] = (snd[p, 0].astype(F32) + rcv[p, 0].astype(F32)).astype(BF16)
        else:
            ag_io[0] = (snd_io[0].astype(F32) + rcv_io[0].astype(F32)).astype(BF16)
        for move in sum_moves(p, 1):
            ag_copy(p, move).start()
    for batch, copy in state_copies:
        if batch == 1:
            copy.start()
    for p in PARTS:
        for move in sum_moves(p, 1):
            ag_copy(p, move).wait_recv()
        for move in sum_moves(p, 0):
            ag_copy(p, move).start()
    for p in PARTS:
        for move in sum_moves(p, 0):
            ag_copy(p, move).wait_recv()
        for code in range(16):
            if p < 4:
                low_out[p, block(p, code)] = ag[p, code]
            else:
                io_out[block(p, code)] = ag_io[code]

    for batch, copy in state_copies:
        copy.wait_recv()
    outs = []
    for mask in (1, 2, 3):
        other = inst_partner(mask)
        copy = pltpu.make_async_copy(got_state.at[other], moved_out.at[other], out_sem.at[mask - 1])
        copy.start()
        outs.append(copy)
    for copy in conv_copies:
        copy.wait_send()
    for batch, copy in state_copies:
        copy.wait_send()
    for p in PARTS:
        for stage in range(3):
            for move in sum_moves(p, stage):
                rs_copy(p, move).wait_send()
                if stage < 2:
                    ag_copy(p, move).wait_send()
    for copy in outs + [u_copy]:
        copy.wait()


def project(leave, land, count, mix, conv, state, weight, bias, down, proj):
    vmem = pl.BlockSpec(memory_space=pltpu.VMEM)
    hbm = pl.BlockSpec(memory_space=pltpu.HBM)
    return pl.pallas_call(
        project_kernel,
        out_shape=(
            jax.ShapeDtypeStruct((4, 16, 32, 256), BF16),
            jax.ShapeDtypeStruct((16, 16, 128), BF16),
            jax.ShapeDtypeStruct((4, 256, 512), BF16),
            jax.ShapeDtypeStruct((8, 256), jnp.int32),
            jax.ShapeDtypeStruct((4, 32, 16, 512), BF16),
        ),
        in_specs=[hbm] * 10,
        out_specs=(vmem, vmem, hbm, vmem, hbm),
        scratch_shapes=[
            pltpu.VMEM((4, 256, 512), BF16),
            pltpu.SMEM((1, 4, 32), jnp.int32),
            pltpu.SMEM((4, 4), jnp.int32),
            pltpu.VMEM((1, 4, 32), jnp.int32),
            pltpu.VMEM((4, 1, 32), jnp.int32),
            pltpu.VMEM((4, 256, 512), BF16),
            pltpu.VMEM((3, 256, 512), BF16),
            pltpu.VMEM((4, 512), F32),
            pltpu.VMEM((1, 512), F32),
            pltpu.VMEM((512, 512), BF16),
            pltpu.VMEM((32, 512), BF16),
            pltpu.VMEM((256, 16, 512), F32),
            pltpu.VMEM((4, 3, 32, 512), BF16),
            pltpu.VMEM((4, 3, 32, 512), BF16),
            pltpu.VMEM((4, 32, 16, 512), BF16),
            pltpu.VMEM((4, 32, 16, 512), BF16),
            pltpu.VMEM((4, 16, 32, 256), F32),
            pltpu.VMEM((16, 16, 128), F32),
            pltpu.VMEM((4, 16, 32, 256), BF16),
            pltpu.VMEM((4, 16, 32, 256), BF16),
            pltpu.VMEM((4, 16, 32, 256), BF16),
            pltpu.VMEM((16, 16, 128), BF16),
            pltpu.VMEM((16, 16, 128), BF16),
            pltpu.VMEM((16, 16, 128), BF16),
            pltpu.SemaphoreType.DMA((10,)),
            pltpu.SemaphoreType.DMA,
            pltpu.SemaphoreType.DMA((3,)),
            pltpu.SemaphoreType.DMA((3,)),
            pltpu.SemaphoreType.DMA((3, 2)),
            pltpu.SemaphoreType.DMA((3, 2)),
            pltpu.SemaphoreType.DMA((4,)),
            pltpu.SemaphoreType.DMA((5, 7)),
            pltpu.SemaphoreType.DMA((5, 7)),
            pltpu.SemaphoreType.DMA((5, 7)),
            pltpu.SemaphoreType.DMA((5, 7)),
        ],
        compiler_params=pltpu.CompilerParams(
            collective_id=0, has_side_effects=True, vmem_limit_bytes=60 << 20
        ),
        cost_estimate=pl.CostEstimate(flops=60_000_000_000, bytes_accessed=40_000_000, transcendentals=0),
        name="project",
    )(leave, land, count, mix, conv, state, weight, bias, down, proj)


def recur_kernel(start, size, *refs):
    map_ref, low_ref, io_ref, up_ref, dbias_ref, decay_ref, skip_ref, u_ref, gate_ref, state_ref, moved_hbm = refs[:11]
    final_ref, gated_ref, delta, cbd, held, decay, moved_ref, moved_sem = refs[-8:]
    group = pl.program_id(0)

    @pl.when(group == 0)
    def _():
        moved_copy = pltpu.make_async_copy(moved_hbm, moved_ref, moved_sem)
        moved_copy.start()
        decay[...] = jnp.exp(decay_ref[...]) * (-LOG2E)
        io = io_ref[start : start + size, :]
        row = lax.broadcasted_iota(jnp.int32, (128, 256), 0)
        lane = lax.broadcasted_iota(jnp.int32, (128, 256), 1)
        slot = lax.broadcasted_iota(jnp.int32, (size, 256), 0)
        across = lax.broadcasted_iota(jnp.int32, (size, 256), 1)
        same = (slot % GROUP) == (across // NS)
        for t in range(STEPS):
            spread = jnp.where(row == (lane % NS) + (2 * NS * t + NS), 1.0, 0.0).astype(BF16)
            cbd[t] = jnp.where(same, dot_nn(io, spread), 0.0).astype(BF16)
            rate = dot_nn(low_ref[t, 0, start : start + size], up_ref[0:256, :])
            rate = rate + dot_nn(low_ref[t, 1, start : start + size], up_ref[256:512, :])
            delta[t] = jax.nn.softplus(rate + dbias_ref[...])
        moved_copy.wait()

    for part in range(BLOCK // GROUP):
        inner = part * GROUP
        base = pl.multiple_of(group * BLOCK + inner, GROUP)
        terms = jnp.transpose(io_ref[pl.ds(start + base, GROUP), :].astype(F32))
        rates = [delta[t, pl.ds(base, GROUP), :] for t in range(STEPS)]
        signals = [u_ref[t, inner : inner + GROUP, :].astype(F32) for t in range(STEPS)]
        driven = [rates[t] * signals[t] for t in range(STEPS)]
        for s in range(GROUP):
            source = map_ref[0, start + base + s]
            moved = moved_ref[jnp.maximum(source, 0)].astype(F32)
            carried = jnp.where(source >= 0, moved, jnp.where(source == -1, state_ref[inner + s], 0.0))
            for t in range(STEPS):
                decayed = carried * jnp.exp2(rates[t][s : s + 1, :] * decay[...])
                carried = decayed + terms[2 * NS * t : 2 * NS * t + NS, s : s + 1] * driven[t][s : s + 1, :]
                held[part, t, NS * s : NS * s + NS, :] = carried.astype(BF16)
            final_ref[inner + s] = carried
        for t in range(STEPS):
            readout = dot_nn(cbd[t, pl.ds(base, GROUP), :], held[part, t]) + skip_ref[...] * signals[t]
            gate = jax.nn.silu(gate_ref[t, inner : inner + GROUP, :].astype(F32))
            gated_ref[t, inner : inner + GROUP, :] = (readout * gate).astype(BF16)


def recur(start, size, source, low, io, up, dbias, decay, skip, u, gate, state, moved, final=None):
    smem = pl.BlockSpec(memory_space=pltpu.SMEM)
    vmem = pl.BlockSpec(memory_space=pltpu.VMEM)
    groups, lead = size // BLOCK, start // BLOCK
    steps = pl.BlockSpec((STEPS, BLOCK, 512), lambda g: (0, lead + g, 0))
    slots = pl.BlockSpec((BLOCK, NS, 512), lambda g: (lead + g, 0, 0))
    rows = pl.BlockSpec((STEPS, 2, start + size, 256), lambda g: (0, 0, 0, 0))
    terms = pl.BlockSpec((start + size, 128), lambda g: (0, 0))
    extra = [] if final is None else [final]
    return pl.pallas_call(
        functools.partial(recur_kernel, start, size),
        grid=(groups,),
        out_shape=(
            jax.ShapeDtypeStruct((256, NS, 512), F32),
            jax.ShapeDtypeStruct((STEPS, size, 512), BF16),
        ),
        in_specs=[smem, rows, terms, vmem, vmem, vmem, vmem, steps, steps, slots]
        + [pl.BlockSpec(memory_space=pltpu.HBM)] * (1 + len(extra)),
        out_specs=(slots, pl.BlockSpec((STEPS, BLOCK, 512), lambda g: (0, g, 0))),
        scratch_shapes=[
            pltpu.VMEM((STEPS, size, 512), F32),
            pltpu.VMEM((STEPS, size, 256), BF16),
            pltpu.VMEM((BLOCK // GROUP, STEPS, NS * GROUP, 512), BF16),
            pltpu.VMEM((NS, 512), F32),
            pltpu.VMEM((128, NS, 512), BF16),
            pltpu.SemaphoreType.DMA,
        ],
        input_output_aliases={11: 0} if extra else {},
        compiler_params=pltpu.CompilerParams(vmem_limit_bytes=60 << 20),
        cost_estimate=pl.CostEstimate(flops=15_000_000_000, bytes_accessed=20_000_000, transcendentals=0),
        name="recur",
    )(source, low, io, up, dbias, decay, skip, u, gate, state, moved, *extra)


SUM_MASKS = ((1, 2, 3, 4, 5, 6, 7), (8, 16, 24))


def mix_kernel(
    first_hbm, second_hbm, other_hbm, weight_hbm, got_a, got_b, swap_a, swap_b, residual_hbm, gain_hbm,
    out_ref,
    gated, weight, residual_ref, gain_ref, own, snd, rcv, hidden, sums, got_sums,
    in_sem, weight_sem, gate_sem, pair_ss, pair_rs, ss, rs, sum_ss, sum_rs,
):
    place = flips()
    me, delta = place
    core = lax.axis_index("inst") % 2
    half = (me // 4) % 2
    gated_copy = pltpu.make_async_copy(second_hbm, gated.at[:, EARLY:, 0:512], gate_sem)
    gated_copy.start()
    loads = []

    def load(source, target):
        copy = pltpu.make_async_copy(source, target, in_sem.at[len(loads)])
        copy.start()
        loads.append(copy)

    load(first_hbm, gated.at[:, 0:EARLY, 0:512])
    load(other_hbm, gated.at[:, 0:EARLY, 512:1024])

    z_here = me // 8
    z_order = [flipped(place, mask) // 8 for mask in (16, 8, 24)] + [z_here]
    for index, z in enumerate(z_order):
        columns = pl.ds(pl.multiple_of(z * 2048 + half * 1024, 1024), 1024)
        load(weight_hbm.at[:, columns], weight.at[z, 0:512])
        sem = weight_sem.at[index]
        low_part = (z % 2) == 0
        mine = (z // 2) == core

        @pl.when(mine & low_part)
        def _():
            pltpu.make_async_copy(got_a, weight.at[z, 512:1024], sem).start()

        @pl.when(mine & ~low_part)
        def _():
            pltpu.make_async_copy(got_b, weight.at[z, 512:1024], sem).start()

        @pl.when(~mine & low_part)
        def _():
            pltpu.make_async_copy(swap_a, weight.at[z, 512:1024], sem).start()

        @pl.when(~mine & ~low_part)
        def _():
            pltpu.make_async_copy(swap_b, weight.at[z, 512:1024], sem).start()

    load(residual_hbm, residual_ref)
    load(gain_hbm.at[:, pl.ds(pl.multiple_of(me * 256, 256), 256)], gain_ref)
    barrier = pltpu.get_barrier_semaphore()
    masks = [mask for group in SUM_MASKS for mask in group]
    for mask in masks:
        pl.semaphore_signal(
            barrier, inc=1, device_id=tp_device(flipped(place, mask)), device_id_type=MESH
        )
    gated_copy.wait()
    pl.semaphore_wait(barrier, len(masks))
    pair_copies = []
    for start, size in CHUNKS[1:]:
        copy = pltpu.make_async_remote_copy(
            gated.at[:, start : start + size, 0:512], gated.at[:, start : start + size, 512:1024],
            pair_ss.at[len(pair_copies)], pair_rs.at[len(pair_copies)],
            device_id=tp_device(flipped(place, 4)), device_id_type=MESH,
        )
        copy.start()
        pair_copies.append(copy)
    loads[0].wait()
    loads[1].wait()

    def copy_of(chunk, p, code, level):
        start, size = CHUNKS[chunk]
        return pltpu.make_async_remote_copy(
            snd.at[p, code, start : start + size], rcv.at[p, code, start : start + size],
            ss.at[chunk, p, code], rs.at[chunk, p, code],
            device_id=tp_device(flipped(place, pair_of(p, level))), device_id_type=MESH,
        )

    def products(chunk):
        start, size = CHUNKS[chunk]

        def product(i, carry):
            if chunk == 0:
                for index, z in enumerate(z_order):

                    @pl.when(i == index)
                    def _():
                        loads[2 + index].wait()
                        pltpu.make_async_copy(got_a, weight.at[z, 512:1024], weight_sem.at[index]).wait()

            bits = [((15 - i) // (1 << (3 - j))) % 2 for j in range(LEVELS)]
            flip = [0] * 5
            for j in range(LEVELS):
                for bit in range(5):
                    if (PAIRS[j] >> bit) & 1:
                        flip[bit] = flip[bit] + bits[j]
            owner = me
            for bit in range(5):
                owner = owner + (flip[bit] % 2) * delta[bit]
            columns = pl.ds(pl.multiple_of((owner % 4) * 256, 256), 256)
            rows = gated[:, start : start + size, :].reshape(STEPS * size, 1024)
            acc = dot_nn(rows, weight[owner // 8, :, columns]).reshape(STEPS, size, 256)
            for p in range(4):
                code = sum(bits[(p + j) % 4] * (1 << (3 - j)) for j in range(LEVELS))

                @pl.when(bits[p] == 1)
                def _():
                    snd[p, code, start : start + size] = acc[p].astype(BF16)
                    copy_of(chunk, p, code, 0).start()

                @pl.when(bits[p] == 0)
                def _():
                    own[p, code, start : start + size] = acc[p]

            return carry

        lax.fori_loop(0, 16, product, 0)

    def summed(chunk, p, code, level):
        start, size = CHUNKS[chunk]
        acc = own[p, code, start : start + size]
        for j in range(level):
            copy_of(chunk, p, (1 << (3 - j)) + code, j).wait_recv()
            acc = acc + rcv[p, (1 << (3 - j)) + code, start : start + size].astype(F32)
        return acc

    which = lax.broadcasted_iota(jnp.int32, (8, 256), 0)
    for chunk, level in ORDER:
        if (chunk, level) == (0, LEVELS):
            loads[6].wait()
            loads[7].wait()
        start, size = CHUNKS[chunk]
        if level == 0:
            if chunk:
                pair_copies[chunk - 1].wait_recv()
            products(chunk)
        elif level < LEVELS:
            n = 1 << (3 - level)

            def send(i, carry):
                code = 2 * n - 1 - i
                for p in range(4):
                    acc = summed(chunk, p, code, level)
                    snd[p, code, start : start + size] = acc.astype(BF16)
                    copy_of(chunk, p, code, level).start()
                return carry

            lax.fori_loop(0, n, send, 0)
        else:
            for p in range(4):
                acc = summed(chunk, p, 0, LEVELS)
                acc = acc + residual_ref[p, start : start + size].astype(F32)
                hidden[p, start : start + size] = acc
                pick = jnp.where(which == p, 1.0, 0.0).astype(BF16)
                squares = dot_nt(pick, (acc * acc).astype(BF16))
                total = squares if p == 0 else total + squares
            sums[0, :, start : start + size] = total

    slot = 0
    sum_copies = []
    for stage, group in enumerate(SUM_MASKS):
        here = []
        for mask in group:
            copy = pltpu.make_async_remote_copy(
                sums.at[stage], got_sums.at[slot], sum_ss.at[slot], sum_rs.at[slot],
                device_id=tp_device(flipped(place, mask)), device_id_type=MESH,
            )
            copy.start()
            here.append((copy, slot))
            slot += 1
        total = sums[stage]
        for copy, index in here:
            copy.wait_recv()
            total = total + got_sums[index]
            sum_copies.append(copy)
        sums[stage + 1] = total
    scale = lax.rsqrt(sums[len(SUM_MASKS)] * (1.0 / D) + EPSILON)
    gain = gain_ref[...]
    coarse = scale.astype(BF16)
    fine = (scale - coarse.astype(F32)).astype(BF16)
    for p in range(4):
        pick = jnp.where(which == p, 1.0, 0.0).astype(BF16)
        factor = dot_tn(coarse, pick) + dot_tn(fine, pick)
        out_ref[p] = (hidden[p] * factor * gain).astype(BF16)

    for copy in sum_copies + pair_copies:
        copy.wait_send()
    for chunk in range(len(CHUNKS)):
        for level in range(LEVELS):
            n = 1 << (3 - level)

            def drain(i, carry):
                for p in range(4):
                    copy_of(chunk, p, n + i, level).wait_send()
                return carry

            lax.fori_loop(0, n, drain, 0)


def mix(first, second, other, weight, received, residual, gain):
    vmem = pl.BlockSpec(memory_space=pltpu.VMEM)
    hbm = pl.BlockSpec(memory_space=pltpu.HBM)
    return pl.pallas_call(
        mix_kernel,
        out_shape=jax.ShapeDtypeStruct((STEPS, 256, 256), BF16),
        in_specs=[hbm] * 10,
        out_specs=vmem,
        scratch_shapes=[
            pltpu.VMEM((STEPS, 256, 1024), BF16),
            pltpu.VMEM((4, 1024, 1024), BF16),
            pltpu.VMEM((STEPS, 256, 256), BF16),
            pltpu.VMEM((1, 256), F32),
            pltpu.VMEM((4, 8, 256, 256), F32),
            pltpu.VMEM((4, 16, 256, 256), BF16),
            pltpu.VMEM((4, 16, 256, 256), BF16),
            pltpu.VMEM((STEPS, 256, 256), F32),
            pltpu.VMEM((3, 8, 256), F32),
            pltpu.VMEM((10, 8, 256), F32),
            pltpu.SemaphoreType.DMA((8,)),
            pltpu.SemaphoreType.DMA((4,)),
            pltpu.SemaphoreType.DMA,
            pltpu.SemaphoreType.DMA((2,)),
            pltpu.SemaphoreType.DMA((2,)),
            pltpu.SemaphoreType.DMA((2, 4, 16)),
            pltpu.SemaphoreType.DMA((2, 4, 16)),
            pltpu.SemaphoreType.DMA((10,)),
            pltpu.SemaphoreType.DMA((10,)),
        ],
        compiler_params=pltpu.CompilerParams(
            collective_id=1, has_side_effects=True, vmem_limit_bytes=60 << 20
        ),
        name="mix",
    )(first, second, other, weight, *received, residual, gain)


def permuted(value, inst_mask, tp_mask):
    places = [(i, t) for i in range(4) for t in range(32)]
    pairs = [(i * 32 + t, (i ^ inst_mask) * 32 + (t ^ tp_mask)) for i, t in places]
    return lax.ppermute(value, ("inst", "tp"), pairs)


def on_device(
    mixer_input,
    gate_input,
    conv_state,
    scan_state,
    leave_slot,
    land_slot,
    move_count,
    conv_weight,
    conv_bias,
    delta_down,
    state_proj,
    delta_up,
    delta_bias,
    decay_log,
    skip_gain,
    out_weight,
    residual,
    norm_gain,
):
    core = lax.axis_index("inst") % 2
    far = 1 - (lax.axis_index("tp") // 4) % 2
    received = []
    for piece in range(2):
        column = (2 * core + piece) * 2048 + far * 1024
        received.append(permuted(lax.dynamic_slice(out_weight, (0, column), (512, 1024)), 2, 4))
    low, io, conv_out, source, moved = project(
        leave_slot, land_slot, move_count, mixer_input, jnp.transpose(conv_state, (1, 0, 2)), scan_state,
        conv_weight, conv_bias.reshape(1, -1), delta_down, state_proj,
    )
    low, received[0] = lax.optimization_barrier((low, received[0]))
    operands = (
        source, low.reshape(4, 2, 256, 256), io.reshape(256, 128), delta_up, delta_bias.reshape(1, -1),
        decay_log, skip_gain.reshape(1, -1), conv_out, gate_input, scan_state, moved.reshape(128, NS, 512),
    )
    final_state, first = recur(0, EARLY, *operands)
    first, received[1] = lax.optimization_barrier((first, received[1]))
    received = received + [permuted(piece, 1, 0) for piece in received]
    other = permuted(first, 0, 4)
    final_state, second = recur(EARLY, 256 - EARLY, *operands, final_state)
    normed = mix(first, second, other, out_weight, received, residual, norm_gain.reshape(1, -1))
    return (normed, final_state)


def solution(mesh):
    in_specs = (
        P(None, "inst", "tp"),
        P(None, "inst", "tp"),
        P("inst", None, "tp"),
        P("inst", None, "tp"),
        P("inst", None, None),
        P(None, "inst", None),
        P(),
        P(None, "tp"),
        P("tp"),
        P("tp", None),
        P(None, "tp"),
        P(None, "tp"),
        P("tp"),
        P(None, "tp"),
        P("tp"),
        P("tp", None),
        P(None, "inst", "tp"),
        P(),
    )
    out_specs = (P(None, "inst", "tp"), P("inst", None, "tp"))
    return jax.shard_map(
        on_device, mesh=mesh, in_specs=in_specs, out_specs=out_specs, check_vma=False
    )
```
